32 devices in a mesh: groups: 2 (over y), rows: 4 (over z), segment: 2 (over x), sub: 2 (over core).
Axes of the slice: x: 2, y: 2, z: 4, core: 2. Of those that a mesh axis runs over, the one named last changes fastest.
Arguments:
- activations: bfloat16 [2, 8, 32, 256, 128], P('segment', 'groups', 'rows', 'sub'), parts along dimension 1, may hold values from -16 to 16
- latent: bfloat16 [8, 4, 32, 256], P('groups', None, 'rows', 'sub'), parts along dimension 0, may hold values from -6 to 6
- recon: bfloat16 [8, 3, 32, 256], P('groups', None, 'rows', 'sub'), parts along dimension 0, may hold values from -8 to 8, as said below
- target: bfloat16 [8, 3, 32, 256], P('groups', None, 'rows', 'sub'), parts along dimension 0, may hold values from -6 to 6
- boxes: int32 [8, 4, 4], P('groups'), parts along dimension 0, may hold values from 0 to 8, as said below
- kernel: bfloat16 [2, 1152, 128], P('segment'), may hold values from -0.1875 to 0.1875
- mod_weight: bfloat16 [2, 4, 256], P('segment'), may hold values from -3 to 3
- scale_bias: bfloat16 [2, 128], P('segment'), may hold values from 0.5 to 1.5
- shift_bias: bfloat16 [2, 128], P('segment'), may hold values from -3 to 3
- out_weight: bfloat16 [3, 128], replicated, may hold values from -3.5 to 3.5
Outputs:
- grad_acts: bfloat16 [2, 8, 32, 256, 128], P('segment', 'groups', 'rows', 'sub'), parts along dimension 1
- grad_kernel: float32 [2, 2304, 128], P('segment', 'groups'), parts along dimension 1
- grad_mod_weight: float32 [2, 8, 256], P('segment', 'groups'), parts along dimension 1
- grad_bias: float32 [2, 512], P('segment', 'groups'), parts along dimension 1
The draws below stay inside these ranges and needn't reach their ends.
There are 2 independent parts, one for each index of `groups`. The reference program is written for one: setup_inputs(seed, part) draws one part's arguments, and reference() takes and returns one part's arrays. A program takes and returns all parts, laid end to end along the dimension named above; an argument that names none is the same for every part. Nothing has to cross between parts.
Inputs may be any that keep to these rules, and one draw needn't show every extreme that they name: `recon`: saved reconstruction. `boxes`: every box lies inside the image; its height is at least 0 tiles and its width at least 2 tiles, and box 0 of micro-batch 0 covers the whole image.
All inputs are finite; a program needn't handle non-finite values.
Results may differ from the reference program's by a relative error of at most 0.019.
Values may be sent and summed in bfloat16 or wider, within the bound.
No kernel may reach another device: no remote copies, remote signals or barrier semaphores. Data moves between devices by JAX's collectives and lax.ppermute only.
A program may use at most 64 MiB of HBM per device.

```python
import jax
import jax.numpy as jnp
from jax import lax

CHANNELS = 128
GROUPS = 32
LATENT = 4
ROWS_DEV = 8
MICRO = 4
CROPS = 4
TILE = 32
SECTIONS = 2
IMAGE_ROWS = 32
IMAGE_COLUMNS = 256


def draw_activations(key, part):
    key = jax.random.fold_in(key, 11)
    key_base = jax.random.fold_in(key, 0)
    key_chan = jax.random.fold_in(key, 1)
    key_gain = jax.random.fold_in(key, 3)
    key_level = jax.random.fold_in(key, 4)
    shape = (SECTIONS, MICRO, IMAGE_ROWS, IMAGE_COLUMNS, CHANNELS)
    bands = IMAGE_ROWS // ROWS_DEV
    band_shape = (SECTIONS, MICRO, bands, 1, CHANNELS)
    band_gain = jnp.exp(jax.random.uniform(key_gain, band_shape, minval=-0.6, maxval=0.6))
    band_level = jax.random.uniform(key_level, band_shape, minval=-1.5, maxval=1.5)
    row_gain = jnp.repeat(band_gain, ROWS_DEV, axis=2)
    row_level = jnp.repeat(band_level, ROWS_DEV, axis=2)
    channel_scale = jnp.exp(jax.random.uniform(key_chan, (SECTIONS, 1, 1, 1, CHANNELS), minval=-0.5, maxval=0.5))
    base = jnp.clip(jax.random.normal(key_base, shape), -4.0, 4.0)
    values = base * row_gain * channel_scale + row_level
    return jnp.clip(values, -16.0, 16.0).astype(jnp.bfloat16)


def draw_recon(key, part):
    key_noise = jax.random.fold_in(key, 0)
    shape = (MICRO, 3, IMAGE_ROWS, IMAGE_COLUMNS)
    noise = jnp.clip(jax.random.normal(key_noise, shape), -5.0, 5.0)
    return jnp.clip(noise, -8.0, 8.0).astype(jnp.bfloat16)


def draw_boxes(key, part):
    key_h, key_w, key_r, key_c = jax.random.split(key, 4)
    tiles_high = IMAGE_ROWS // TILE
    tiles_wide = IMAGE_COLUMNS // TILE
    least_high = max(1, tiles_high // 4)
    least_wide = max(1, tiles_wide // 4)
    heights = least_high + jax.random.randint(key_h, (MICRO, CROPS), 0, tiles_high - least_high + 1)
    widths = least_wide + jax.random.randint(key_w, (MICRO, CROPS), 0, tiles_wide - least_wide + 1)
    firsts = jax.random.randint(key_r, (MICRO, CROPS), 0, tiles_high - heights + 1)
    lefts = jax.random.randint(key_c, (MICRO, CROPS), 0, tiles_wide - widths + 1)
    heights = heights.at[0, 0].set(tiles_high)
    widths = widths.at[0, 0].set(tiles_wide)
    firsts = firsts.at[0, 0].set(0)
    lefts = lefts.at[0, 0].set(0)
    return jnp.stack([firsts, lefts, heights, widths], axis=-1).astype(jnp.int32)


def block_levels(key, extent, cuts, smallest, top_value):
    gain, own = 1.0, jax.random.fold_in(key, 6)
    for dim, shards_of in cuts:
        steps = jnp.exp(jax.random.uniform(jax.random.fold_in(own, dim), (shards_of,), jnp.float32, smallest / len(cuts), top_value / len(cuts)))
        gain = gain * jnp.repeat(steps, extent[dim] // shards_of).reshape([-1 if axis == dim else 1 for axis in range(len(extent))])
    return gain


def gaussian(own_key, shape, width, limit, shards=(), kind=jnp.bfloat16):
    factor_of = block_levels(own_key, shape, shards, -0.22, 0.18) if shards else 1.0
    values = jax.random.normal(own_key, shape, jnp.float32) * width * factor_of
    return jnp.minimum(jnp.maximum(values, -limit), limit).astype(kind)


def setup_inputs(seed: int = 0, part: int = 0) -> dict:
    seeds = jax.random.split(jax.random.key(seed), 11)
    own_keys = jax.random.split(jax.random.fold_in(seeds[10], part), 11)
    return {
        "activations": draw_activations(jax.random.fold_in(jax.random.fold_in(seeds[10], part), 71), part),
        "latent": gaussian(own_keys[1], (MICRO, LATENT, IMAGE_ROWS, IMAGE_COLUMNS), 1.0, 6.0, ((2, 4), (3, 2))),
        "recon": draw_recon(jax.random.fold_in(jax.random.fold_in(seeds[10], part), 71), part),
        "target": gaussian(own_keys[3], (MICRO, 3, IMAGE_ROWS, IMAGE_COLUMNS), 1.0, 6.0, ((2, 4), (3, 2))),
        "boxes": draw_boxes(jax.random.fold_in(jax.random.fold_in(seeds[10], part), 71), part),
        "kernel": gaussian(seeds[5], (SECTIONS, 9 * CHANNELS, CHANNELS), (9 * CHANNELS) ** -0.5, 0.1875, ((0, 2),)),
        "mod_weight": gaussian(seeds[6], (SECTIONS, LATENT, 2 * CHANNELS), LATENT ** -0.5, 3.0, ((0, 2),)),
        "scale_bias": jnp.clip(1.0 + 0.1 * jax.random.normal(seeds[7], (SECTIONS, CHANNELS), jnp.float32), 0.5, 1.5).astype(jnp.bfloat16),
        "shift_bias": gaussian(seeds[8], (SECTIONS, CHANNELS), 0.5, 3.0, ((0, 2),)),
        "out_weight": gaussian(seeds[9], (3, CHANNELS), 3 ** -0.5, 3.5),
    }


EPS = 1e-06

def crop_weights(boxes, row_start, col_start, row_count, col_count, total_rows, total_cols):
    row_tile = (row_start + jnp.arange(row_count, dtype=jnp.int32)) // TILE
    col_tile = (col_start + jnp.arange(col_count, dtype=jnp.int32)) // TILE
    first_row = boxes[:, :, 0:1]
    first_col = boxes[:, :, 1:2]
    box_height = boxes[:, :, 2:3]
    box_width = boxes[:, :, 3:4]
    in_rows = ((row_tile >= first_row) & (row_tile < first_row + box_height)).astype(jnp.float32)
    in_cols = ((col_tile >= first_col) & (col_tile < first_col + box_width)).astype(jnp.float32)
    tiles = total_rows // TILE * (total_cols // TILE)
    share = tiles / (boxes.shape[1] * (box_height * box_width).astype(jnp.float32))
    return jnp.einsum('mkr,mkc->mrc', in_rows * share, in_cols)

def top_gradient(recon, target, cropped, out_weight):
    diff = 2.0 * (recon.astype(jnp.float32) - target.astype(jnp.float32)) * cropped[:, None]
    return jnp.einsum('mkhw,kc->mhwc', diff, out_weight.astype(jnp.float32)).astype(jnp.bfloat16)

def expand(stat):
    return stat[None, None, :, None]

def taps(padded, row_count, col_count, flipped):
    pieces = []
    for tap_row in range(3):
        for tap_col in range(3):
            if flipped:
                row_offset, col_offset = (2 - tap_row, 2 - tap_col)
            else:
                row_offset, col_offset = (tap_row, tap_col)
            pieces.append(padded[row_offset:row_offset + row_count, col_offset:col_offset + col_count])
    return jnp.concatenate(pieces, axis=-1).reshape(row_count * col_count, -1)

def section_backward(acts, latent_m, incoming, weights_t, mix_weight, scale_row, shift_row, count):
    channel_count = CHANNELS
    value_array = acts.astype(jnp.float32)
    shaped = value_array.reshape(IMAGE_ROWS, IMAGE_COLUMNS, GROUPS, channel_count // GROUPS)
    mean_val = lax.optimization_barrier(jnp.sum(shaped, axis=(0, 1, 3))) / count
    msq_val = lax.optimization_barrier(jnp.sum(shaped * shaped, axis=(0, 1, 3))) / count
    rstd_val = lax.rsqrt(msq_val - mean_val * mean_val + EPS)
    reshaped_normalized = (shaped - expand(mean_val)) * expand(rstd_val)
    centered_scaled = reshaped_normalized.reshape(IMAGE_ROWS, IMAGE_COLUMNS, channel_count)
    latent_f = latent_m.astype(jnp.float32)
    coeff = jnp.einsum('zhw,zc->hwc', latent_f, mix_weight.astype(jnp.float32))
    spatial_scale = coeff[..., :channel_count] + scale_row.astype(jnp.float32)
    spatial_shift = coeff[..., channel_count:] + shift_row.astype(jnp.float32)
    pre_activation = centered_scaled * spatial_scale + spatial_shift
    hidden = jax.nn.silu(pre_activation).astype(jnp.bfloat16)
    padded_h = jnp.pad(hidden, ((1, 1), (1, 1), (0, 0)))
    padded_g = jnp.pad(incoming, ((1, 1), (1, 1), (0, 0)))
    patches = taps(padded_h, IMAGE_ROWS, IMAGE_COLUMNS, False)
    kernel_term = lax.dot_general(patches, incoming.reshape(-1, channel_count), (((0,), (0,)), ((), ())), preferred_element_type=jnp.float32)
    hidden_grad = jnp.dot(taps(padded_g, IMAGE_ROWS, IMAGE_COLUMNS, True), weights_t, preferred_element_type=jnp.float32).reshape(IMAGE_ROWS, IMAGE_COLUMNS, channel_count)
    sig = jax.nn.sigmoid(pre_activation)
    pre_activation_gradient = hidden_grad * (sig * (1.0 + pre_activation * (1.0 - sig)))
    paired_parts = jnp.concatenate([pre_activation_gradient * centered_scaled, pre_activation_gradient], axis=-1)
    mod_term = jnp.einsum('zhw,hwc->zc', latent_f, paired_parts)
    bias_term = lax.optimization_barrier(jnp.sum(paired_parts, axis=(0, 1)))
    shaped_grad = (pre_activation_gradient * spatial_scale).reshape(IMAGE_ROWS, IMAGE_COLUMNS, GROUPS, channel_count // GROUPS)
    mean_grad = lax.optimization_barrier(jnp.sum(shaped_grad, axis=(0, 1, 3))) / count
    mean_cross = lax.optimization_barrier(jnp.sum(shaped_grad * reshaped_normalized, axis=(0, 1, 3))) / count
    adjust = expand(rstd_val) * (shaped_grad - expand(mean_grad) - reshaped_normalized * expand(mean_cross))
    result = (incoming.astype(jnp.float32) + adjust.reshape(IMAGE_ROWS, IMAGE_COLUMNS, channel_count)).astype(jnp.bfloat16)
    return (result, kernel_term, mod_term, bias_term)

def reference(activations, latent, recon, target, boxes, kernel, mod_weight, scale_bias, shift_bias, out_weight):
    channel_count = CHANNELS
    cropped = crop_weights(boxes, 0, 0, IMAGE_ROWS, IMAGE_COLUMNS, IMAGE_ROWS, IMAGE_COLUMNS)
    incoming_all = top_gradient(recon, target, cropped, out_weight)
    count = IMAGE_ROWS * IMAGE_COLUMNS * (channel_count // GROUPS)
    grads_list = [None] * SECTIONS
    kernel_list = [None] * SECTIONS
    mod_list = [None] * SECTIONS
    bias_list = [None] * SECTIONS
    for section in reversed(range(SECTIONS)):
        weights_t = kernel[section].reshape(9, channel_count, channel_count).transpose(0, 2, 1).reshape(9 * channel_count, channel_count)
        kernel_sum = jnp.zeros((9 * channel_count, channel_count), jnp.float32)
        mod_sum = jnp.zeros((LATENT, 2 * channel_count), jnp.float32)
        bias_sum = jnp.zeros((2 * channel_count,), jnp.float32)
        results = []
        for micro_index in range(MICRO):
            result, kernel_term, mod_term, bias_term = section_backward(activations[section, micro_index], latent[micro_index], incoming_all[micro_index], weights_t, mod_weight[section], scale_bias[section], shift_bias[section], count)
            results.append(result)
            kernel_sum = kernel_sum + kernel_term
            mod_sum = mod_sum + mod_term
            bias_sum = bias_sum + bias_term
        incoming_all = jnp.stack(results)
        grads_list[section] = incoming_all
        kernel_list[section] = kernel_sum
        mod_list[section] = mod_sum
        bias_list[section] = bias_sum
    return (jnp.stack(grads_list), jnp.stack(kernel_list), jnp.stack(mod_list), jnp.stack(bias_list))
```

```python
import functools

import jax
import jax.numpy as jnp
from jax import lax
from jax.experimental import pallas as pl
from jax.experimental.pallas import tpu as pltpu
from jax.sharding import PartitionSpec as P

GROUPS = 32
TILE = 32


EPS = 1e-06


def extended(block, sides, width):
    for axis, dim in sides:
        count = lax.axis_size(axis)
        forward = [(i, i + 1) for i in range(count - 1)]
        backward = [(target, source) for source, target in forward]
        low = lax.ppermute(
            lax.slice_in_dim(block, block.shape[dim] - width, None, axis=dim), axis, forward
        )
        high = lax.ppermute(lax.slice_in_dim(block, 0, width, axis=dim), axis, backward)
        block = jnp.concatenate([low, block, high], axis=dim)
    return block


def from_behind(value, axis, steps):
    count = lax.axis_size(axis)
    initial, last = (max(0, -steps), min(count, count - steps))
    return lax.ppermute(value, axis, [(source, source + steps) for source in range(initial, last)])


def crop_weights(boxes, row_start, col_start, row_count, col_count, total_rows, total_cols):
    row_tile = (row_start + jnp.arange(row_count, dtype=jnp.int32)) // TILE
    col_tile = (col_start + jnp.arange(col_count, dtype=jnp.int32)) // TILE
    first_row = boxes[:, :, 0:1]
    first_col = boxes[:, :, 1:2]
    box_height = boxes[:, :, 2:3]
    box_width = boxes[:, :, 3:4]
    in_rows = ((row_tile >= first_row) & (row_tile < first_row + box_height)).astype(jnp.float32)
    in_cols = ((col_tile >= first_col) & (col_tile < first_col + box_width)).astype(jnp.float32)
    tiles = total_rows // TILE * (total_cols // TILE)
    share = tiles / (boxes.shape[1] * (box_height * box_width).astype(jnp.float32))
    return jnp.einsum("mkr,mkc->mrc", in_rows * share, in_cols)


def top_gradient(recon, target, cropped, out_weight):
    diff = 2.0 * (recon.astype(jnp.float32) - target.astype(jnp.float32)) * cropped[:, None]
    return jnp.einsum("mkhw,kc->mhwc", diff, out_weight.astype(jnp.float32)).astype(jnp.bfloat16)


def loss_gradient(
    boxes,
    recon,
    target,
    out_weight,
    row_start,
    col_start,
    row_count,
    col_count,
    total_rows,
    total_cols,
):
    cropped = crop_weights(
        boxes, row_start, col_start, row_count, col_count, total_rows, total_cols
    )
    return top_gradient(recon, target, cropped, out_weight)


def grouped_layout(value_array):
    return value_array.reshape(value_array.shape[:-1] + (GROUPS, value_array.shape[-1] // GROUPS))


def group_sums(value_array):
    shaped = grouped_layout(value_array)
    return (jnp.sum(shaped, axis=(-4, -3, -1)), jnp.sum(shaped * shaped, axis=(-4, -3, -1)))


def expand(stat):
    return stat[..., None, None, :, None]


def normalized_values(value_array, mean_val, rstd_val):
    shaped = grouped_layout(value_array)
    return ((shaped - expand(mean_val)) * expand(rstd_val)).reshape(value_array.shape)


def modulation(latent_batch, mix_weight, scale_row, shift_row):
    channel_count = scale_row.shape[-1]
    coefficients = jnp.einsum(
        "bzhw,zc->bhwc", latent_batch.astype(jnp.float32), mix_weight.astype(jnp.float32)
    )
    return (
        coefficients[..., :channel_count] + scale_row.astype(jnp.float32),
        coefficients[..., channel_count:] + shift_row.astype(jnp.float32),
    )


def transposed(weights):
    channel_count = weights.shape[-1]
    return (
        weights.reshape(9, channel_count, channel_count)
        .transpose(0, 2, 1)
        .reshape(9 * channel_count, channel_count)
    )


def taps(padded, row_count, col_count, flipped):
    pieces = []
    for tap_row in range(3):
        for tap_col in range(3):
            if flipped:
                row_offset, col_offset = (2 - tap_row, 2 - tap_col)
            else:
                row_offset, col_offset = (tap_row, tap_col)
            pieces.append(
                padded[:, row_offset : row_offset + row_count, col_offset : col_offset + col_count]
            )
    return jnp.concatenate(pieces, axis=-1).reshape(-1, 9 * padded.shape[-1])


def pick(value_array, index):
    return lax.dynamic_slice_in_dim(value_array, index, 1, 0)


def section_backward(
    value_array, latent_batch, incoming, spatial_scale, spatial_shift, weights_t, count
):
    batch, row_count, col_count, channel_count = value_array.shape
    sum_one, sum_two = group_sums(value_array)
    sum_one, sum_two = lax.psum((sum_one, sum_two), ("rows", "sub"))
    group_mean = sum_one / count
    inverse_deviation = lax.rsqrt(sum_two / count - group_mean * group_mean + EPS)
    centered_scaled = normalized_values(value_array, group_mean, inverse_deviation)
    pre_activation = centered_scaled * spatial_scale + spatial_shift
    hidden = jax.nn.silu(pre_activation).astype(jnp.bfloat16)
    padded_h = extended(hidden, (("rows", 1), ("sub", 2)), 1)
    padded_g = extended(incoming, (("rows", 1), ("sub", 2)), 1)
    patches = taps(padded_h, row_count, col_count, False)
    kernel_term = lax.dot_general(
        patches,
        incoming.reshape(-1, channel_count),
        (((0,), (0,)), ((), ())),
        preferred_element_type=jnp.float32,
    )
    hidden_grad = jnp.dot(
        taps(padded_g, row_count, col_count, True), weights_t, preferred_element_type=jnp.float32
    ).reshape(value_array.shape)
    sig = jax.nn.sigmoid(pre_activation)
    pre_activation_gradient = hidden_grad * (sig * (1.0 + pre_activation * (1.0 - sig)))
    paired_parts = jnp.concatenate(
        [pre_activation_gradient * centered_scaled, pre_activation_gradient], axis=-1
    )
    mod_term = jnp.einsum("bzhw,bhwc->zc", latent_batch.astype(jnp.float32), paired_parts)
    bias_term = jnp.sum(paired_parts, axis=(0, 1, 2))
    shaped_grad = grouped_layout(pre_activation_gradient * spatial_scale)
    reshaped_normalized = grouped_layout(centered_scaled)
    part_one = jnp.sum(shaped_grad, axis=(1, 2, 4))
    part_two = jnp.sum(shaped_grad * reshaped_normalized, axis=(1, 2, 4))
    part_one, part_two = lax.psum((part_one, part_two), ("rows", "sub"))
    mean_grad = part_one / count
    mean_cross = part_two / count
    adjust = expand(inverse_deviation) * (
        shaped_grad - expand(mean_grad) - reshaped_normalized * expand(mean_cross)
    )
    result = (incoming.astype(jnp.float32) + adjust.reshape(value_array.shape)).astype(jnp.bfloat16)
    return (result, kernel_term, mod_term, bias_term)


def general_body(
    activations,
    latent,
    recon,
    target,
    boxes,
    kernel,
    mod_weight,
    scale_bias,
    shift_bias,
    out_weight,
):
    segments = lax.axis_size("segment")
    segment_index = lax.axis_index("segment")
    micro, row_count, col_count, channel_count = activations.shape[1:]
    total_rows = row_count * lax.axis_size("rows")
    total_cols = col_count * lax.axis_size("sub")
    count = total_rows * total_cols * (channel_count // GROUPS)
    row_start = lax.axis_index("rows") * row_count
    col_start = lax.axis_index("sub") * col_count
    acts = activations[0]
    weights_t = transposed(kernel[0])
    mix_weight = mod_weight[0]
    scale_row = scale_bias[0]
    shift_row = shift_bias[0]
    top = loss_gradient(
        boxes,
        recon,
        target,
        out_weight,
        row_start,
        col_start,
        row_count,
        col_count,
        total_rows,
        total_cols,
    )

    def tick(step, carry):
        passing, grads_out, kernel_grad, mod_grad, bias_grad = carry
        offset = step - (segments - 1 - segment_index)
        valid = (offset >= 0) & (offset < micro)
        index = jnp.clip(offset, 0, micro - 1)
        received = from_behind(passing, "segment", -1)
        incoming = jnp.where(segment_index == segments - 1, pick(top, index), received)
        value_array = pick(acts, index).astype(jnp.float32)
        latent_m = pick(latent, index)
        spatial_scale, spatial_shift = modulation(latent_m, mix_weight, scale_row, shift_row)
        result, kernel_term, mod_term, bias_term = section_backward(
            value_array, latent_m, incoming, spatial_scale, spatial_shift, weights_t, count
        )
        weight = valid.astype(jnp.float32)
        current = pick(grads_out, index)
        grads_out = lax.dynamic_update_slice_in_dim(
            grads_out, jnp.where(valid, result, current), index, 0
        )
        return (
            result,
            grads_out,
            kernel_grad + weight * kernel_term,
            mod_grad + weight * mod_term,
            bias_grad + weight * bias_term,
        )

    initial = (
        jnp.zeros((1, row_count, col_count, channel_count), jnp.bfloat16),
        jnp.zeros_like(acts),
        jnp.zeros((9 * channel_count, channel_count), jnp.float32),
        jnp.zeros((mix_weight.shape[0], 2 * channel_count), jnp.float32),
        jnp.zeros((2 * channel_count,), jnp.float32),
    )
    final = lax.fori_loop(0, micro + segments - 1, tick, initial)
    grads_out = final[1][None]
    kernel_grad = final[2][None]
    mod_grad = final[3][None]
    bias_grad = final[4][None]
    kernel_grad, mod_grad, bias_grad = lax.psum((kernel_grad, mod_grad, bias_grad), ("rows", "sub"))
    return (grads_out, kernel_grad, mod_grad, bias_grad)


HALO = 32
EXACT = lax.Precision.HIGHEST
TN = (((0,), (0,)), ((), ()))
NT = (((1,), (1,)), ((), ()))
F32 = jnp.float32
BF16 = jnp.bfloat16


def swap(value, axis):
    return lax.ppermute(value, axis, [(0, 1), (1, 0)])


def shift(value, axis, steps):
    count = lax.axis_size(axis)
    return lax.ppermute(value, axis, [(i, (i + steps) % count) for i in range(count)])


def pixel_total(value):
    value = value + swap(value, "sub")
    one, two, three = [shift(value, "rows", steps) for steps in (1, 2, 3)]
    return (value + two) + (one + three)


def same_group(channels):
    per = channels // GROUPS
    left = lax.broadcasted_iota(jnp.int32, (channels, channels), 0) // per
    right = lax.broadcasted_iota(jnp.int32, (channels, channels), 1) // per
    return (left == right).astype(F32)


def statistics(sums_ref, micro, micros, member, count):
    both = jnp.concatenate([sums_ref[pl.ds(micro, 1), :], sums_ref[pl.ds(micros + micro, 1), :]], axis=0)
    both = jnp.dot(both, member, precision=EXACT, preferred_element_type=F32) / count
    mean = both[0:1]
    return mean, lax.rsqrt(both[1:2] - mean * mean + EPS)


def gradient_means(total, mix_ref, member, count):
    mix = mix_ref[...].astype(F32)
    channels = mix.shape[-1] // 2
    mean_grad = jnp.sum(mix[:, :channels] * total[:, channels:], axis=0, keepdims=True)
    mean_cross = jnp.sum(mix[:, :channels] * total[:, :channels], axis=0, keepdims=True)
    both = jnp.concatenate([mean_grad, mean_cross], axis=0)
    both = jnp.dot(both, member, precision=EXACT, preferred_element_type=F32) / count
    return both[0:1], both[1:2]


def sums_kernel(acts_ref, out_ref):
    micro, micros = pl.program_id(0), pl.num_programs(0)
    value = acts_ref[0].astype(F32)
    out_ref[pl.ds(micro, 1), :] = jnp.sum(value, axis=0, keepdims=True)
    out_ref[pl.ds(micros + micro, 1), :] = jnp.sum(value * value, axis=0, keepdims=True)


def top_kernel(pixels, diff_ref, out_weight_ref, main_ref, halo_ref):
    diff = diff_ref[0]
    high = diff.astype(BF16)
    rest = diff - high.astype(F32)
    middle = rest.astype(BF16)
    low = (rest - middle.astype(F32)).astype(BF16)
    weight = out_weight_ref[...]
    total = lax.dot_general(low, weight, TN, preferred_element_type=F32)
    total = total + lax.dot_general(middle, weight, TN, preferred_element_type=F32)
    total = total + lax.dot_general(high, weight, TN, preferred_element_type=F32)
    total = total.astype(BF16)
    main_ref[0] = total[:pixels]
    halo_ref[0] = total[pixels : pixels + halo_ref.shape[1]]


def spread(rows, cols, grad_ref, halo_ref, shifted):
    channels = grad_ref.shape[-1]
    sides = halo_ref[0, 2 * cols : 2 * cols + HALO, :].astype(F32)
    place = lax.broadcasted_iota(jnp.int32, (cols, channels), 0)
    for r in range(rows + 2):
        if r == 0:
            here = halo_ref[0, 0:cols, :]
        elif r == rows + 1:
            here = halo_ref[0, cols : 2 * cols, :]
        else:
            here = grad_ref[0, (r - 1) * cols : r * cols, :]
        value = here.astype(F32)
        left = jnp.where(place == 0, sides[r : r + 1], pltpu.roll(value, 1, 0))
        right = jnp.where(place == cols - 1, sides[HALO // 2 + r : HALO // 2 + r + 1], pltpu.roll(value, cols - 1, 0))
        at = slice(r * cols, (r + 1) * cols)
        shifted[at, 0:channels] = left.astype(BF16)
        shifted[at, channels : 2 * channels] = here
        shifted[at, 2 * channels :] = right.astype(BF16)


def tap_of(row, col):
    return 3 * (2 - row) + (2 - col)


def arrange_weights(kernel_ref, weights):
    channels = kernel_ref.shape[-1]
    for row in range(3):
        for col in range(3):
            tap = tap_of(row, col)
            weights[row, :, col * channels : (col + 1) * channels] = kernel_ref[tap * channels : (tap + 1) * channels, :]


def hidden_gradient(rows, cols, shifted, weights, hidden_grad):
    pixels = rows * cols
    total = lax.dot_general(shifted[0:pixels, :], weights[0], NT, preferred_element_type=F32)
    total = total + lax.dot_general(shifted[cols : cols + pixels, :], weights[1], NT, preferred_element_type=F32)
    hidden_grad[...] = total + lax.dot_general(
        shifted[2 * cols : 2 * cols + pixels, :], weights[2], NT, preferred_element_type=F32
    )


def pixel_values(at, acts_ref, latent_ref, mix_ref, mean, rstd):
    channels = mean.shape[-1]
    xhat = (acts_ref[0, at, :].astype(F32) - mean) * rstd
    mixed = lax.dot_general(latent_ref[0, :, at], mix_ref[...], TN, preferred_element_type=F32)
    scale = mixed[:, :channels]
    pre = xhat * scale + mixed[:, channels:]
    sig = 0.5 * jnp.tanh(0.5 * pre) + 0.5
    hidden = pre * sig
    return xhat, scale, hidden, sig + hidden * (1.0 - sig)


def block_kernel(
    segment,
    first,
    micros,
    rows,
    cols,
    count,
    segment_ref,
    sums_ref,
    acts_ref,
    latent_ref,
    grad_ref,
    halo_ref,
    kernel_ref,
    mix_ref,
    before_ref,
    norm_ref,
    reduced_ref,
    kernel_grad_ref,
    shifted,
    weights,
    hidden_grad,
    hidden_keep,
    pairs,
    total_kernel,
):
    step = pl.program_id(0)
    channels = acts_ref.shape[-1]
    pixels = rows * cols
    active = segment_ref[0] == segment

    @pl.when(active)
    def _():
        @pl.when(step == 0)
        def _():
            arrange_weights(kernel_ref, weights)
            total_kernel[...] = jnp.zeros_like(total_kernel)

        member = same_group(channels)
        mean, rstd = statistics(sums_ref, first + step, micros, member, count)
        spread(rows, cols, grad_ref, halo_ref, shifted)
        hidden_gradient(rows, cols, shifted, weights, hidden_grad)

        def one_row(r, carry):
            at = pl.ds(pl.multiple_of(r * cols, cols), cols)
            xhat, scale, hidden, slope = pixel_values(at, acts_ref, latent_ref, mix_ref, mean, rstd)
            hidden_keep[at, :] = hidden.astype(BF16)
            pre_grad = hidden_grad[at, :] * slope
            norm_ref[0, at, :] = pre_grad * scale
            pairs[at, 0:channels] = (pre_grad * xhat).astype(BF16)
            pairs[at, channels:] = pre_grad.astype(BF16)
            return carry

        lax.fori_loop(0, rows, one_row, 0)
        reduced_ref[0] = jnp.dot(latent_ref[0], pairs[...], preferred_element_type=F32)
        for row in range(3):
            total_kernel[row] += lax.dot_general(
                hidden_keep[...], shifted[row * cols : row * cols + pixels, :], TN, preferred_element_type=F32
            )

    @pl.when(jnp.logical_not(active))
    def _():
        reduced_ref[...] = jnp.zeros_like(reduced_ref)

    @pl.when(step == pl.num_programs(0) - 1)
    def _():
        @pl.when(active)
        def _():
            for row in range(3):
                for col in range(3):
                    tap = tap_of(row, col)
                    at = slice(tap * channels, (tap + 1) * channels)
                    kernel_grad_ref[at, :] = before_ref[at, :] + total_kernel[row, :, col * channels : (col + 1) * channels]

        @pl.when(jnp.logical_not(active))
        def _():
            kernel_grad_ref[...] = before_ref[...]


def redo_kernel(
    first,
    micros,
    rows,
    cols,
    count,
    segment_ref,
    sums_ref,
    total_ref,
    acts_ref,
    norm_ref,
    passed_ref,
    latent_ref,
    grad_ref,
    halo_ref,
    kernel_ref,
    mix_ref,
    result_ref,
    shifted,
    weights,
    hidden_grad,
):
    step = pl.program_id(0)
    channels = acts_ref.shape[-1]
    upper = segment_ref[0] == 1
    member = same_group(channels)
    mean, rstd = statistics(sums_ref, first + step, micros, member, count)
    mean_grad, mean_cross = gradient_means(total_ref[0], mix_ref, member, count)

    def finish(at, norm_grad, xhat):
        change = rstd * (norm_grad - mean_grad - xhat * mean_cross)
        result_ref[0, at, :] = (grad_ref[0, at, :].astype(F32) + change).astype(BF16)

    @pl.when(upper)
    def _():
        def one_row(r, carry):
            at = pl.ds(pl.multiple_of(r * cols, cols), cols)
            xhat = (acts_ref[0, at, :].astype(F32) - mean) * rstd
            finish(at, norm_ref[0, at, :], xhat)
            return carry

        lax.fori_loop(0, rows, one_row, 0)

    @pl.when(jnp.logical_not(upper))
    def _():
        @pl.when(step == 0)
        def _():
            arrange_weights(kernel_ref, weights)

        spread(rows, cols, grad_ref, halo_ref, shifted)
        hidden_gradient(rows, cols, shifted, weights, hidden_grad)

        def one_row(r, carry):
            at = pl.ds(pl.multiple_of(r * cols, cols), cols)
            xhat, scale, _, slope = pixel_values(at, passed_ref, latent_ref, mix_ref, mean, rstd)
            finish(at, hidden_grad[at, :] * slope * scale, xhat)
            return carry

        lax.fori_loop(0, rows, one_row, 0)


def last_kernel(
    first, micros, rows, cols, count, segment_ref, sums_ref, total_ref, acts_ref, norm_ref, grad_ref, mix_ref, result_ref
):
    step = pl.program_id(0)
    lower = segment_ref[0] == 0

    @pl.when(lower)
    def _():
        member = same_group(acts_ref.shape[-1])
        mean, rstd = statistics(sums_ref, first + step, micros, member, count)
        mean_grad, mean_cross = gradient_means(total_ref[0], mix_ref, member, count)

        def one_row(r, carry):
            at = pl.ds(pl.multiple_of(r * cols, cols), cols)
            xhat = (acts_ref[0, at, :].astype(F32) - mean) * rstd
            change = rstd * (norm_ref[0, at, :] - mean_grad - xhat * mean_cross)
            result_ref[0, at, :] = (grad_ref[0, at, :].astype(F32) + change).astype(BF16)
            return carry

        lax.fori_loop(0, rows, one_row, 0)

    @pl.when(jnp.logical_not(lower))
    def _():
        result_ref[...] = grad_ref[...]


def by_micro(shape, first=0):
    rest = (0,) * (len(shape) - 1)
    return pl.BlockSpec((1,) + tuple(shape[1:]), lambda m: (m + first,) + rest)


def whole(shape):
    return pl.BlockSpec(tuple(shape), lambda m: (0,) * len(shape))


SCALAR = pl.BlockSpec(memory_space=pltpu.SMEM)
PARAMS = pltpu.CompilerParams(vmem_limit_bytes=40 * 1024 * 1024)


def run_block(segment, first, size, micros, rows, cols, count, me, sums, acts, latent, grad, halo, kernel, mix, before):
    channels = acts.shape[-1]
    pixels = rows * cols
    return pl.pallas_call(
        functools.partial(block_kernel, segment, first, micros, rows, cols, count),
        grid=(size,),
        in_specs=[
            SCALAR,
            whole(sums.shape),
            by_micro(acts.shape, first),
            by_micro(latent.shape, first),
            by_micro(grad.shape),
            by_micro(halo.shape),
            whole(kernel.shape),
            whole(mix.shape),
            whole(before.shape),
        ],
        out_specs=[
            by_micro((size, pixels, channels)),
            by_micro((size, 8, 2 * channels)),
            whole(before.shape),
        ],
        out_shape=[
            jax.ShapeDtypeStruct((size, pixels, channels), F32),
            jax.ShapeDtypeStruct((size, 8, 2 * channels), F32),
            jax.ShapeDtypeStruct(before.shape, F32),
        ],
        scratch_shapes=[
            pltpu.VMEM(((rows + 2) * cols, 3 * channels), BF16),
            pltpu.VMEM((3, channels, 3 * channels), BF16),
            pltpu.VMEM((pixels, channels), F32),
            pltpu.VMEM((pixels, channels), BF16),
            pltpu.VMEM((pixels, 2 * channels), BF16),
            pltpu.VMEM((3, channels, 3 * channels), F32),
        ],
        compiler_params=PARAMS,
        name="block_backward",
    )(me, sums, acts, latent, grad, halo, kernel, mix, before)


def run_redo(first, size, micros, rows, cols, count, me, sums, totals, acts, norm, passed, latent, grad, halo, kernel, mix):
    channels = acts.shape[-1]
    pixels = rows * cols
    return pl.pallas_call(
        functools.partial(redo_kernel, first, micros, rows, cols, count),
        grid=(size,),
        in_specs=[
            SCALAR,
            whole(sums.shape),
            by_micro(totals.shape, first),
            by_micro(acts.shape, first),
            by_micro(norm.shape, first),
            by_micro(passed.shape),
            by_micro(latent.shape, first),
            by_micro(grad.shape, first),
            by_micro(halo.shape, first),
            whole(kernel.shape),
            whole(mix.shape),
        ],
        out_specs=by_micro((size, pixels, channels)),
        out_shape=jax.ShapeDtypeStruct((size, pixels, channels), BF16),
        scratch_shapes=[
            pltpu.VMEM(((rows + 2) * cols, 3 * channels), BF16),
            pltpu.VMEM((3, channels, 3 * channels), BF16),
            pltpu.VMEM((pixels, channels), F32),
        ],
        compiler_params=PARAMS,
        name="redo_upper",
    )(me, sums, totals, acts, norm, passed, latent, grad, halo, kernel, mix)


def pad_rows(value, rows):
    return jnp.pad(value, ((0, 0),) * (value.ndim - 2) + ((0, rows - value.shape[-2]), (0, 0)))


def pair_body(
    activations, latent, recon, target, boxes, kernel, mod_weight, scale_bias, shift_bias, out_weight
):
    micros, rows, cols, channels = activations.shape[1:]
    colors = recon.shape[1]
    pixels = rows * cols
    bands = lax.axis_size("rows")
    total_rows, total_cols = rows * bands, cols * 2
    count = float(total_rows * total_cols * (channels // GROUPS))
    segment = lax.axis_index("segment")
    band = lax.axis_index("rows")
    side = lax.axis_index("sub")
    row_start, col_start = band * rows, side * cols
    me = segment.astype(jnp.int32).reshape(1)
    acts = activations[0].reshape(micros, pixels, channels)

    mix = jnp.concatenate(
        [mod_weight[0], jnp.concatenate([scale_bias, shift_bias], axis=1), jnp.zeros((3, 2 * channels), BF16)]
    )
    half = kernel.shape[1] // 2
    mine = jnp.concatenate(
        [lax.dynamic_slice_in_dim(kernel[0], side * half, half), mix.reshape(2 * mix.shape[0], channels)]
    )
    mine = swap(mine, "segment")
    half_passed, mix_passed = mine[:half], mine[half:].reshape(mix.shape)
    other = swap(half_passed, "sub")
    kernel_passed = jnp.where(
        side == 0, jnp.concatenate([half_passed, other]), jnp.concatenate([other, half_passed])
    )
    passed = [swap(acts[m : m + 1], "segment") for m in range(micros)]

    sums = pl.pallas_call(
        sums_kernel,
        grid=(micros,),
        in_specs=[by_micro(acts.shape)],
        out_specs=whole((2 * micros, channels)),
        out_shape=jax.ShapeDtypeStruct((2 * micros, channels), F32),
        name="input_sums",
    )(acts)
    diff = (recon.astype(F32) - target.astype(F32)).reshape(micros * colors, rows, cols)
    planes = micros * colors
    edge = jnp.where(side == 0, diff[:, :, cols - 1], diff[:, :, 0])
    lines = -(-planes * rows // channels)
    flat = jnp.pad(edge.reshape(-1), (0, lines * channels - planes * rows)).reshape(lines, channels)
    got = swap(jnp.concatenate([sums, flat]), "sub")
    sums = sums + got[: 2 * micros]
    edge = got[2 * micros :].reshape(-1)[: planes * rows].reshape(planes, rows)

    def with_row(r):
        corner = jnp.pad(edge[:, r], (0, channels - planes)).reshape(1, channels)
        return jnp.concatenate([sums, diff[:, r], corner])

    from_up = shift(with_row(rows - 1), "rows", 1)
    from_down = shift(with_row(0), "rows", bands - 1)
    across = shift(sums, "rows", 2)
    sums = (sums + across) + (from_up[: 2 * micros] + from_down[: 2 * micros])
    up, down = from_up[2 * micros : 2 * micros + planes], from_down[2 * micros : 2 * micros + planes]
    inner = jnp.concatenate(
        [from_up[-1, :planes, None], edge, from_down[-1, :planes, None], jnp.zeros((planes, HALO // 2 - rows - 2), F32)], axis=1
    )
    blank = jnp.zeros_like(inner)
    lanes = -(-(pixels + 2 * cols + HALO) // 128) * 128
    diff = jnp.concatenate(
        [
            diff.reshape(planes, pixels),
            up,
            down,
            jnp.where(side == 1, inner, blank),
            jnp.where(side == 0, inner, blank),
            jnp.zeros((planes, lanes - pixels - 2 * cols - HALO), F32),
        ],
        axis=1,
    ).reshape(micros, colors, lanes)
    lane = jnp.arange(lanes, dtype=jnp.int32)
    tail = lane - pixels - 2 * cols
    low, high = tail < HALO // 2, tail < HALO
    lane_row = jnp.where(
        lane < pixels,
        lane // cols,
        jnp.where(lane < pixels + cols, -1, jnp.where(tail < 0, rows, tail % (HALO // 2) - 1)),
    )
    lane_col = jnp.where(tail < 0, lane % cols, jnp.where(low, -1, cols))
    row_tile, col_tile = (row_start + lane_row) // TILE, (col_start + lane_col) // TILE
    row_0, col_0, height, width = [boxes[:, :, i : i + 1] for i in range(4)]
    contains = (row_tile >= row_0) & (row_tile < row_0 + height) & (col_tile >= col_0) & (col_tile < col_0 + width)
    contains = contains & ((tail < 0) | (high & (tail % (HALO // 2) < rows + 2)))
    tiles = total_rows // TILE * (total_cols // TILE)
    share = tiles / (boxes.shape[1] * (height * width).astype(F32))
    cropped = jnp.sum(jnp.where(contains, share, 0.0), axis=1)
    diff = pad_rows(2.0 * diff * cropped[:, None], 8)
    halo_rows = 2 * cols + HALO
    top, top_halo = pl.pallas_call(
        functools.partial(top_kernel, pixels),
        grid=(micros,),
        in_specs=[by_micro(diff.shape), whole((8, channels))],
        out_specs=[by_micro((micros, pixels, channels)), by_micro((micros, halo_rows, channels))],
        out_shape=[
            jax.ShapeDtypeStruct((micros, pixels, channels), BF16),
            jax.ShapeDtypeStruct((micros, halo_rows, channels), BF16),
        ],
        name="top_gradient",
    )(diff, pad_rows(out_weight, 8))

    latent = latent.reshape(micros, latent.shape[1], pixels)
    latents = latent.shape[1]
    latent = jnp.concatenate(
        [latent, jnp.ones((micros, 1, pixels), BF16), jnp.zeros((micros, 7 - latents, pixels), BF16)], axis=1
    )

    fixed = (micros, rows, cols, count, me)
    norm_upper, reduced, kernel_grad = run_block(
        1, 0, micros, *fixed, sums, acts, latent, top, top_halo, kernel[0], mix, jnp.zeros(kernel.shape[1:], F32)
    )
    totals_own = pixel_total(reduced.reshape(micros * 8, 2 * channels))
    from_above = swap(jnp.concatenate([sums, totals_own.reshape(-1, channels)]), "segment")
    lower = segment == 0
    sums_upper = jnp.where(lower, from_above[: 2 * micros], sums)
    totals_upper = jnp.where(lower, from_above[2 * micros :].reshape(totals_own.shape), totals_own)
    totals_upper = totals_upper.reshape(micros, 8, 2 * channels)
    kernel_upper = jnp.where(lower, kernel_passed, kernel[0])
    mix_upper = jnp.where(lower, mix_passed, mix)

    def with_border(value):
        size = value.shape[0]
        value = value.reshape(size, rows, cols, channels)
        near = jnp.where(side == 0, value[:, :, cols - 1], value[:, :, 0])
        near = swap(near, "sub")

        def payload(r):
            return jnp.concatenate([value[:, r], near[:, r : r + 1], jnp.zeros((size, 15, channels), BF16)], axis=1)

        above = shift(payload(rows - 1), "rows", 1)
        below = shift(payload(0), "rows", bands - 1)
        above = jnp.where(band == 0, jnp.zeros_like(above), above)
        below = jnp.where(band == bands - 1, jnp.zeros_like(below), below)
        column = jnp.concatenate(
            [
                above[:, cols : cols + 1],
                near,
                below[:, cols : cols + 1],
                jnp.zeros((size, HALO // 2 - rows - 2, channels), BF16),
            ],
            axis=1,
        )
        nothing = jnp.zeros_like(column)
        return jnp.concatenate(
            [above[:, :cols], below[:, :cols], jnp.where(side == 1, column, nothing), jnp.where(side == 0, column, nothing)],
            axis=1,
        )

    results, norms, parts = [], [], []
    early = micros - 1
    for first, size in ((0, early), (early, micros - early)):
        given = passed[first] if size == 1 else jnp.concatenate(passed[first : first + size])
        result = run_redo(
            first, size, *fixed, sums_upper, totals_upper, acts, norm_upper, given, latent, top, top_halo, kernel_upper, mix_upper
        )
        norm, part, kernel_grad = run_block(
            0, first, size, *fixed, sums, acts, latent, result, with_border(result), kernel[0], mix, kernel_grad
        )
        results.append(result)
        norms.append(norm)
        parts.append(part)
    parts = jnp.concatenate(parts)
    totals = pixel_total(parts.reshape(micros * 8, 2 * channels))
    totals = jnp.where(lower, totals, totals_own).reshape(micros, 8, 2 * channels)
    grads = []
    for first, size, norm, result in ((0, early, norms[0], results[0]), (early, micros - early, norms[1], results[1])):
        grads.append(
            pl.pallas_call(
                functools.partial(last_kernel, first, micros, rows, cols, count),
                grid=(size,),
                in_specs=[
                    SCALAR,
                    whole(sums.shape),
                    by_micro(totals.shape, first),
                    by_micro(acts.shape, first),
                    by_micro(norm.shape),
                    by_micro(result.shape),
                    whole(mix.shape),
                ],
                out_specs=by_micro(result.shape),
                out_shape=jax.ShapeDtypeStruct(result.shape, BF16),
                name="input_gradient",
            )(me, sums, totals, acts, norm, result, mix)
        )
    grads = jnp.concatenate(grads).reshape(activations.shape)

    give = lax.dynamic_slice_in_dim(kernel_grad, (1 - side) * half, half)
    keep = lax.dynamic_slice_in_dim(kernel_grad, side * half, half)
    keep = (keep + swap(give, "sub")).astype(BF16)
    one, two, three = [shift(keep, "rows", steps).astype(F32) for steps in (1, 2, 3)]
    keep = (keep.astype(F32) + two) + (one + three)
    give = swap(keep, "sub")
    kernel_grad = jnp.where(side == 0, jnp.concatenate([keep, give]), jnp.concatenate([give, keep]))
    parameter = jnp.sum(totals, axis=0)
    return (grads, kernel_grad[None], parameter[None, :latents], parameter[None, latents])


def solution(mesh):
    pair = mesh.shape["segment"] == 2 and mesh.shape["rows"] == 4 and mesh.shape["sub"] == 2
    body = pair_body if pair else general_body
    placed = (
        P("segment", "groups", "rows", "sub", None),
        P("groups", None, "rows", "sub"),
        P("groups", None, "rows", "sub"),
        P("groups", None, "rows", "sub"),
        P("groups", None, None),
        P("segment", None, None),
        P("segment", None, None),
        P("segment", None),
        P("segment", None),
        P(),
    )
    return jax.shard_map(
        body,
        mesh=mesh,
        in_specs=placed,
        out_specs=(
            P("segment", "groups", "rows", "sub", None),
            P("segment", "groups", None),
            P("segment", "groups", None),
            P("segment", "groups"),
        ),
        check_vma=False,
    )
```

```python
import functools

import jax
import jax.numpy as jnp
from jax import lax
from jax.experimental import pallas as pl
from jax.experimental.pallas import tpu as pltpu
from jax.sharding import PartitionSpec as P

GROUPS = 32
TILE = 32


EPS = 1e-06


def extended(block, sides, width):
    for axis, dim in sides:
        count = lax.axis_size(axis)
        forward = [(i, i + 1) for i in range(count - 1)]
        backward = [(target, source) for source, target in forward]
        low = lax.ppermute(
            lax.slice_in_dim(block, block.shape[dim] - width, None, axis=dim), axis, forward
        )
        high = lax.ppermute(lax.slice_in_dim(block, 0, width, axis=dim), axis, backward)
        block = jnp.concatenate([low, block, high], axis=dim)
    return block


def from_behind(value, axis, steps):
    count = lax.axis_size(axis)
    initial, last = (max(0, -steps), min(count, count - steps))
    return lax.ppermute(value, axis, [(source, source + steps) for source in range(initial, last)])


def crop_weights(boxes, row_start, col_start, row_count, col_count, total_rows, total_cols):
    row_tile = (row_start + jnp.arange(row_count, dtype=jnp.int32)) // TILE
    col_tile = (col_start + jnp.arange(col_count, dtype=jnp.int32)) // TILE
    first_row = boxes[:, :, 0:1]
    first_col = boxes[:, :, 1:2]
    box_height = boxes[:, :, 2:3]
    box_width = boxes[:, :, 3:4]
    in_rows = ((row_tile >= first_row) & (row_tile < first_row + box_height)).astype(jnp.float32)
    in_cols = ((col_tile >= first_col) & (col_tile < first_col + box_width)).astype(jnp.float32)
    tiles = total_rows // TILE * (total_cols // TILE)
    share = tiles / (boxes.shape[1] * (box_height * box_width).astype(jnp.float32))
    return jnp.einsum("mkr,mkc->mrc", in_rows * share, in_cols)


def top_gradient(recon, target, cropped, out_weight):
    diff = 2.0 * (recon.astype(jnp.float32) - target.astype(jnp.float32)) * cropped[:, None]
    return jnp.einsum("mkhw,kc->mhwc", diff, out_weight.astype(jnp.float32)).astype(jnp.bfloat16)


def loss_gradient(
    boxes,
    recon,
    target,
    out_weight,
    row_start,
    col_start,
    row_count,
    col_count,
    total_rows,
    total_cols,
):
    cropped = crop_weights(
        boxes, row_start, col_start, row_count, col_count, total_rows, total_cols
    )
    return top_gradient(recon, target, cropped, out_weight)


def grouped_layout(value_array):
    return value_array.reshape(value_array.shape[:-1] + (GROUPS, value_array.shape[-1] // GROUPS))


def group_sums(value_array):
    shaped = grouped_layout(value_array)
    return (jnp.sum(shaped, axis=(-4, -3, -1)), jnp.sum(shaped * shaped, axis=(-4, -3, -1)))


def expand(stat):
    return stat[..., None, None, :, None]


def normalized_values(value_array, mean_val, rstd_val):
    shaped = grouped_layout(value_array)
    return ((shaped - expand(mean_val)) * expand(rstd_val)).reshape(value_array.shape)


def modulation(latent_batch, mix_weight, scale_row, shift_row):
    channel_count = scale_row.shape[-1]
    coefficients = jnp.einsum(
        "bzhw,zc->bhwc", latent_batch.astype(jnp.float32), mix_weight.astype(jnp.float32)
    )
    return (
        coefficients[..., :channel_count] + scale_row.astype(jnp.float32),
        coefficients[..., channel_count:] + shift_row.astype(jnp.float32),
    )


def transposed(weights):
    channel_count = weights.shape[-1]
    return (
        weights.reshape(9, channel_count, channel_count)
        .transpose(0, 2, 1)
        .reshape(9 * channel_count, channel_count)
    )


def taps(padded, row_count, col_count, flipped):
    pieces = []
    for tap_row in range(3):
        for tap_col in range(3):
            if flipped:
                row_offset, col_offset = (2 - tap_row, 2 - tap_col)
            else:
                row_offset, col_offset = (tap_row, tap_col)
            pieces.append(
                padded[:, row_offset : row_offset + row_count, col_offset : col_offset + col_count]
            )
    return jnp.concatenate(pieces, axis=-1).reshape(-1, 9 * padded.shape[-1])


def pick(value_array, index):
    return lax.dynamic_slice_in_dim(value_array, index, 1, 0)


def section_backward(
    value_array, latent_batch, incoming, spatial_scale, spatial_shift, weights_t, count
):
    batch, row_count, col_count, channel_count = value_array.shape
    sum_one, sum_two = group_sums(value_array)
    sum_one, sum_two = lax.psum((sum_one, sum_two), ("rows", "sub"))
    group_mean = sum_one / count
    inverse_deviation = lax.rsqrt(sum_two / count - group_mean * group_mean + EPS)
    centered_scaled = normalized_values(value_array, group_mean, inverse_deviation)
    pre_activation = centered_scaled * spatial_scale + spatial_shift
    hidden = jax.nn.silu(pre_activation).astype(jnp.bfloat16)
    padded_h = extended(hidden, (("rows", 1), ("sub", 2)), 1)
    padded_g = extended(incoming, (("rows", 1), ("sub", 2)), 1)
    patches = taps(padded_h, row_count, col_count, False)
    kernel_term = lax.dot_general(
        patches,
        incoming.reshape(-1, channel_count),
        (((0,), (0,)), ((), ())),
        preferred_element_type=jnp.float32,
    )
    hidden_grad = jnp.dot(
        taps(padded_g, row_count, col_count, True), weights_t, preferred_element_type=jnp.float32
    ).reshape(value_array.shape)
    sig = jax.nn.sigmoid(pre_activation)
    pre_activation_gradient = hidden_grad * (sig * (1.0 + pre_activation * (1.0 - sig)))
    paired_parts = jnp.concatenate(
        [pre_activation_gradient * centered_scaled, pre_activation_gradient], axis=-1
    )
    mod_term = jnp.einsum("bzhw,bhwc->zc", latent_batch.astype(jnp.float32), paired_parts)
    bias_term = jnp.sum(paired_parts, axis=(0, 1, 2))
    shaped_grad = grouped_layout(pre_activation_gradient * spatial_scale)
    reshaped_normalized = grouped_layout(centered_scaled)
    part_one = jnp.sum(shaped_grad, axis=(1, 2, 4))
    part_two = jnp.sum(shaped_grad * reshaped_normalized, axis=(1, 2, 4))
    part_one, part_two = lax.psum((part_one, part_two), ("rows", "sub"))
    mean_grad = part_one / count
    mean_cross = part_two / count
    adjust = expand(inverse_deviation) * (
        shaped_grad - expand(mean_grad) - reshaped_normalized * expand(mean_cross)
    )
    result = (incoming.astype(jnp.float32) + adjust.reshape(value_array.shape)).astype(jnp.bfloat16)
    return (result, kernel_term, mod_term, bias_term)


def general_body(
    activations,
    latent,
    recon,
    target,
    boxes,
    kernel,
    mod_weight,
    scale_bias,
    shift_bias,
    out_weight,
):
    segments = lax.axis_size("segment")
    segment_index = lax.axis_index("segment")
    micro, row_count, col_count, channel_count = activations.shape[1:]
    total_rows = row_count * lax.axis_size("rows")
    total_cols = col_count * lax.axis_size("sub")
    count = total_rows * total_cols * (channel_count // GROUPS)
    row_start = lax.axis_index("rows") * row_count
    col_start = lax.axis_index("sub") * col_count
    acts = activations[0]
    weights_t = transposed(kernel[0])
    mix_weight = mod_weight[0]
    scale_row = scale_bias[0]
    shift_row = shift_bias[0]
    top = loss_gradient(
        boxes,
        recon,
        target,
        out_weight,
        row_start,
        col_start,
        row_count,
        col_count,
        total_rows,
        total_cols,
    )

    def tick(step, carry):
        passing, grads_out, kernel_grad, mod_grad, bias_grad = carry
        offset = step - (segments - 1 - segment_index)
        valid = (offset >= 0) & (offset < micro)
        index = jnp.clip(offset, 0, micro - 1)
        received = from_behind(passing, "segment", -1)
        incoming = jnp.where(segment_index == segments - 1, pick(top, index), received)
        value_array = pick(acts, index).astype(jnp.float32)
        latent_m = pick(latent, index)
        spatial_scale, spatial_shift = modulation(latent_m, mix_weight, scale_row, shift_row)
        result, kernel_term, mod_term, bias_term = section_backward(
            value_array, latent_m, incoming, spatial_scale, spatial_shift, weights_t, count
        )
        weight = valid.astype(jnp.float32)
        current = pick(grads_out, index)
        grads_out = lax.dynamic_update_slice_in_dim(
            grads_out, jnp.where(valid, result, current), index, 0
        )
        return (
            result,
            grads_out,
            kernel_grad + weight * kernel_term,
            mod_grad + weight * mod_term,
            bias_grad + weight * bias_term,
        )

    initial = (
        jnp.zeros((1, row_count, col_count, channel_count), jnp.bfloat16),
        jnp.zeros_like(acts),
        jnp.zeros((9 * channel_count, channel_count), jnp.float32),
        jnp.zeros((mix_weight.shape[0], 2 * channel_count), jnp.float32),
        jnp.zeros((2 * channel_count,), jnp.float32),
    )
    final = lax.fori_loop(0, micro + segments - 1, tick, initial)
    grads_out = final[1][None]
    kernel_grad = final[2][None]
    mod_grad = final[3][None]
    bias_grad = final[4][None]
    kernel_grad, mod_grad, bias_grad = lax.psum((kernel_grad, mod_grad, bias_grad), ("rows", "sub"))
    return (grads_out, kernel_grad, mod_grad, bias_grad)


EXACT = lax.Precision.HIGHEST
TN = (((0,), (0,)), ((), ()))
NT = (((1,), (1,)), ((), ()))
F32 = jnp.float32
BF16 = jnp.bfloat16


def swap(value, axis):
    return lax.ppermute(value, axis, [(0, 1), (1, 0)])


def shift(value, axis, steps):
    count = lax.axis_size(axis)
    return lax.ppermute(value, axis, [(i, (i + steps) % count) for i in range(count)])


def swap_and_shift(value, steps):
    count = lax.axis_size("rows")
    pairs = [(2 * i + s, 2 * ((i + steps) % count) + 1 - s) for i in range(count) for s in range(2)]
    return lax.ppermute(value, ("rows", "segment"), pairs)


def pixel_total(value):
    value = value + swap(value, "sub")
    one, two, three = [shift(value, "rows", steps) for steps in (1, 2, 3)]
    return (value + two) + (one + three)


def same_group(channels):
    per = channels // GROUPS
    left = lax.broadcasted_iota(jnp.int32, (channels, channels), 0) // per
    right = lax.broadcasted_iota(jnp.int32, (channels, channels), 1) // per
    return (left == right).astype(F32)


def statistics(sums_ref, micro, micros, member, count):
    both = jnp.concatenate([sums_ref[pl.ds(micro, 1), :], sums_ref[pl.ds(micros + micro, 1), :]], axis=0)
    both = jnp.dot(both, member, precision=EXACT, preferred_element_type=F32) / count
    mean = both[0:1]
    return mean, lax.rsqrt(both[1:2] - mean * mean + EPS)


def gradient_means(total, mix, member, count):
    mean_grad = jnp.sum(mix[:8] * total[8:], axis=0, keepdims=True)
    mean_cross = jnp.sum(mix[:8] * total[:8], axis=0, keepdims=True)
    both = jnp.concatenate([mean_grad, mean_cross], axis=0)
    both = jnp.dot(both, member, precision=EXACT, preferred_element_type=F32) / count
    return both[0:1], both[1:2]


def side_by_side(mix):
    return jnp.concatenate([mix[:8], mix[8:]], axis=1).astype(BF16)


def sums_kernel(acts_ref, out_ref):
    micro, micros = pl.program_id(0), pl.num_programs(0)
    value = acts_ref[0].astype(F32)
    out_ref[pl.ds(micro, 1), :] = jnp.sum(value, axis=0, keepdims=True)
    out_ref[pl.ds(micros + micro, 1), :] = jnp.sum(value * value, axis=0, keepdims=True)


class Top:
    def __init__(self, shape, micro, place_ref, boxes_ref, weight_ref, up_ref, diff_ref, down_ref):
        self.rows, self.cols, total_rows, total_cols, crops = shape
        self.refs = (up_ref, diff_ref, down_ref)
        self.side, self.row_start = place_ref[1], place_ref[2]
        lane = lax.broadcasted_iota(jnp.int32, (1, self.cols), 1)
        tiles = total_rows // TILE * (total_cols // TILE)
        self.boxes = []
        for k in range(crops):
            row, col, height, width = [boxes_ref[micro, k, i] for i in range(4)]
            area = jnp.full((1, self.cols), crops * height * width, jnp.int32).astype(F32)
            share = tiles / area
            inside = []
            for side in (self.side, 1 - self.side):
                at = lane + side * self.cols
                inside.append(jnp.where((at >= col * TILE) & (at < (col + width) * TILE), share, 0.0))
            self.boxes.append((row * TILE, (row + height) * TILE, inside[0], inside[1]))
        weight = weight_ref[...].astype(F32)
        blank = jnp.zeros((8 - weight.shape[0], weight.shape[1]), F32)
        own = jnp.concatenate([weight, blank])
        other = jnp.concatenate([blank[:3], weight, blank[3:]])
        self.own = jnp.concatenate([own] * 3).astype(BF16)
        self.other = jnp.concatenate([other] * 3).astype(BF16)

    def row(self, index):
        up_ref, diff_ref, down_ref = self.refs
        if index < 2:
            diff = up_ref[0, index]
        elif index < self.rows + 2:
            diff = diff_ref[0, index - 2]
        else:
            diff = down_ref[0, index - self.rows - 2]
        at = self.row_start + (index - 2)
        own = jnp.zeros((1, self.cols), F32)
        other = jnp.zeros((1, self.cols), F32)
        for first, end, own_share, other_share in self.boxes:
            here = (at >= first) & (at < end)
            own = own + jnp.where(here, own_share, 0.0)
            other = other + jnp.where(here, other_share, 0.0)
        plane = lax.broadcasted_iota(jnp.int32, (8, self.cols), 0)
        diff = 2.0 * diff * jnp.where(plane < 3, own, other)
        high = diff.astype(BF16).astype(F32)
        middle = (diff - high).astype(BF16).astype(F32)
        parts = jnp.concatenate([high, middle, diff - high - middle]).astype(BF16)
        value = lax.dot_general(parts, self.own, TN, preferred_element_type=F32).astype(BF16)
        beside = lax.dot_general(parts, self.other, TN, preferred_element_type=F32).astype(BF16).astype(F32)
        return value, jnp.where(self.side == 0, beside[0:1], beside[self.cols - 1 : self.cols])

    def main_row(self, r):
        return self.row(r + 2)[0]


def spread(index, cols, value, near, side, shifted):
    channels = value.shape[-1]
    at = slice(index * cols, (index + 1) * cols)
    place = lax.broadcasted_iota(jnp.int32, (cols, channels), 0)
    wide = value.astype(F32)
    before = jnp.where(side == 1, near, 0.0)
    behind = jnp.where(side == 0, near, 0.0)
    shifted[at, 0:channels] = jnp.where(place == 0, before, pltpu.roll(wide, 1, 0)).astype(BF16)
    shifted[at, channels : 2 * channels] = value
    shifted[at, 2 * channels :] = jnp.where(place == cols - 1, behind, pltpu.roll(wide, cols - 1, 0)).astype(BF16)


def tap_of(row, col):
    return 3 * (2 - row) + (2 - col)


def arrange_weights(kernel_ref, weights):
    channels = kernel_ref.shape[-1]
    for row in range(3):
        for col in range(3):
            tap = tap_of(row, col)
            weights[row, :, col * channels : (col + 1) * channels] = kernel_ref[tap * channels : (tap + 1) * channels, :]


def hidden_gradient(rows, cols, shifted, weights, hidden_grad):
    pixels = rows * cols
    total = lax.dot_general(shifted[0:pixels, :], weights[0], NT, preferred_element_type=F32)
    total = total + lax.dot_general(shifted[cols : cols + pixels, :], weights[1], NT, preferred_element_type=F32)
    hidden_grad[0:pixels, :] = total + lax.dot_general(
        shifted[2 * cols : 2 * cols + pixels, :], weights[2], NT, preferred_element_type=F32
    )


def pixel_values(acts, latent, mix, mean, rstd):
    channels = mean.shape[-1]
    xhat = (acts.astype(F32) - mean) * rstd
    mixed = lax.dot_general(latent, mix, TN, preferred_element_type=F32)
    scale = mixed[:, :channels]
    pre = xhat * scale + mixed[:, channels:]
    sig = 0.5 * jnp.tanh(0.5 * pre) + 0.5
    hidden = pre * sig
    return xhat, scale, hidden, sig + hidden * (1.0 - sig)


def block_step(
    rows, cols, mean, rstd, mix, acts_ref, latent_ref, norm_ref, reduced_ref, shifted, weights, hidden_grad, hidden_keep, pairs, total_kernel
):
    channels = acts_ref.shape[-1]
    pixels = rows * cols
    hidden_gradient(rows, cols, shifted, weights, hidden_grad)
    for r in range(rows):
        at = slice(r * cols, (r + 1) * cols)
        latent = latent_ref[0, :, (r + 1) * cols : (r + 2) * cols]
        xhat, scale, hidden, slope = pixel_values(acts_ref[0, at, :], latent, mix, mean, rstd)
        hidden_keep[at, :] = hidden.astype(BF16)
        pre_grad = hidden_grad[at, :] * slope
        norm_ref[0, at, :] = (pre_grad * scale).astype(BF16)
        pairs[at, 0:channels] = (pre_grad * xhat).astype(BF16)
        pairs[at, channels:] = pre_grad.astype(BF16)
    reduced = jnp.dot(latent_ref[0, :, cols : cols + pixels], pairs[...], preferred_element_type=F32)
    reduced_ref[0, 0:8, :] = reduced[:, :channels]
    reduced_ref[0, 8:16, :] = reduced[:, channels:]
    for row in range(3):
        total_kernel[row] += lax.dot_general(
            hidden_keep[...], shifted[row * cols : row * cols + pixels, :], TN, preferred_element_type=F32
        )


def write_kernel_grad(total_kernel, kernel_grad_ref):
    channels = kernel_grad_ref.shape[-1]
    for row in range(3):
        for col in range(3):
            tap = tap_of(row, col)
            kernel_grad_ref[tap * channels : (tap + 1) * channels, :] = total_kernel[row, :, col * channels : (col + 1) * channels]


def upper_kernel(
    shape,
    micros,
    count,
    place_ref,
    boxes_ref,
    sums_ref,
    mix_ref,
    weight_ref,
    kernel_ref,
    up_ref,
    diff_ref,
    down_ref,
    acts_ref,
    latent_ref,
    norm_ref,
    reduced_ref,
    kernel_grad_ref,
    shifted,
    weights,
    hidden_grad,
    hidden_keep,
    pairs,
    total_kernel,
):
    step = pl.program_id(0)
    rows, cols = shape[:2]
    active = place_ref[0] == 1

    @pl.when(active)
    def _():
        @pl.when(step == 0)
        def _():
            arrange_weights(kernel_ref, weights)
            total_kernel[...] = jnp.zeros_like(total_kernel)

        mean, rstd = statistics(sums_ref, step, micros, same_group(acts_ref.shape[-1]), count)
        top = Top(shape, step, place_ref, boxes_ref, weight_ref, up_ref, diff_ref, down_ref)
        for r in range(rows + 2):
            spread(r, cols, *top.row(r + 1), place_ref[1], shifted)
        block_step(
            rows,
            cols,
            mean,
            rstd,
            side_by_side(mix_ref[...]),
            acts_ref,
            latent_ref,
            norm_ref,
            reduced_ref,
            shifted,
            weights,
            hidden_grad,
            hidden_keep,
            pairs,
            total_kernel,
        )

        @pl.when(step == micros - 1)
        def _():
            write_kernel_grad(total_kernel, kernel_grad_ref)

    @pl.when(jnp.logical_not(active))
    def _():
        reduced_ref[...] = jnp.zeros_like(reduced_ref)


def redo_kernel(
    shape,
    micros,
    count,
    place_ref,
    boxes_ref,
    packed_ref,
    weight_ref,
    kernel_ref,
    up_ref,
    diff_ref,
    down_ref,
    acts_ref,
    norm_ref,
    passed_ref,
    above_ref,
    below_ref,
    latent_ref,
    result_ref,
    edge_ref,
    shifted,
    weights,
    hidden_grad,
):
    step = pl.program_id(0)
    rows, cols, total_rows = shape[:3]
    channels = acts_ref.shape[-1]
    upper = place_ref[0] == 1
    side = place_ref[1]
    member = same_group(channels)
    mean, rstd = statistics(packed_ref, step, micros, member, count)
    mix = packed_ref[2 * micros + 16 * micros :, :]
    total = packed_ref[pl.ds(pl.multiple_of(2 * micros + 16 * step, 8), 16), :]
    mean_grad, mean_cross = gradient_means(total, mix, member, count)
    top = Top(shape, step, place_ref, boxes_ref, weight_ref, up_ref, diff_ref, down_ref)

    @pl.when(upper)
    def _():
        for r in range(rows):
            at = slice(r * cols, (r + 1) * cols)
            xhat = (acts_ref[0, at, :].astype(F32) - mean) * rstd
            change = rstd * (norm_ref[0, at, :].astype(F32) - mean_grad - xhat * mean_cross)
            result_ref[0, (r + 1) * cols : (r + 2) * cols, :] = (top.main_row(r).astype(F32) + change).astype(BF16)

    @pl.when(jnp.logical_not(upper))
    def _():
        @pl.when(step == 0)
        def _():
            arrange_weights(kernel_ref, weights)

        for r in range(rows + 4):
            spread(r, cols, *top.row(r), side, shifted)
        hidden_gradient(rows + 2, cols, shifted, weights, hidden_grad)
        wide_mix = side_by_side(mix)
        edges = []
        for r in range(rows + 2):
            at = slice(r * cols, (r + 1) * cols)
            if r == 0:
                acts = above_ref[0]
            elif r == rows + 1:
                acts = below_ref[0]
            else:
                acts = passed_ref[0, (r - 1) * cols : r * cols, :]
            xhat, scale, _, slope = pixel_values(acts, latent_ref[0, :, at], wide_mix, mean, rstd)
            change = rstd * (hidden_grad[at, :] * slope * scale - mean_grad - xhat * mean_cross)
            middle = shifted[(r + 1) * cols : (r + 2) * cols, channels : 2 * channels]
            value = middle.astype(F32) + change
            if r == 0 or r == rows + 1:
                row = place_ref[2] + (r - 1)
                value = jnp.where((row >= 0) & (row < total_rows), value, 0.0)
            result_ref[0, at, :] = value.astype(BF16)
            edges.append(jnp.where(side == 0, value[cols - 1 : cols], value[0:1]))
        edges.append(jnp.zeros((16 - rows - 2, channels), F32))
        edge_ref[0] = jnp.concatenate(edges).astype(BF16)


def lower_kernel(
    shape,
    micros,
    count,
    place_ref,
    sums_ref,
    mix_ref,
    kernel_ref,
    grad_ref,
    near_ref,
    acts_ref,
    latent_ref,
    before_ref,
    norm_ref,
    reduced_ref,
    kernel_grad_ref,
    shifted,
    weights,
    hidden_grad,
    hidden_keep,
    pairs,
    total_kernel,
):
    step = pl.program_id(0)
    rows, cols = shape[:2]
    active = place_ref[0] == 0

    @pl.when(active)
    def _():
        @pl.when(step == 0)
        def _():
            arrange_weights(kernel_ref, weights)
            total_kernel[...] = jnp.zeros_like(total_kernel)

        mean, rstd = statistics(sums_ref, step, micros, same_group(acts_ref.shape[-1]), count)
        near = near_ref[0].astype(F32)
        for r in range(rows + 2):
            spread(r, cols, grad_ref[0, r * cols : (r + 1) * cols, :], near[r : r + 1], place_ref[1], shifted)
        block_step(
            rows,
            cols,
            mean,
            rstd,
            side_by_side(mix_ref[...]),
            acts_ref,
            latent_ref,
            norm_ref,
            reduced_ref,
            shifted,
            weights,
            hidden_grad,
            hidden_keep,
            pairs,
            total_kernel,
        )

        @pl.when(step == micros - 1)
        def _():
            write_kernel_grad(total_kernel, kernel_grad_ref)

    @pl.when(jnp.logical_not(active))
    def _():
        reduced_ref[...] = jnp.zeros_like(reduced_ref)

        @pl.when(step == micros - 1)
        def _():
            kernel_grad_ref[...] = before_ref[...]


def last_kernel(rows, cols, micros, count, place_ref, sums_ref, mix_ref, total_ref, acts_ref, norm_ref, grad_ref, result_ref):
    step = pl.program_id(0)
    lower = place_ref[0] == 0

    @pl.when(lower)
    def _():
        member = same_group(acts_ref.shape[-1])
        mean, rstd = statistics(sums_ref, step, micros, member, count)
        mean_grad, mean_cross = gradient_means(total_ref[0], mix_ref[...], member, count)
        for r in range(rows):
            at = slice(r * cols, (r + 1) * cols)
            xhat = (acts_ref[0, at, :].astype(F32) - mean) * rstd
            change = rstd * (norm_ref[0, at, :].astype(F32) - mean_grad - xhat * mean_cross)
            result_ref[0, at, :] = (grad_ref[0, (r + 1) * cols : (r + 2) * cols, :].astype(F32) + change).astype(BF16)

    @pl.when(jnp.logical_not(lower))
    def _():
        result_ref[0] = grad_ref[0, cols : (rows + 1) * cols, :]


def by_micro(value):
    rest = (0,) * (len(value.shape) - 1)
    return pl.BlockSpec((1,) + tuple(value.shape[1:]), lambda m: (m,) + rest)


def whole(value):
    return pl.BlockSpec(tuple(value.shape), lambda m: (0,) * len(value.shape))


def call(kernel, name, micros, scalars, fixed, per_micro, outs, fixed_outs=(), scratch=(), tail=()):
    out_shape = [jax.ShapeDtypeStruct(s, d) for s, d in outs] + [jax.ShapeDtypeStruct(s, d) for s, d in fixed_outs]
    return pl.pallas_call(
        kernel,
        grid=(micros,),
        in_specs=[pl.BlockSpec(memory_space=pltpu.SMEM) for _ in scalars]
        + [whole(v) for v in fixed]
        + [by_micro(v) for v in per_micro]
        + [whole(v) for v in tail],
        out_specs=[by_micro(s) for s in out_shape[: len(outs)]] + [whole(s) for s in out_shape[len(outs) :]],
        out_shape=out_shape,
        scratch_shapes=[pltpu.VMEM(s, d) for s, d in scratch],
        compiler_params=pltpu.CompilerParams(vmem_limit_bytes=20 * 1024 * 1024),
        cost_estimate=pl.CostEstimate(flops=1, bytes_accessed=1, transcendentals=0),
        name=name,
    )(*scalars, *fixed, *per_micro, *tail)


def pair_body(
    activations, latent, recon, target, boxes, kernel, mod_weight, scale_bias, shift_bias, out_weight
):
    micros, rows, cols, channels = activations.shape[1:]
    latents, colors = latent.shape[1], recon.shape[1]
    pixels = rows * cols
    bands = lax.axis_size("rows")
    total_rows, total_cols = rows * bands, cols * 2
    count = float(total_rows * total_cols * (channels // GROUPS))
    segment = lax.axis_index("segment")
    side = lax.axis_index("sub")
    place = jnp.stack([segment, side, lax.axis_index("rows") * rows]).astype(jnp.int32)
    acts = activations[0].reshape(micros, pixels, channels)

    passed = swap(acts, "segment")
    above = swap_and_shift(acts[:, pixels - cols :], 1)
    below = swap_and_shift(acts[:, :cols], bands - 1)
    kernel_passed = swap(kernel[0], "segment")

    (sums,) = call(sums_kernel, "input_sums", micros, [], [], [acts], [], [((2 * micros, channels), F32)])
    diff = (recon.astype(F32) - target.astype(F32)).transpose(0, 2, 1, 3)
    flat = diff.reshape(micros * rows * colors, channels)
    got = swap(jnp.concatenate([sums, flat]), "sub")
    sums = sums + got[: 2 * micros]
    other = got[2 * micros :].reshape(diff.shape)

    def border(first, r):
        extra = latent[:, :, r].astype(F32).reshape(micros, 2, latents // 2, cols)
        two = jnp.concatenate([diff[:, first : first + 2], other[:, first : first + 2], extra], axis=2)
        return jnp.concatenate([sums, two.reshape(micros * 16, cols)])

    from_up = shift(border(rows - 2, rows - 1), "rows", 1)
    from_down = shift(border(0, 0), "rows", bands - 1)
    across = shift(sums, "rows", 2)
    sums = (sums + across) + (from_up[: 2 * micros] + from_down[: 2 * micros])
    up = from_up[2 * micros :].reshape(micros, 2, 8, cols)
    down = from_down[2 * micros :].reshape(micros, 2, 8, cols)
    diff = jnp.concatenate([diff, other, jnp.zeros((micros, rows, 2, cols), F32)], axis=2)
    beyond = [v[:, :, 6:8].reshape(micros, latents, cols).astype(BF16) for v in (up, down)]
    wide = (rows + 2) * cols
    latent = jnp.concatenate([beyond[0], latent.reshape(micros, latents, pixels), beyond[1]], axis=2)
    latent = jnp.concatenate(
        [latent, jnp.ones((micros, 1, wide), BF16), jnp.zeros((micros, 7 - latents, wide), BF16)], axis=1
    )
    mix = jnp.concatenate([mod_weight[0], jnp.concatenate([scale_bias, shift_bias], axis=1)]).astype(F32)
    mix = jnp.pad(mix, ((0, 7 - latents), (0, 0)))
    mix = jnp.concatenate([mix[:, :channels], mix[:, channels:]])

    shape = (rows, cols, total_rows, total_cols, boxes.shape[1])
    triple = 3 * channels
    work = [
        ((wide, triple), BF16),
        ((3, channels, triple), BF16),
        ((pixels, channels), F32),
        ((pixels, channels), BF16),
        ((pixels, 2 * channels), BF16),
        ((3, channels, triple), F32),
    ]
    produced = [((micros, pixels, channels), BF16), ((micros, 16, channels), F32)]
    kernel_shape = [(kernel.shape[1:], F32)]
    norm_upper, reduced, kernel_grad = call(
        functools.partial(upper_kernel, shape, micros, count),
        "upper_block",
        micros,
        [place, boxes],
        [sums, mix, out_weight, kernel[0]],
        [up, diff, down, acts, latent],
        produced,
        kernel_shape,
        work,
    )
    totals = pixel_total(reduced.reshape(micros * 16, channels))
    lower = segment == 0
    packed = jnp.concatenate([sums, totals, mix])
    packed = jnp.where(lower, swap(packed, "segment"), packed)
    result, edge = call(
        functools.partial(redo_kernel, shape, micros, count),
        "redo_upper",
        micros,
        [place, boxes],
        [packed, out_weight, kernel_passed],
        [up, diff, down, acts, norm_upper, passed, above, below, latent],
        [((micros, wide, channels), BF16), ((micros, 16, channels), BF16)],
        (),
        [(((rows + 4) * cols, triple), BF16), ((3, channels, triple), BF16), ((wide, channels), F32)],
    )
    near = swap(edge, "sub")
    norm, reduced, kernel_grad = call(
        functools.partial(lower_kernel, shape, micros, count),
        "lower_block",
        micros,
        [place],
        [sums, mix, kernel[0]],
        [result, near, acts, latent],
        produced,
        kernel_shape,
        work,
        [kernel_grad],
    )

    half = kernel.shape[1] // 2
    give = lax.dynamic_slice_in_dim(kernel_grad, (1 - side) * half, half)
    keep = lax.dynamic_slice_in_dim(kernel_grad, side * half, half)
    keep = (keep + swap(give, "sub")).astype(BF16)
    one, two, three = [shift(keep, "rows", steps).astype(F32) for steps in (1, 2, 3)]
    keep = (keep.astype(F32) + two) + (one + three)
    give = swap(keep, "sub")
    kernel_grad = jnp.where(side == 0, jnp.concatenate([keep, give]), jnp.concatenate([give, keep]))

    totals = jnp.where(lower, pixel_total(reduced.reshape(micros * 16, channels)), totals)
    totals = totals.reshape(micros, 16, channels)
    (grads,) = call(
        functools.partial(last_kernel, rows, cols, micros, count),
        "input_gradient",
        micros,
        [place],
        [sums, mix],
        [totals, acts, norm, result],
        [((micros, pixels, channels), BF16)],
    )
    parameter = jnp.sum(totals, axis=0)
    parameter = jnp.concatenate([parameter[:8], parameter[8:]], axis=1)
    return (
        grads.reshape(activations.shape),
        kernel_grad[None],
        parameter[None, :latents],
        parameter[None, latents],
    )


def solution(mesh):
    pair = mesh.shape["segment"] == 2 and mesh.shape["rows"] == 4 and mesh.shape["sub"] == 2
    body = pair_body if pair else general_body
    placed = (
        P("segment", "groups", "rows", "sub", None),
        P("groups", None, "rows", "sub"),
        P("groups", None, "rows", "sub"),
        P("groups", None, "rows", "sub"),
        P("groups", None, None),
        P("segment", None, None),
        P("segment", None, None),
        P("segment", None),
        P("segment", None),
        P(),
    )
    return jax.shard_map(
        body,
        mesh=mesh,
        in_specs=placed,
        out_specs=(
            P("segment", "groups", "rows", "sub", None),
            P("segment", "groups", None),
            P("segment", "groups", None),
            P("segment", "groups"),
        ),
        check_vma=False,
    )
```

```python
import functools

import jax
import jax.numpy as jnp
from jax import lax
from jax.experimental import pallas as pl
from jax.experimental.pallas import tpu as pltpu
from jax.sharding import PartitionSpec as P

GROUPS = 32
TILE = 32


EPS = 1e-06


def extended(block, sides, width):
    for axis, dim in sides:
        count = lax.axis_size(axis)
        forward = [(i, i + 1) for i in range(count - 1)]
        backward = [(target, source) for source, target in forward]
        low = lax.ppermute(
            lax.slice_in_dim(block, block.shape[dim] - width, None, axis=dim), axis, forward
        )
        high = lax.ppermute(lax.slice_in_dim(block, 0, width, axis=dim), axis, backward)
        block = jnp.concatenate([low, block, high], axis=dim)
    return block


def from_behind(value, axis, steps):
    count = lax.axis_size(axis)
    initial, last = (max(0, -steps), min(count, count - steps))
    return lax.ppermute(value, axis, [(source, source + steps) for source in range(initial, last)])


def crop_weights(boxes, row_start, col_start, row_count, col_count, total_rows, total_cols):
    row_tile = (row_start + jnp.arange(row_count, dtype=jnp.int32)) // TILE
    col_tile = (col_start + jnp.arange(col_count, dtype=jnp.int32)) // TILE
    first_row = boxes[:, :, 0:1]
    first_col = boxes[:, :, 1:2]
    box_height = boxes[:, :, 2:3]
    box_width = boxes[:, :, 3:4]
    in_rows = ((row_tile >= first_row) & (row_tile < first_row + box_height)).astype(jnp.float32)
    in_cols = ((col_tile >= first_col) & (col_tile < first_col + box_width)).astype(jnp.float32)
    tiles = total_rows // TILE * (total_cols // TILE)
    share = tiles / (boxes.shape[1] * (box_height * box_width).astype(jnp.float32))
    return jnp.einsum("mkr,mkc->mrc", in_rows * share, in_cols)


def top_gradient(recon, target, cropped, out_weight):
    diff = 2.0 * (recon.astype(jnp.float32) - target.astype(jnp.float32)) * cropped[:, None]
    return jnp.einsum("mkhw,kc->mhwc", diff, out_weight.astype(jnp.float32)).astype(jnp.bfloat16)


def loss_gradient(
    boxes,
    recon,
    target,
    out_weight,
    row_start,
    col_start,
    row_count,
    col_count,
    total_rows,
    total_cols,
):
    cropped = crop_weights(
        boxes, row_start, col_start, row_count, col_count, total_rows, total_cols
    )
    return top_gradient(recon, target, cropped, out_weight)


def grouped_layout(value_array):
    return value_array.reshape(value_array.shape[:-1] + (GROUPS, value_array.shape[-1] // GROUPS))


def group_sums(value_array):
    shaped = grouped_layout(value_array)
    return (jnp.sum(shaped, axis=(-4, -3, -1)), jnp.sum(shaped * shaped, axis=(-4, -3, -1)))


def expand(stat):
    return stat[..., None, None, :, None]


def normalized_values(value_array, mean_val, rstd_val):
    shaped = grouped_layout(value_array)
    return ((shaped - expand(mean_val)) * expand(rstd_val)).reshape(value_array.shape)


def modulation(latent_batch, mix_weight, scale_row, shift_row):
    channel_count = scale_row.shape[-1]
    coefficients = jnp.einsum(
        "bzhw,zc->bhwc", latent_batch.astype(jnp.float32), mix_weight.astype(jnp.float32)
    )
    return (
        coefficients[..., :channel_count] + scale_row.astype(jnp.float32),
        coefficients[..., channel_count:] + shift_row.astype(jnp.float32),
    )


def transposed(weights):
    channel_count = weights.shape[-1]
    return (
        weights.reshape(9, channel_count, channel_count)
        .transpose(0, 2, 1)
        .reshape(9 * channel_count, channel_count)
    )


def taps(padded, row_count, col_count, flipped):
    pieces = []
    for tap_row in range(3):
        for tap_col in range(3):
            if flipped:
                row_offset, col_offset = (2 - tap_row, 2 - tap_col)
            else:
                row_offset, col_offset = (tap_row, tap_col)
            pieces.append(
                padded[:, row_offset : row_offset + row_count, col_offset : col_offset + col_count]
            )
    return jnp.concatenate(pieces, axis=-1).reshape(-1, 9 * padded.shape[-1])


def pick(value_array, index):
    return lax.dynamic_slice_in_dim(value_array, index, 1, 0)


def section_backward(
    value_array, latent_batch, incoming, spatial_scale, spatial_shift, weights_t, count
):
    batch, row_count, col_count, channel_count = value_array.shape
    sum_one, sum_two = group_sums(value_array)
    sum_one, sum_two = lax.psum((sum_one, sum_two), ("rows", "sub"))
    group_mean = sum_one / count
    inverse_deviation = lax.rsqrt(sum_two / count - group_mean * group_mean + EPS)
    centered_scaled = normalized_values(value_array, group_mean, inverse_deviation)
    pre_activation = centered_scaled * spatial_scale + spatial_shift
    hidden = jax.nn.silu(pre_activation).astype(jnp.bfloat16)
    padded_h = extended(hidden, (("rows", 1), ("sub", 2)), 1)
    padded_g = extended(incoming, (("rows", 1), ("sub", 2)), 1)
    patches = taps(padded_h, row_count, col_count, False)
    kernel_term = lax.dot_general(
        patches,
        incoming.reshape(-1, channel_count),
        (((0,), (0,)), ((), ())),
        preferred_element_type=jnp.float32,
    )
    hidden_grad = jnp.dot(
        taps(padded_g, row_count, col_count, True), weights_t, preferred_element_type=jnp.float32
    ).reshape(value_array.shape)
    sig = jax.nn.sigmoid(pre_activation)
    pre_activation_gradient = hidden_grad * (sig * (1.0 + pre_activation * (1.0 - sig)))
    paired_parts = jnp.concatenate(
        [pre_activation_gradient * centered_scaled, pre_activation_gradient], axis=-1
    )
    mod_term = jnp.einsum("bzhw,bhwc->zc", latent_batch.astype(jnp.float32), paired_parts)
    bias_term = jnp.sum(paired_parts, axis=(0, 1, 2))
    shaped_grad = grouped_layout(pre_activation_gradient * spatial_scale)
    reshaped_normalized = grouped_layout(centered_scaled)
    part_one = jnp.sum(shaped_grad, axis=(1, 2, 4))
    part_two = jnp.sum(shaped_grad * reshaped_normalized, axis=(1, 2, 4))
    part_one, part_two = lax.psum((part_one, part_two), ("rows", "sub"))
    mean_grad = part_one / count
    mean_cross = part_two / count
    adjust = expand(inverse_deviation) * (
        shaped_grad - expand(mean_grad) - reshaped_normalized * expand(mean_cross)
    )
    result = (incoming.astype(jnp.float32) + adjust.reshape(value_array.shape)).astype(jnp.bfloat16)
    return (result, kernel_term, mod_term, bias_term)


def general_body(
    activations,
    latent,
    recon,
    target,
    boxes,
    kernel,
    mod_weight,
    scale_bias,
    shift_bias,
    out_weight,
):
    segments = lax.axis_size("segment")
    segment_index = lax.axis_index("segment")
    micro, row_count, col_count, channel_count = activations.shape[1:]
    total_rows = row_count * lax.axis_size("rows")
    total_cols = col_count * lax.axis_size("sub")
    count = total_rows * total_cols * (channel_count // GROUPS)
    row_start = lax.axis_index("rows") * row_count
    col_start = lax.axis_index("sub") * col_count
    acts = activations[0]
    weights_t = transposed(kernel[0])
    mix_weight = mod_weight[0]
    scale_row = scale_bias[0]
    shift_row = shift_bias[0]
    top = loss_gradient(
        boxes,
        recon,
        target,
        out_weight,
        row_start,
        col_start,
        row_count,
        col_count,
        total_rows,
        total_cols,
    )

    def tick(step, carry):
        passing, grads_out, kernel_grad, mod_grad, bias_grad = carry
        offset = step - (segments - 1 - segment_index)
        valid = (offset >= 0) & (offset < micro)
        index = jnp.clip(offset, 0, micro - 1)
        received = from_behind(passing, "segment", -1)
        incoming = jnp.where(segment_index == segments - 1, pick(top, index), received)
        value_array = pick(acts, index).astype(jnp.float32)
        latent_m = pick(latent, index)
        spatial_scale, spatial_shift = modulation(latent_m, mix_weight, scale_row, shift_row)
        result, kernel_term, mod_term, bias_term = section_backward(
            value_array, latent_m, incoming, spatial_scale, spatial_shift, weights_t, count
        )
        weight = valid.astype(jnp.float32)
        current = pick(grads_out, index)
        grads_out = lax.dynamic_update_slice_in_dim(
            grads_out, jnp.where(valid, result, current), index, 0
        )
        return (
            result,
            grads_out,
            kernel_grad + weight * kernel_term,
            mod_grad + weight * mod_term,
            bias_grad + weight * bias_term,
        )

    initial = (
        jnp.zeros((1, row_count, col_count, channel_count), jnp.bfloat16),
        jnp.zeros_like(acts),
        jnp.zeros((9 * channel_count, channel_count), jnp.float32),
        jnp.zeros((mix_weight.shape[0], 2 * channel_count), jnp.float32),
        jnp.zeros((2 * channel_count,), jnp.float32),
    )
    final = lax.fori_loop(0, micro + segments - 1, tick, initial)
    grads_out = final[1][None]
    kernel_grad = final[2][None]
    mod_grad = final[3][None]
    bias_grad = final[4][None]
    kernel_grad, mod_grad, bias_grad = lax.psum((kernel_grad, mod_grad, bias_grad), ("rows", "sub"))
    return (grads_out, kernel_grad, mod_grad, bias_grad)


EXACT = lax.Precision.HIGHEST
TN = (((0,), (0,)), ((), ()))
NT = (((1,), (1,)), ((), ()))
F32 = jnp.float32
BF16 = jnp.bfloat16


def swap(value, axis):
    return lax.ppermute(value, axis, [(0, 1), (1, 0)])


def shift(value, axis, steps):
    count = lax.axis_size(axis)
    return lax.ppermute(value, axis, [(i, (i + steps) % count) for i in range(count)])


def swap_and_shift(value, steps):
    count = lax.axis_size("rows")
    pairs = [(2 * i + s, 2 * ((i + steps) % count) + 1 - s) for i in range(count) for s in range(2)]
    return lax.ppermute(value, ("rows", "segment"), pairs)


def pixel_total(value):
    value = value + swap(value, "sub")
    one, two, three = [shift(value, "rows", steps) for steps in (1, 2, 3)]
    return (value + two) + (one + three)


def same_group(channels):
    per = channels // GROUPS
    left = lax.broadcasted_iota(jnp.int32, (channels, channels), 0) // per
    right = lax.broadcasted_iota(jnp.int32, (channels, channels), 1) // per
    return (left == right).astype(F32)


def statistics(sums_ref, micro, micros, member, count):
    both = jnp.concatenate([sums_ref[pl.ds(micro, 1), :], sums_ref[pl.ds(micros + micro, 1), :]], axis=0)
    both = jnp.dot(both, member, precision=EXACT, preferred_element_type=F32) / count
    mean = both[0:1]
    return mean, lax.rsqrt(both[1:2] - mean * mean + EPS)


def gradient_means(total, mix, member, count):
    mean_grad = jnp.sum(mix[:8] * total[8:], axis=0, keepdims=True)
    mean_cross = jnp.sum(mix[:8] * total[:8], axis=0, keepdims=True)
    both = jnp.concatenate([mean_grad, mean_cross], axis=0)
    both = jnp.dot(both, member, precision=EXACT, preferred_element_type=F32) / count
    return both[0:1], both[1:2]


def side_by_side(mix):
    return jnp.concatenate([mix[:8], mix[8:]], axis=1).astype(BF16)


def sums_kernel(acts_ref, out_ref):
    micro, micros = pl.program_id(0), pl.num_programs(0)
    value = acts_ref[0].astype(F32)
    out_ref[pl.ds(micro, 1), :] = jnp.sum(value, axis=0, keepdims=True)
    out_ref[pl.ds(micros + micro, 1), :] = jnp.sum(value * value, axis=0, keepdims=True)


class Top:
    def __init__(self, shape, micro, place_ref, boxes_ref, weight_ref, up_ref, diff_ref, down_ref):
        self.rows, self.cols, total_rows, total_cols, crops = shape
        self.refs = (up_ref, diff_ref, down_ref)
        self.side, self.row_start = place_ref[1], place_ref[2]
        lane = lax.broadcasted_iota(jnp.int32, (1, self.cols), 1)
        tiles = total_rows // TILE * (total_cols // TILE)
        self.boxes = []
        for k in range(crops):
            row, col, height, width = [boxes_ref[micro, k, i] for i in range(4)]
            area = jnp.full((1, self.cols), crops * height * width, jnp.int32).astype(F32)
            share = tiles / area
            inside = []
            for side in (self.side, 1 - self.side):
                at = lane + side * self.cols
                inside.append(jnp.where((at >= col * TILE) & (at < (col + width) * TILE), share, 0.0))
            self.boxes.append((row * TILE, (row + height) * TILE, inside[0], inside[1]))
        weight = weight_ref[...].astype(F32)
        blank = jnp.zeros((8 - weight.shape[0], weight.shape[1]), F32)
        own = jnp.concatenate([weight, blank])
        other = jnp.concatenate([blank[:3], weight, blank[3:]])
        self.own = jnp.concatenate([own] * 3).astype(BF16)
        self.other = jnp.concatenate([other] * 3).astype(BF16)

    def row(self, index):
        up_ref, diff_ref, down_ref = self.refs
        if index < 2:
            diff = up_ref[0, index]
        elif index < self.rows + 2:
            diff = diff_ref[0, index - 2]
        else:
            diff = down_ref[0, index - self.rows - 2]
        at = self.row_start + (index - 2)
        own = jnp.zeros((1, self.cols), F32)
        other = jnp.zeros((1, self.cols), F32)
        for first, end, own_share, other_share in self.boxes:
            here = (at >= first) & (at < end)
            own = own + jnp.where(here, own_share, 0.0)
            other = other + jnp.where(here, other_share, 0.0)
        plane = lax.broadcasted_iota(jnp.int32, (8, self.cols), 0)
        diff = 2.0 * diff * jnp.where(plane < 3, own, other)
        high = diff.astype(BF16).astype(F32)
        middle = (diff - high).astype(BF16).astype(F32)
        parts = jnp.concatenate([high, middle, diff - high - middle]).astype(BF16)
        value = lax.dot_general(parts, self.own, TN, preferred_element_type=F32).astype(BF16)
        beside = lax.dot_general(parts, self.other, TN, preferred_element_type=F32).astype(BF16).astype(F32)
        return value, jnp.where(self.side == 0, beside[0:1], beside[self.cols - 1 : self.cols])

    def main_row(self, r):
        return self.row(r + 2)[0]


def spread(index, cols, value, near, side, shifted):
    channels = value.shape[-1]
    at = slice(index * cols, (index + 1) * cols)
    place = lax.broadcasted_iota(jnp.int32, (cols, channels), 0)
    wide = value.astype(F32)
    before = jnp.where(side == 1, near, 0.0)
    behind = jnp.where(side == 0, near, 0.0)
    shifted[at, 0:channels] = jnp.where(place == 0, before, pltpu.roll(wide, 1, 0)).astype(BF16)
    shifted[at, channels : 2 * channels] = value
    shifted[at, 2 * channels :] = jnp.where(place == cols - 1, behind, pltpu.roll(wide, cols - 1, 0)).astype(BF16)


def tap_of(row, col):
    return 3 * (2 - row) + (2 - col)


def arrange_weights(kernel_ref, weights):
    channels = kernel_ref.shape[-1]
    for row in range(3):
        for col in range(3):
            tap = tap_of(row, col)
            weights[row, :, col * channels : (col + 1) * channels] = kernel_ref[tap * channels : (tap + 1) * channels, :]


def hidden_gradient(rows, cols, shifted, weights, hidden_grad):
    pixels = rows * cols
    total = lax.dot_general(shifted[0:pixels, :], weights[0], NT, preferred_element_type=F32)
    total = total + lax.dot_general(shifted[cols : cols + pixels, :], weights[1], NT, preferred_element_type=F32)
    hidden_grad[0:pixels, :] = total + lax.dot_general(
        shifted[2 * cols : 2 * cols + pixels, :], weights[2], NT, preferred_element_type=F32
    )


def pixel_values(acts, latent, mix, mean, rstd):
    channels = mean.shape[-1]
    xhat = (acts.astype(F32) - mean) * rstd
    mixed = lax.dot_general(latent, mix, TN, preferred_element_type=F32)
    scale = mixed[:, :channels]
    pre = xhat * scale + mixed[:, channels:]
    sig = 0.5 * jnp.tanh(0.5 * pre) + 0.5
    hidden = pre * sig
    return xhat, scale, hidden, sig + hidden * (1.0 - sig)


def block_step(
    rows, cols, mean, rstd, mix, acts_ref, latent_ref, norm_ref, reduced_ref, shifted, weights, hidden_grad, hidden_keep, pairs, total_kernel
):
    channels = acts_ref.shape[-1]
    pixels = rows * cols
    hidden_gradient(rows, cols, shifted, weights, hidden_grad)
    for r in range(rows):
        at = slice(r * cols, (r + 1) * cols)
        latent = latent_ref[0, :, (r + 1) * cols : (r + 2) * cols]
        xhat, scale, hidden, slope = pixel_values(acts_ref[0, at, :], latent, mix, mean, rstd)
        hidden_keep[at, :] = hidden.astype(BF16)
        pre_grad = hidden_grad[at, :] * slope
        norm_ref[0, at, :] = (pre_grad * scale).astype(BF16)
        pairs[at, 0:channels] = (pre_grad * xhat).astype(BF16)
        pairs[at, channels:] = pre_grad.astype(BF16)
    reduced = jnp.dot(latent_ref[0, :, cols : cols + pixels], pairs[...], preferred_element_type=F32)
    reduced_ref[0, 0:8, :] = reduced[:, :channels]
    reduced_ref[0, 8:16, :] = reduced[:, channels:]
    for row in range(3):
        total_kernel[row] += lax.dot_general(
            hidden_keep[...], shifted[row * cols : row * cols + pixels, :], TN, preferred_element_type=F32
        )


def write_kernel_grad(total_kernel, side, keep_ref, give_ref):
    half, channels = keep_ref.shape
    for which in range(2):
        for ref, owner in ((keep_ref, which), (give_ref, 1 - which)):

            @pl.when(side == owner)
            def _(ref=ref, first=which * half):
                for row in range(3):
                    for col in range(3):
                        at = tap_of(row, col) * channels - first
                        low, high = max(at, 0), min(at + channels, half)
                        if low < high:
                            ref[low:high, :] = total_kernel[row, low - at : high - at, col * channels : (col + 1) * channels]


def upper_kernel(
    shape,
    micros,
    count,
    place_ref,
    boxes_ref,
    sums_ref,
    mix_ref,
    weight_ref,
    kernel_ref,
    up_ref,
    diff_ref,
    down_ref,
    acts_ref,
    latent_ref,
    norm_ref,
    reduced_ref,
    keep_ref,
    give_ref,
    shifted,
    weights,
    hidden_grad,
    hidden_keep,
    pairs,
    total_kernel,
):
    step = pl.program_id(0)
    rows, cols = shape[:2]
    active = place_ref[0] == 1

    @pl.when(active)
    def _():
        @pl.when(step == 0)
        def _():
            arrange_weights(kernel_ref, weights)
            total_kernel[...] = jnp.zeros_like(total_kernel)

        mean, rstd = statistics(sums_ref, step, micros, same_group(acts_ref.shape[-1]), count)
        top = Top(shape, step, place_ref, boxes_ref, weight_ref, up_ref, diff_ref, down_ref)
        for r in range(rows + 2):
            spread(r, cols, *top.row(r + 1), place_ref[1], shifted)
        block_step(
            rows,
            cols,
            mean,
            rstd,
            side_by_side(mix_ref[...]),
            acts_ref,
            latent_ref,
            norm_ref,
            reduced_ref,
            shifted,
            weights,
            hidden_grad,
            hidden_keep,
            pairs,
            total_kernel,
        )

        @pl.when(step == micros - 1)
        def _():
            write_kernel_grad(total_kernel, place_ref[1], keep_ref, give_ref)

    @pl.when(jnp.logical_not(active))
    def _():
        reduced_ref[...] = jnp.zeros_like(reduced_ref)


def redo_kernel(
    shape,
    micros,
    count,
    place_ref,
    boxes_ref,
    packed_ref,
    weight_ref,
    kernel_ref,
    up_ref,
    diff_ref,
    down_ref,
    acts_ref,
    norm_ref,
    passed_early_ref,
    passed_late_ref,
    above_ref,
    below_ref,
    latent_ref,
    result_ref,
    edge_ref,
    shifted,
    weights,
    hidden_grad,
):
    step = pl.program_id(0)
    rows, cols, total_rows = shape[:3]
    channels = acts_ref.shape[-1]
    upper = place_ref[0] == 1
    side = place_ref[1]
    member = same_group(channels)
    mean, rstd = statistics(packed_ref, step, micros, member, count)
    mix = packed_ref[2 * micros + 16 * micros :, :]
    total = packed_ref[pl.ds(pl.multiple_of(2 * micros + 16 * step, 8), 16), :]
    mean_grad, mean_cross = gradient_means(total, mix, member, count)
    top = Top(shape, step, place_ref, boxes_ref, weight_ref, up_ref, diff_ref, down_ref)

    @pl.when(upper)
    def _():
        for r in range(rows):
            at = slice(r * cols, (r + 1) * cols)
            xhat = (acts_ref[0, at, :].astype(F32) - mean) * rstd
            change = rstd * (norm_ref[0, at, :].astype(F32) - mean_grad - xhat * mean_cross)
            result_ref[0, (r + 1) * cols : (r + 2) * cols, :] = (top.main_row(r).astype(F32) + change).astype(BF16)

    @pl.when(jnp.logical_not(upper))
    def _():
        @pl.when(step == 0)
        def _():
            arrange_weights(kernel_ref, weights)

        for r in range(rows + 4):
            spread(r, cols, *top.row(r), side, shifted)
        hidden_gradient(rows + 2, cols, shifted, weights, hidden_grad)
        wide_mix = side_by_side(mix)
        edges = []
        for r in range(rows + 2):
            at = slice(r * cols, (r + 1) * cols)
            if r == 0:
                acts = above_ref[0]
            elif r == rows + 1:
                acts = below_ref[0]
            else:
                row = slice((r - 1) * cols, r * cols)
                acts = jnp.where(step < micros // 2, passed_early_ref[0, row, :], passed_late_ref[0, row, :])
            xhat, scale, _, slope = pixel_values(acts, latent_ref[0, :, at], wide_mix, mean, rstd)
            change = rstd * (hidden_grad[at, :] * slope * scale - mean_grad - xhat * mean_cross)
            middle = shifted[(r + 1) * cols : (r + 2) * cols, channels : 2 * channels]
            value = middle.astype(F32) + change
            if r == 0 or r == rows + 1:
                row = place_ref[2] + (r - 1)
                value = jnp.where((row >= 0) & (row < total_rows), value, 0.0)
            result_ref[0, at, :] = value.astype(BF16)
            edges.append(jnp.where(side == 0, value[cols - 1 : cols], value[0:1]))
        edges.append(jnp.zeros((16 - rows - 2, channels), F32))
        edge_ref[0] = jnp.concatenate(edges).astype(BF16)


def lower_kernel(
    shape,
    micros,
    count,
    place_ref,
    sums_ref,
    mix_ref,
    kernel_ref,
    grad_ref,
    near_ref,
    acts_ref,
    latent_ref,
    before_keep_ref,
    before_give_ref,
    norm_ref,
    reduced_ref,
    keep_ref,
    give_ref,
    shifted,
    weights,
    hidden_grad,
    hidden_keep,
    pairs,
    total_kernel,
):
    step = pl.program_id(0)
    rows, cols = shape[:2]
    active = place_ref[0] == 0

    @pl.when(active)
    def _():
        @pl.when(step == 0)
        def _():
            arrange_weights(kernel_ref, weights)
            total_kernel[...] = jnp.zeros_like(total_kernel)

        mean, rstd = statistics(sums_ref, step, micros, same_group(acts_ref.shape[-1]), count)
        near = near_ref[0].astype(F32)
        for r in range(rows + 2):
            spread(r, cols, grad_ref[0, r * cols : (r + 1) * cols, :], near[r : r + 1], place_ref[1], shifted)
        block_step(
            rows,
            cols,
            mean,
            rstd,
            side_by_side(mix_ref[...]),
            acts_ref,
            latent_ref,
            norm_ref,
            reduced_ref,
            shifted,
            weights,
            hidden_grad,
            hidden_keep,
            pairs,
            total_kernel,
        )

        @pl.when(step == micros - 1)
        def _():
            write_kernel_grad(total_kernel, place_ref[1], keep_ref, give_ref)

    @pl.when(jnp.logical_not(active))
    def _():
        reduced_ref[...] = jnp.zeros_like(reduced_ref)

        @pl.when(step == micros - 1)
        def _():
            keep_ref[...] = before_keep_ref[...]
            give_ref[...] = before_give_ref[...]


def last_kernel(rows, cols, micros, count, place_ref, sums_ref, mix_ref, total_ref, acts_ref, norm_ref, grad_ref, result_ref):
    step = pl.program_id(0)
    lower = place_ref[0] == 0

    @pl.when(lower)
    def _():
        member = same_group(acts_ref.shape[-1])
        mean, rstd = statistics(sums_ref, step, micros, member, count)
        mean_grad, mean_cross = gradient_means(total_ref[0], mix_ref[...], member, count)
        for r in range(rows):
            at = slice(r * cols, (r + 1) * cols)
            xhat = (acts_ref[0, at, :].astype(F32) - mean) * rstd
            change = rstd * (norm_ref[0, at, :].astype(F32) - mean_grad - xhat * mean_cross)
            result_ref[0, at, :] = (grad_ref[0, (r + 1) * cols : (r + 2) * cols, :].astype(F32) + change).astype(BF16)

    @pl.when(jnp.logical_not(lower))
    def _():
        result_ref[0] = grad_ref[0, cols : (rows + 1) * cols, :]


def by_micro(value):
    if isinstance(value, tuple):
        value, first, size = value
        return pl.BlockSpec((1,) + tuple(value.shape[1:]), lambda m: (jnp.clip(m - first, 0, size - 1), 0, 0))
    rest = (0,) * (len(value.shape) - 1)
    return pl.BlockSpec((1,) + tuple(value.shape[1:]), lambda m: (m,) + rest)


def whole(value):
    return pl.BlockSpec(tuple(value.shape), lambda m: (0,) * len(value.shape))


def call(kernel, name, micros, scalars, fixed, per_micro, outs, fixed_outs=(), scratch=(), tail=(), work=4, room=62):
    out_shape = [jax.ShapeDtypeStruct(s, d) for s, d in outs] + [jax.ShapeDtypeStruct(s, d) for s, d in fixed_outs]
    return pl.pallas_call(
        kernel,
        grid=(micros,),
        in_specs=[pl.BlockSpec(memory_space=pltpu.SMEM) for _ in scalars]
        + [whole(v) for v in fixed]
        + [by_micro(v) for v in per_micro]
        + [whole(v) for v in tail],
        out_specs=[by_micro(s) for s in out_shape[: len(outs)]] + [whole(s) for s in out_shape[len(outs) :]],
        out_shape=out_shape,
        scratch_shapes=[pltpu.VMEM(s, d) for s, d in scratch],
        compiler_params=pltpu.CompilerParams(vmem_limit_bytes=room * 1024 * 1024),
        cost_estimate=pl.CostEstimate(flops=work, bytes_accessed=work // 4, transcendentals=0),
        name=name,
    )(*scalars, *fixed, *[v[0] if isinstance(v, tuple) else v for v in per_micro], *tail)


def pair_body(
    activations, latent, recon, target, boxes, kernel, mod_weight, scale_bias, shift_bias, out_weight
):
    micros, rows, cols, channels = activations.shape[1:]
    latents, colors = latent.shape[1], recon.shape[1]
    pixels = rows * cols
    bands = lax.axis_size("rows")
    total_rows, total_cols = rows * bands, cols * 2
    count = float(total_rows * total_cols * (channels // GROUPS))
    segment = lax.axis_index("segment")
    side = lax.axis_index("sub")
    place = jnp.stack([segment, side, lax.axis_index("rows") * rows]).astype(jnp.int32)
    acts = activations[0].reshape(micros, pixels, channels)

    early = micros // 2
    passed = [swap(acts[:early], "segment"), swap(acts[early:], "segment")]
    above = swap_and_shift(acts[:, pixels - cols :], 1)
    below = swap_and_shift(acts[:, :cols], bands - 1)
    kernel_passed = swap(kernel[0], "segment")

    (sums,) = call(sums_kernel, "input_sums", micros, [], [], [acts], [], [((2 * micros, channels), F32)], room=16)
    diff = (recon.astype(F32) - target.astype(F32)).transpose(0, 2, 1, 3)
    flat = diff.reshape(micros * rows * colors, channels)
    got = swap(jnp.concatenate([sums, flat]), "sub")
    sums = sums + got[: 2 * micros]
    other = got[2 * micros :].reshape(diff.shape)

    def border(first, r):
        extra = latent[:, :, r].astype(F32).reshape(micros, 2, latents // 2, cols)
        two = jnp.concatenate([diff[:, first : first + 2], other[:, first : first + 2], extra], axis=2)
        return jnp.concatenate([sums, two.reshape(micros * 16, cols)])

    from_up = shift(border(rows - 2, rows - 1), "rows", 1)
    from_down = shift(border(0, 0), "rows", bands - 1)
    across = shift(sums, "rows", 2)
    sums = (sums + across) + (from_up[: 2 * micros] + from_down[: 2 * micros])
    up = from_up[2 * micros :].reshape(micros, 2, 8, cols)
    down = from_down[2 * micros :].reshape(micros, 2, 8, cols)
    diff = jnp.concatenate([diff, other, jnp.zeros((micros, rows, 2, cols), F32)], axis=2)
    beyond = [v[:, :, 6:8].reshape(micros, latents, cols).astype(BF16) for v in (up, down)]
    wide = (rows + 2) * cols
    latent = jnp.concatenate([beyond[0], latent.reshape(micros, latents, pixels), beyond[1]], axis=2)
    latent = jnp.concatenate(
        [latent, jnp.ones((micros, 1, wide), BF16), jnp.zeros((micros, 7 - latents, wide), BF16)], axis=1
    )
    mix = jnp.concatenate([mod_weight[0], jnp.concatenate([scale_bias, shift_bias], axis=1)]).astype(F32)
    mix = jnp.pad(mix, ((0, 7 - latents), (0, 0)))
    mix = jnp.concatenate([mix[:, :channels], mix[:, channels:]])

    shape = (rows, cols, total_rows, total_cols, boxes.shape[1])
    triple = 3 * channels
    work = [
        ((wide, triple), BF16),
        ((3, channels, triple), BF16),
        ((pixels, channels), F32),
        ((pixels, channels), BF16),
        ((pixels, 2 * channels), BF16),
        ((3, channels, triple), F32),
    ]
    produced = [((micros, pixels, channels), BF16), ((micros, 16, channels), F32)]
    kernel_shape = [((kernel.shape[1] // 2, channels), F32)] * 2
    up, above, below, kernel_passed = lax.optimization_barrier((up, above, below, kernel_passed))
    norm_upper, reduced, *kernel_grad = call(
        functools.partial(upper_kernel, shape, micros, count),
        "upper_block",
        micros,
        [place, boxes],
        [sums, mix, out_weight, kernel[0]],
        [up, diff, down, acts, latent],
        produced,
        kernel_shape,
        work,
    )
    reduced, passed[0] = lax.optimization_barrier((reduced, passed[0]))
    totals = pixel_total(reduced.reshape(micros * 16, channels))
    lower = segment == 0
    packed = jnp.concatenate([sums, totals, mix])
    packed, passed[1] = lax.optimization_barrier((packed, passed[1]))
    packed = jnp.where(lower, swap(packed, "segment"), packed)
    result, edge = call(
        functools.partial(redo_kernel, shape, micros, count),
        "redo_upper",
        micros,
        [place, boxes],
        [packed, out_weight, kernel_passed],
        [up, diff, down, acts, norm_upper, (passed[0], 0, early), (passed[1], early, micros - early), above, below, latent],
        [((micros, wide, channels), BF16), ((micros, 16, channels), BF16)],
        (),
        [(((rows + 4) * cols, triple), BF16), ((3, channels, triple), BF16), ((wide, channels), F32)],
    )
    near = swap(edge, "sub")
    norm, reduced, keep, give = call(
        functools.partial(lower_kernel, shape, micros, count),
        "lower_block",
        micros,
        [place],
        [sums, mix, kernel[0]],
        [result, near, acts, latent],
        produced,
        kernel_shape,
        work,
        kernel_grad,
    )

    keep = (keep + swap(give, "sub")).astype(BF16)
    others = [shift(keep, "rows", steps) for steps in (1, 2, 3)]
    totals = jnp.where(lower, pixel_total(reduced.reshape(micros * 16, channels)), totals)
    totals = totals.reshape(micros, 16, channels)
    (grads,) = call(
        functools.partial(last_kernel, rows, cols, micros, count),
        "input_gradient",
        micros,
        [place],
        [sums, mix],
        [totals, acts, norm, result],
        [((micros, pixels, channels), BF16)],
        work=1 << 25,
    )
    grads, *others = lax.optimization_barrier((grads, *others))
    one, two, three = [value.astype(F32) for value in others]
    keep = (keep.astype(F32) + two) + (one + three)
    give = swap(keep, "sub")
    kernel_grad = jnp.where(side == 0, jnp.concatenate([keep, give]), jnp.concatenate([give, keep]))

    parameter = jnp.sum(totals, axis=0)
    parameter = jnp.concatenate([parameter[:8], parameter[8:]], axis=1)
    return (
        grads.reshape(activations.shape),
        kernel_grad[None],
        parameter[None, :latents],
        parameter[None, latents],
    )


def solution(mesh):
    pair = mesh.shape["segment"] == 2 and mesh.shape["rows"] == 4 and mesh.shape["sub"] == 2
    body = pair_body if pair else general_body
    placed = (
        P("segment", "groups", "rows", "sub", None),
        P("groups", None, "rows", "sub"),
        P("groups", None, "rows", "sub"),
        P("groups", None, "rows", "sub"),
        P("groups", None, None),
        P("segment", None, None),
        P("segment", None, None),
        P("segment", None),
        P("segment", None),
        P(),
    )
    return jax.shard_map(
        body,
        mesh=mesh,
        in_specs=placed,
        out_specs=(
            P("segment", "groups", "rows", "sub", None),
            P("segment", "groups", None),
            P("segment", "groups", None),
            P("segment", "groups"),
        ),
        check_vma=False,
    )
```

```python
import functools
import types

import jax
import jax.numpy as jnp
from jax import lax
from jax.experimental import pallas as pl
from jax.experimental.pallas import tpu as pltpu
from jax.sharding import PartitionSpec as P

GROUPS = 32
TILE = 32


EPS = 1e-06


def extended(block, sides, width):
    for axis, dim in sides:
        count = lax.axis_size(axis)
        forward = [(i, i + 1) for i in range(count - 1)]
        backward = [(target, source) for source, target in forward]
        low = lax.ppermute(
            lax.slice_in_dim(block, block.shape[dim] - width, None, axis=dim), axis, forward
        )
        high = lax.ppermute(lax.slice_in_dim(block, 0, width, axis=dim), axis, backward)
        block = jnp.concatenate([low, block, high], axis=dim)
    return block


def from_behind(value, axis, steps):
    count = lax.axis_size(axis)
    initial, last = (max(0, -steps), min(count, count - steps))
    return lax.ppermute(value, axis, [(source, source + steps) for source in range(initial, last)])


def crop_weights(boxes, row_start, col_start, row_count, col_count, total_rows, total_cols):
    row_tile = (row_start + jnp.arange(row_count, dtype=jnp.int32)) // TILE
    col_tile = (col_start + jnp.arange(col_count, dtype=jnp.int32)) // TILE
    first_row = boxes[:, :, 0:1]
    first_col = boxes[:, :, 1:2]
    box_height = boxes[:, :, 2:3]
    box_width = boxes[:, :, 3:4]
    in_rows = ((row_tile >= first_row) & (row_tile < first_row + box_height)).astype(jnp.float32)
    in_cols = ((col_tile >= first_col) & (col_tile < first_col + box_width)).astype(jnp.float32)
    tiles = total_rows // TILE * (total_cols // TILE)
    share = tiles / (boxes.shape[1] * (box_height * box_width).astype(jnp.float32))
    return jnp.einsum("mkr,mkc->mrc", in_rows * share, in_cols)


def top_gradient(recon, target, cropped, out_weight):
    diff = 2.0 * (recon.astype(jnp.float32) - target.astype(jnp.float32)) * cropped[:, None]
    return jnp.einsum("mkhw,kc->mhwc", diff, out_weight.astype(jnp.float32)).astype(jnp.bfloat16)


def loss_gradient(
    boxes,
    recon,
    target,
    out_weight,
    row_start,
    col_start,
    row_count,
    col_count,
    total_rows,
    total_cols,
):
    cropped = crop_weights(
        boxes, row_start, col_start, row_count, col_count, total_rows, total_cols
    )
    return top_gradient(recon, target, cropped, out_weight)


def grouped_layout(value_array):
    return value_array.reshape(value_array.shape[:-1] + (GROUPS, value_array.shape[-1] // GROUPS))


def group_sums(value_array):
    shaped = grouped_layout(value_array)
    return (jnp.sum(shaped, axis=(-4, -3, -1)), jnp.sum(shaped * shaped, axis=(-4, -3, -1)))


def expand(stat):
    return stat[..., None, None, :, None]


def normalized_values(value_array, mean_val, rstd_val):
    shaped = grouped_layout(value_array)
    return ((shaped - expand(mean_val)) * expand(rstd_val)).reshape(value_array.shape)


def modulation(latent_batch, mix_weight, scale_row, shift_row):
    channel_count = scale_row.shape[-1]
    coefficients = jnp.einsum(
        "bzhw,zc->bhwc", latent_batch.astype(jnp.float32), mix_weight.astype(jnp.float32)
    )
    return (
        coefficients[..., :channel_count] + scale_row.astype(jnp.float32),
        coefficients[..., channel_count:] + shift_row.astype(jnp.float32),
    )


def transposed(weights):
    channel_count = weights.shape[-1]
    return (
        weights.reshape(9, channel_count, channel_count)
        .transpose(0, 2, 1)
        .reshape(9 * channel_count, channel_count)
    )


def taps(padded, row_count, col_count, flipped):
    pieces = []
    for tap_row in range(3):
        for tap_col in range(3):
            if flipped:
                row_offset, col_offset = (2 - tap_row, 2 - tap_col)
            else:
                row_offset, col_offset = (tap_row, tap_col)
            pieces.append(
                padded[:, row_offset : row_offset + row_count, col_offset : col_offset + col_count]
            )
    return jnp.concatenate(pieces, axis=-1).reshape(-1, 9 * padded.shape[-1])


def pick(value_array, index):
    return lax.dynamic_slice_in_dim(value_array, index, 1, 0)


def section_backward(
    value_array, latent_batch, incoming, spatial_scale, spatial_shift, weights_t, count
):
    batch, row_count, col_count, channel_count = value_array.shape
    sum_one, sum_two = group_sums(value_array)
    sum_one, sum_two = lax.psum((sum_one, sum_two), ("rows", "sub"))
    group_mean = sum_one / count
    inverse_deviation = lax.rsqrt(sum_two / count - group_mean * group_mean + EPS)
    centered_scaled = normalized_values(value_array, group_mean, inverse_deviation)
    pre_activation = centered_scaled * spatial_scale + spatial_shift
    hidden = jax.nn.silu(pre_activation).astype(jnp.bfloat16)
    padded_h = extended(hidden, (("rows", 1), ("sub", 2)), 1)
    padded_g = extended(incoming, (("rows", 1), ("sub", 2)), 1)
    patches = taps(padded_h, row_count, col_count, False)
    kernel_term = lax.dot_general(
        patches,
        incoming.reshape(-1, channel_count),
        (((0,), (0,)), ((), ())),
        preferred_element_type=jnp.float32,
    )
    hidden_grad = jnp.dot(
        taps(padded_g, row_count, col_count, True), weights_t, preferred_element_type=jnp.float32
    ).reshape(value_array.shape)
    sig = jax.nn.sigmoid(pre_activation)
    pre_activation_gradient = hidden_grad * (sig * (1.0 + pre_activation * (1.0 - sig)))
    paired_parts = jnp.concatenate(
        [pre_activation_gradient * centered_scaled, pre_activation_gradient], axis=-1
    )
    mod_term = jnp.einsum("bzhw,bhwc->zc", latent_batch.astype(jnp.float32), paired_parts)
    bias_term = jnp.sum(paired_parts, axis=(0, 1, 2))
    shaped_grad = grouped_layout(pre_activation_gradient * spatial_scale)
    reshaped_normalized = grouped_layout(centered_scaled)
    part_one = jnp.sum(shaped_grad, axis=(1, 2, 4))
    part_two = jnp.sum(shaped_grad * reshaped_normalized, axis=(1, 2, 4))
    part_one, part_two = lax.psum((part_one, part_two), ("rows", "sub"))
    mean_grad = part_one / count
    mean_cross = part_two / count
    adjust = expand(inverse_deviation) * (
        shaped_grad - expand(mean_grad) - reshaped_normalized * expand(mean_cross)
    )
    result = (incoming.astype(jnp.float32) + adjust.reshape(value_array.shape)).astype(jnp.bfloat16)
    return (result, kernel_term, mod_term, bias_term)


def general_body(
    activations,
    latent,
    recon,
    target,
    boxes,
    kernel,
    mod_weight,
    scale_bias,
    shift_bias,
    out_weight,
):
    segments = lax.axis_size("segment")
    segment_index = lax.axis_index("segment")
    micro, row_count, col_count, channel_count = activations.shape[1:]
    total_rows = row_count * lax.axis_size("rows")
    total_cols = col_count * lax.axis_size("sub")
    count = total_rows * total_cols * (channel_count // GROUPS)
    row_start = lax.axis_index("rows") * row_count
    col_start = lax.axis_index("sub") * col_count
    acts = activations[0]
    weights_t = transposed(kernel[0])
    mix_weight = mod_weight[0]
    scale_row = scale_bias[0]
    shift_row = shift_bias[0]
    top = loss_gradient(
        boxes,
        recon,
        target,
        out_weight,
        row_start,
        col_start,
        row_count,
        col_count,
        total_rows,
        total_cols,
    )

    def tick(step, carry):
        passing, grads_out, kernel_grad, mod_grad, bias_grad = carry
        offset = step - (segments - 1 - segment_index)
        valid = (offset >= 0) & (offset < micro)
        index = jnp.clip(offset, 0, micro - 1)
        received = from_behind(passing, "segment", -1)
        incoming = jnp.where(segment_index == segments - 1, pick(top, index), received)
        value_array = pick(acts, index).astype(jnp.float32)
        latent_m = pick(latent, index)
        spatial_scale, spatial_shift = modulation(latent_m, mix_weight, scale_row, shift_row)
        result, kernel_term, mod_term, bias_term = section_backward(
            value_array, latent_m, incoming, spatial_scale, spatial_shift, weights_t, count
        )
        weight = valid.astype(jnp.float32)
        current = pick(grads_out, index)
        grads_out = lax.dynamic_update_slice_in_dim(
            grads_out, jnp.where(valid, result, current), index, 0
        )
        return (
            result,
            grads_out,
            kernel_grad + weight * kernel_term,
            mod_grad + weight * mod_term,
            bias_grad + weight * bias_term,
        )

    initial = (
        jnp.zeros((1, row_count, col_count, channel_count), jnp.bfloat16),
        jnp.zeros_like(acts),
        jnp.zeros((9 * channel_count, channel_count), jnp.float32),
        jnp.zeros((mix_weight.shape[0], 2 * channel_count), jnp.float32),
        jnp.zeros((2 * channel_count,), jnp.float32),
    )
    final = lax.fori_loop(0, micro + segments - 1, tick, initial)
    grads_out = final[1][None]
    kernel_grad = final[2][None]
    mod_grad = final[3][None]
    bias_grad = final[4][None]
    kernel_grad, mod_grad, bias_grad = lax.psum((kernel_grad, mod_grad, bias_grad), ("rows", "sub"))
    return (grads_out, kernel_grad, mod_grad, bias_grad)


EXACT = lax.Precision.HIGHEST
TN = (((0,), (0,)), ((), ()))
NT = (((1,), (1,)), ((), ()))
F32 = jnp.float32
BF16 = jnp.bfloat16


def swap(value, axis):
    return lax.ppermute(value, axis, [(0, 1), (1, 0)])


def shift(value, axis, steps):
    count = lax.axis_size(axis)
    return lax.ppermute(value, axis, [(i, (i + steps) % count) for i in range(count)])


def swap_and_shift(value, steps):
    count = lax.axis_size("rows")
    pairs = [(2 * i + s, 2 * ((i + steps) % count) + 1 - s) for i in range(count) for s in range(2)]
    return lax.ppermute(value, ("rows", "segment"), pairs)


def pixel_total(value):
    value = value + swap(value, "sub")
    one, two, three = [shift(value, "rows", steps) for steps in (1, 2, 3)]
    return (value + two) + (one + three)


def same_group(channels):
    per = channels // GROUPS
    left = lax.broadcasted_iota(jnp.int32, (channels, channels), 0) // per
    right = lax.broadcasted_iota(jnp.int32, (channels, channels), 1) // per
    return (left == right).astype(F32)


def statistics(sums_ref, micro, micros, count):
    member = same_group(sums_ref.shape[-1])
    both = jnp.concatenate([sums_ref[pl.ds(micro, 1), :], sums_ref[pl.ds(micros + micro, 1), :]], axis=0)
    both = jnp.dot(both, member, precision=EXACT, preferred_element_type=F32) / count
    mean = both[0:1]
    return mean, lax.rsqrt(both[1:2] - mean * mean + EPS)


def gradient_means(total, mix, count):
    mean_grad = jnp.sum(mix[:8] * total[8:], axis=0, keepdims=True)
    mean_cross = jnp.sum(mix[:8] * total[:8], axis=0, keepdims=True)
    both = jnp.concatenate([mean_grad, mean_cross], axis=0)
    both = jnp.dot(both, same_group(total.shape[-1]), precision=EXACT, preferred_element_type=F32) / count
    return both[0:1], both[1:2]


def side_by_side(mix):
    return jnp.concatenate([mix[:8], mix[8:]], axis=1).astype(BF16)


def sums_kernel(n, micro):
    micros = n.sums.shape[0] // 2
    value = n.acts[0].astype(F32)
    n.sums[pl.ds(micro, 1), :] = jnp.sum(value, axis=0, keepdims=True)
    n.sums[pl.ds(micros + micro, 1), :] = jnp.sum(value * value, axis=0, keepdims=True)


class Band:
    def __init__(self, n, micro, rows, cols, bands):
        self.n, self.rows, self.cols = n, rows, cols
        self.head = n.from_up.shape[0] - 16 * (n.from_up.shape[0] // 16)
        self.micro = micro
        self.side = lax.axis_index("sub")
        self.row_start = lax.axis_index("rows") * rows
        self.total_rows = rows * bands
        lane = lax.broadcasted_iota(jnp.int32, (1, cols), 1)
        crops = n.boxes.shape[1]
        tiles = self.total_rows // TILE * (2 * cols // TILE)
        self.boxes = []
        for k in range(crops):
            row, col, height, width = [n.boxes[micro, k, i] for i in range(4)]
            share = tiles / jnp.full((1, cols), crops * height * width, jnp.int32).astype(F32)
            inside = []
            for side in (self.side, 1 - self.side):
                at = lane + side * cols
                inside.append(jnp.where((at >= col * TILE) & (at < (col + width) * TILE), share, 0.0))
            self.boxes.append((row * TILE, (row + height) * TILE, inside[0], inside[1]))
        weight = n.out_weight[...].astype(F32)
        blank = jnp.zeros((8 - weight.shape[0], weight.shape[1]), F32)
        self.own = jnp.concatenate([jnp.concatenate([weight, blank])] * 3).astype(BF16)
        self.other = jnp.concatenate([jnp.concatenate([blank[:3], weight, blank[3:]])] * 3).astype(BF16)

    def border(self, ref, which):
        return ref[pl.ds(pl.multiple_of(self.head + 16 * self.micro + 8 * which, 8), 8), :]

    def planes(self, r):
        if r < 0:
            return self.border(self.n.from_up, r + 2)
        if r >= self.rows:
            return self.border(self.n.from_down, r - self.rows)
        own = self.n.recon[0, :, r, :].astype(F32) - self.n.target[0, :, r, :].astype(F32)
        beside = self.n.recon_beside[0, :, r, :].astype(F32) - self.n.target_beside[0, :, r, :].astype(F32)
        return jnp.concatenate([own, beside, jnp.zeros((2, self.cols), F32)])

    def latent(self, r):
        if r < 0 or r >= self.rows:
            ref = self.n.from_up if r < 0 else self.n.from_down
            value = jnp.concatenate([self.border(ref, 0)[6:8], self.border(ref, 1)[6:8]])
        else:
            value = self.n.latent[0, :, r, :].astype(F32)
        count = value.shape[0]
        return jnp.concatenate([value, jnp.ones((1, self.cols), F32), jnp.zeros((7 - count, self.cols), F32)]).astype(BF16)

    def row(self, r):
        diff = self.planes(r)
        at = self.row_start + r
        own = jnp.zeros((1, self.cols), F32)
        other = jnp.zeros((1, self.cols), F32)
        for first, end, own_share, other_share in self.boxes:
            here = (at >= first) & (at < end)
            own = own + jnp.where(here, own_share, 0.0)
            other = other + jnp.where(here, other_share, 0.0)
        plane = lax.broadcasted_iota(jnp.int32, (8, self.cols), 0)
        diff = 2.0 * diff * jnp.where(plane < 3, own, other)
        high = diff.astype(BF16).astype(F32)
        middle = (diff - high).astype(BF16).astype(F32)
        parts = jnp.concatenate([high, middle, diff - high - middle]).astype(BF16)
        value = lax.dot_general(parts, self.own, TN, preferred_element_type=F32).astype(BF16)
        beside = lax.dot_general(parts, self.other, TN, preferred_element_type=F32).astype(BF16).astype(F32)
        return value, jnp.where(self.side == 0, beside[0:1], beside[self.cols - 1 : self.cols])


def spread(index, cols, value, near, shifted):
    channels = value.shape[-1]
    side = lax.axis_index("sub")
    at = slice(index * cols, (index + 1) * cols)
    place = lax.broadcasted_iota(jnp.int32, (cols, channels), 0)
    wide = value.astype(F32)
    before = jnp.where(side == 1, near, 0.0)
    behind = jnp.where(side == 0, near, 0.0)
    shifted[at, 0:channels] = jnp.where(place == 0, before, pltpu.roll(wide, 1, 0)).astype(BF16)
    shifted[at, channels : 2 * channels] = value
    shifted[at, 2 * channels :] = jnp.where(place == cols - 1, behind, pltpu.roll(wide, cols - 1, 0)).astype(BF16)


def tap_of(row, col):
    return 3 * (2 - row) + (2 - col)


def arrange_weights(kernel_ref, weights):
    channels = kernel_ref.shape[-1]
    for row in range(3):
        for col in range(3):
            tap = tap_of(row, col)
            weights[row, :, col * channels : (col + 1) * channels] = kernel_ref[tap * channels : (tap + 1) * channels, :]


def hidden_gradient(rows, cols, shifted, weights, hidden_grad):
    pixels = rows * cols
    total = lax.dot_general(shifted[0:pixels, :], weights[0], NT, preferred_element_type=F32)
    total = total + lax.dot_general(shifted[cols : cols + pixels, :], weights[1], NT, preferred_element_type=F32)
    hidden_grad[0:pixels, :] = total + lax.dot_general(
        shifted[2 * cols : 2 * cols + pixels, :], weights[2], NT, preferred_element_type=F32
    )


def pixel_values(acts, latent, mix, mean, rstd):
    channels = mean.shape[-1]
    xhat = (acts.astype(F32) - mean) * rstd
    mixed = lax.dot_general(latent, mix, TN, preferred_element_type=F32)
    scale = mixed[:, :channels]
    pre = xhat * scale + mixed[:, channels:]
    sig = 0.5 * jnp.tanh(0.5 * pre) + 0.5
    hidden = pre * sig
    return xhat, scale, hidden, sig + hidden * (1.0 - sig)


def reduce_block(n, band, mean, rstd, mix):
    rows, cols = band.rows, band.cols
    channels = n.acts.shape[-1]
    hidden_gradient(rows, cols, n.shifted, n.weights, n.hidden_grad)
    for r in range(rows):
        at = slice(r * cols, (r + 1) * cols)
        latent = band.latent(r)
        n.latent_keep[:, at] = latent
        xhat, scale, _, slope = pixel_values(n.acts[0, at, :], latent, mix, mean, rstd)
        pre_grad = n.hidden_grad[at, :] * slope
        n.norm[0, at, :] = (pre_grad * scale).astype(BF16)
        n.pairs[at, 0:channels] = (pre_grad * xhat).astype(BF16)
        n.pairs[at, channels:] = pre_grad.astype(BF16)
    reduced = jnp.dot(n.latent_keep[...], n.pairs[...], preferred_element_type=F32)
    n.reduced[0, 0:8, :] = reduced[:, :channels]
    n.reduced[0, 8:16, :] = reduced[:, channels:]


def upper_kernel(rows, cols, bands, micros, count, n, step):
    active = lax.axis_index("segment") == 1

    @pl.when(active)
    def _():
        @pl.when(step == 0)
        def _():
            arrange_weights(n.kernel, n.weights)
            head = 2 * micros
            n.sums_keep[...] = (n.sums[...] + n.across[...]) + (n.from_up[0:head, :] + n.from_down[0:head, :])

        mean, rstd = statistics(n.sums_keep, step, micros, count)
        channels = mean.shape[-1]
        mix = [n.mod_weight[0].astype(F32), jnp.concatenate([n.scale_bias[...], n.shift_bias[...]], axis=1).astype(F32)]
        mix.append(jnp.zeros((7 - mix[0].shape[0], 2 * channels), F32))
        band = Band(n, step, rows, cols, bands)
        for r in range(rows + 2):
            spread(r, cols, *band.row(r - 1), n.shifted)
        reduce_block(n, band, mean, rstd, jnp.concatenate(mix).astype(BF16))

    @pl.when(jnp.logical_not(active))
    def _():
        n.reduced[...] = jnp.zeros_like(n.reduced)


def lower_kernel(rows, cols, bands, micros, count, n, step):
    active = lax.axis_index("segment") == 0

    @pl.when(active)
    def _():
        @pl.when(step == 0)
        def _():
            arrange_weights(n.kernel, n.weights)

        mean, rstd = statistics(n.sums, step, micros, count)
        band = Band(n, step, rows, cols, bands)
        near = n.near[0].astype(F32)
        for r in range(rows + 2):
            spread(r, cols, n.result[0, r * cols : (r + 1) * cols, :], near[r : r + 1], n.shifted)
        reduce_block(n, band, mean, rstd, side_by_side(n.mix[...]))

    @pl.when(jnp.logical_not(active))
    def _():
        n.reduced[...] = jnp.zeros_like(n.reduced)


def gradient_kernel(rows, cols, bands, micros, count, n, step):
    pixels = rows * cols
    side = lax.axis_index("sub")
    segment = lax.axis_index("segment")

    @pl.when(step == 0)
    def _():
        n.total[...] = jnp.zeros_like(n.total)

    mean, rstd = statistics(n.sums, step, micros, count)
    band = Band(n, step, rows, cols, bands)

    @pl.when(segment == 1)
    def _():
        for r in range(rows + 2):
            spread(r, cols, *band.row(r - 1), n.shifted)

    @pl.when(segment == 0)
    def _():
        near = n.near[0].astype(F32)
        for r in range(rows + 2):
            spread(r, cols, n.result[0, r * cols : (r + 1) * cols, :], near[r : r + 1], n.shifted)

    mix = side_by_side(n.mix[...])
    for r in range(rows):
        at = slice(r * cols, (r + 1) * cols)
        n.hidden[at, :] = pixel_values(n.acts[0, at, :], band.latent(r), mix, mean, rstd)[2].astype(BF16)
    for row in range(3):
        n.total[row] += lax.dot_general(
            n.hidden[...], n.shifted[row * cols : row * cols + pixels, :], TN, preferred_element_type=F32
        )

    @pl.when(step == micros - 1)
    def _():
        half, channels = n.keep.shape
        for which in range(2):
            for ref, owner in ((n.keep, which), (n.give, 1 - which)):

                @pl.when(side == owner)
                def _(ref=ref, first=which * half):
                    for row in range(3):
                        for col in range(3):
                            at = tap_of(row, col) * channels - first
                            low, high = max(at, 0), min(at + channels, half)
                            if low < high:
                                ref[low:high, :] = n.total[row, low - at : high - at, col * channels : (col + 1) * channels]


def redo_kernel(rows, cols, bands, micros, count, n, step):
    channels = n.acts.shape[-1]
    segment = lax.axis_index("segment")
    side = lax.axis_index("sub")
    mean, rstd = statistics(n.packed, step, micros, count)
    mix = n.packed[2 * micros + 16 * micros :, :]
    total = n.packed[pl.ds(pl.multiple_of(2 * micros + 16 * step, 8), 16), :]
    mean_grad, mean_cross = gradient_means(total, mix, count)
    band = Band(n, step, rows, cols, bands)

    @pl.when(segment == 1)
    def _():
        for r in range(rows):
            at = slice(r * cols, (r + 1) * cols)
            xhat = (n.acts[0, at, :].astype(F32) - mean) * rstd
            change = rstd * (n.norm[0, at, :].astype(F32) - mean_grad - xhat * mean_cross)
            n.result[0, (r + 1) * cols : (r + 2) * cols, :] = (band.row(r)[0].astype(F32) + change).astype(BF16)

    @pl.when(segment == 0)
    def _():
        @pl.when(step == 0)
        def _():
            arrange_weights(n.kernel, n.weights)

        for r in range(rows + 4):
            spread(r, cols, *band.row(r - 2), n.shifted)
        hidden_gradient(rows + 2, cols, n.shifted, n.weights, n.hidden_grad)
        wide_mix = side_by_side(mix)
        edges = []
        for r in range(rows + 2):
            at = slice(r * cols, (r + 1) * cols)
            if r == 0:
                acts = n.above[0]
            elif r == rows + 1:
                acts = n.below[0]
            else:
                row = slice((r - 1) * cols, r * cols)
                acts = jnp.where(step < micros // 2, n.passed_early[0, row, :], n.passed_late[0, row, :])
            xhat, scale, _, slope = pixel_values(acts, band.latent(r - 1), wide_mix, mean, rstd)
            change = rstd * (n.hidden_grad[at, :] * slope * scale - mean_grad - xhat * mean_cross)
            value = n.shifted[(r + 1) * cols : (r + 2) * cols, channels : 2 * channels].astype(F32) + change
            if r == 0 or r == rows + 1:
                row = band.row_start + (r - 1)
                value = jnp.where((row >= 0) & (row < band.total_rows), value, 0.0)
            n.result[0, at, :] = value.astype(BF16)
            edges.append(jnp.where(side == 0, value[cols - 1 : cols], value[0:1]))
        edges.append(jnp.zeros((16 - rows - 2, channels), F32))
        n.edge[0] = jnp.concatenate(edges).astype(BF16)


def last_kernel(rows, cols, micros, count, n, step):
    lower = lax.axis_index("segment") == 0

    @pl.when(step == 0)
    def _():
        latents, channels = n.mod_grad.shape[1], n.total_lower.shape[-1]
        total = jnp.zeros((16, channels), F32)
        for m in range(micros):
            at = slice(16 * m, 16 * (m + 1))
            total = total + jnp.where(lower, n.total_lower[at, :], n.total_upper[at, :])
        total = jnp.concatenate([total[:8], total[8:]], axis=1)
        n.mod_grad[0] = total[:latents]
        n.bias_grad[...] = total[latents : latents + 1]

    @pl.when(lower)
    def _():
        mean, rstd = statistics(n.sums, step, micros, count)
        total = n.total_lower[pl.ds(pl.multiple_of(16 * step, 8), 16), :]
        mean_grad, mean_cross = gradient_means(total, n.mix[...], count)
        for r in range(rows):
            at = slice(r * cols, (r + 1) * cols)
            xhat = (n.acts[0, at, :].astype(F32) - mean) * rstd
            change = rstd * (n.norm[0, at, :].astype(F32) - mean_grad - xhat * mean_cross)
            n.grads[0, at, :] = (n.result[0, (r + 1) * cols : (r + 2) * cols, :].astype(F32) + change).astype(BF16)

    @pl.when(jnp.logical_not(lower))
    def _():
        n.grads[0] = n.result[0, cols : (rows + 1) * cols, :]


def by_micro(value):
    if isinstance(value, tuple):
        value, first, size = value
        return pl.BlockSpec((1,) + tuple(value.shape[1:]), lambda m: (jnp.clip(m - first, 0, size - 1), 0, 0))
    rest = (0,) * (len(value.shape) - 1)
    return pl.BlockSpec((1,) + tuple(value.shape[1:]), lambda m: (m,) + rest)


def whole(value):
    return pl.BlockSpec(tuple(value.shape), lambda m: (0,) * len(value.shape))


def call(kernel, name, micros, scalars, fixed, cut, outs, fixed_outs, scratch, work=4, room=62):
    names = [*scalars, *fixed, *cut, *outs, *fixed_outs, *scratch]
    cut_shape = [jax.ShapeDtypeStruct(s, d) for s, d in outs.values()]
    fixed_shape = [jax.ShapeDtypeStruct(s, d) for s, d in fixed_outs.values()]

    def body(*refs):
        kernel(types.SimpleNamespace(**dict(zip(names, refs))), pl.program_id(0))

    return pl.pallas_call(
        body,
        grid=(micros,),
        in_specs=[pl.BlockSpec(memory_space=pltpu.SMEM) for _ in scalars]
        + [whole(v) for v in fixed.values()]
        + [by_micro(v) for v in cut.values()],
        out_specs=[by_micro(s) for s in cut_shape] + [whole(s) for s in fixed_shape],
        out_shape=cut_shape + fixed_shape,
        scratch_shapes=[pltpu.VMEM(s, d) for s, d in scratch.values()],
        compiler_params=pltpu.CompilerParams(vmem_limit_bytes=room * 1024 * 1024),
        cost_estimate=pl.CostEstimate(flops=work, bytes_accessed=work // 4, transcendentals=0),
        name=name,
    )(*scalars.values(), *fixed.values(), *[v[0] if isinstance(v, tuple) else v for v in cut.values()])


def pair_body(
    activations, latent, recon, target, boxes, kernel, mod_weight, scale_bias, shift_bias, out_weight
):
    micros, rows, cols, channels = activations.shape[1:]
    latents = latent.shape[1]
    pixels = rows * cols
    bands = lax.axis_size("rows")
    count = float(pixels * bands * 2 * (channels // GROUPS))
    segment = lax.axis_index("segment")
    side = lax.axis_index("sub")
    acts = activations[0].reshape(micros, pixels, channels)

    early = micros // 2
    passed = [swap(acts[:early], "segment"), swap(acts[early:], "segment")]
    above = swap_and_shift(acts[:, pixels - cols :], 1)
    below = swap_and_shift(acts[:, :cols], bands - 1)
    kernel_passed = swap(kernel[0], "segment")
    recon_beside, target_beside = swap(recon, "sub"), swap(target, "sub")

    (sums,) = call(sums_kernel, "input_sums", micros, {}, {}, {"acts": acts}, {}, {"sums": ((2 * micros, channels), F32)}, {}, room=16)
    sums = sums + swap(sums, "sub")

    def border(first, r):
        def difference(one, two):
            part = slice(first, first + 2)
            return (one[:, :, part].astype(F32) - two[:, :, part].astype(F32)).transpose(0, 2, 1, 3)

        extra = latent[:, :, r].astype(F32).reshape(micros, 2, latents // 2, cols)
        two = jnp.concatenate([difference(recon, target), difference(recon_beside, target_beside), extra], axis=2)
        return jnp.concatenate([sums, two.reshape(micros * 16, cols)])

    from_up = shift(border(rows - 2, rows - 1), "rows", 1)
    from_down = shift(border(0, 0), "rows", bands - 1)
    across = shift(sums, "rows", 2)

    from_up, above, below, kernel_passed = lax.optimization_barrier((from_up, above, below, kernel_passed))
    image = {
        "latent": latent,
        "recon": recon,
        "target": target,
        "recon_beside": recon_beside,
        "target_beside": target_beside,
    }
    borders = {"from_up": from_up, "from_down": from_down, "out_weight": out_weight}
    wide = (rows + 2) * cols
    triple = 3 * channels
    shifted = {"shifted": ((wide, triple), BF16)}
    work = {
        **shifted,
        "weights": ((3, channels, triple), BF16),
        "hidden_grad": ((pixels, channels), F32),
        "latent_keep": ((8, pixels), BF16),
        "pairs": ((pixels, 2 * channels), BF16),
    }
    produced = {"norm": ((micros, pixels, channels), BF16), "reduced": ((micros, 16, channels), F32)}
    size = (rows, cols, bands, micros, count)
    norm_upper, reduced = call(
        functools.partial(upper_kernel, *size),
        "upper_block",
        micros,
        {"boxes": boxes},
        {
            "sums": sums,
            "across": across,
            "mod_weight": mod_weight,
            "scale_bias": scale_bias,
            "shift_bias": shift_bias,
            "kernel": kernel[0],
            **borders,
        },
        {"acts": acts, **image},
        produced,
        {},
        {**work, "sums_keep": ((2 * micros, channels), F32)},
    )
    reduced, passed[0] = lax.optimization_barrier((reduced, passed[0]))
    total_upper = pixel_total(reduced.reshape(micros * 16, channels))
    sums = (sums + across) + (from_up[: 2 * micros] + from_down[: 2 * micros])
    mix = jnp.concatenate([mod_weight[0], jnp.concatenate([scale_bias, shift_bias], axis=1)]).astype(F32)
    mix = jnp.pad(mix, ((0, 7 - latents), (0, 0)))
    mix = jnp.concatenate([mix[:, :channels], mix[:, channels:]])
    packed = jnp.concatenate([sums, total_upper, mix])
    packed, passed[1] = lax.optimization_barrier((packed, passed[1]))
    packed = jnp.where(segment == 0, swap(packed, "segment"), packed)
    result, edge = call(
        functools.partial(redo_kernel, *size),
        "redo_upper",
        micros,
        {"boxes": boxes},
        {"packed": packed, "kernel": kernel_passed, **borders},
        {
            "acts": acts,
            "norm": norm_upper,
            "passed_early": (passed[0], 0, early),
            "passed_late": (passed[1], early, micros - early),
            "above": above,
            "below": below,
            **image,
        },
        {"result": ((micros, wide, channels), BF16), "edge": ((micros, 16, channels), BF16)},
        {},
        {
            "shifted": (((rows + 4) * cols, triple), BF16),
            "weights": ((3, channels, triple), BF16),
            "hidden_grad": ((wide, channels), F32),
        },
    )
    near = swap(edge, "sub")
    half = kernel.shape[1] // 2
    keep, give = call(
        functools.partial(gradient_kernel, *size),
        "kernel_gradient",
        micros,
        {"boxes": boxes},
        {"sums": sums, "mix": mix, **borders},
        {"result": result, "near": near, "acts": acts, **image},
        {},
        {"keep": ((half, channels), F32), "give": ((half, channels), F32)},
        {**shifted, "hidden": ((pixels, channels), BF16), "total": ((3, channels, triple), F32)},
    )
    keep = (keep + swap(give, "sub")).astype(BF16)
    others = [shift(keep, "rows", steps) for steps in (1, 2, 3)]
    norm, reduced = call(
        functools.partial(lower_kernel, *size),
        "lower_block",
        micros,
        {"boxes": boxes},
        {"sums": sums, "mix": mix, "kernel": kernel[0], **borders},
        {"result": result, "near": near, "acts": acts, **image},
        produced,
        {},
        work,
        work=1 << 27,
    )
    total_lower = pixel_total(reduced.reshape(micros * 16, channels))
    grads, mod_grad, bias_grad = call(
        functools.partial(last_kernel, rows, cols, micros, count),
        "input_gradient",
        micros,
        {},
        {"sums": sums, "mix": mix, "total_lower": total_lower, "total_upper": total_upper},
        {"acts": acts, "norm": norm, "result": result},
        {"grads": ((micros, pixels, channels), BF16)},
        {"mod_grad": ((1, latents, 2 * channels), F32), "bias_grad": ((1, 2 * channels), F32)},
        {},
        work=1 << 25,
    )
    grads, *others = lax.optimization_barrier((grads, *others))
    one, two, three = [value.astype(F32) for value in others]
    keep = (keep.astype(F32) + two) + (one + three)
    give = swap(keep, "sub")
    kernel_grad = jnp.where(side == 0, jnp.concatenate([keep, give]), jnp.concatenate([give, keep]))
    return (grads.reshape(activations.shape), kernel_grad[None], mod_grad, bias_grad)


def solution(mesh):
    pair = mesh.shape["segment"] == 2 and mesh.shape["rows"] == 4 and mesh.shape["sub"] == 2
    body = pair_body if pair else general_body
    placed = (
        P("segment", "groups", "rows", "sub", None),
        P("groups", None, "rows", "sub"),
        P("groups", None, "rows", "sub"),
        P("groups", None, "rows", "sub"),
        P("groups", None, None),
        P("segment", None, None),
        P("segment", None, None),
        P("segment", None),
        P("segment", None),
        P(),
    )
    return jax.shard_map(
        body,
        mesh=mesh,
        in_specs=placed,
        out_specs=(
            P("segment", "groups", "rows", "sub", None),
            P("segment", "groups", None),
            P("segment", "groups", None),
            P("segment", "groups"),
        ),
        check_vma=False,
    )
```

```python
import functools
import types

import jax
import jax.numpy as jnp
from jax import lax
from jax.experimental import pallas as pl
from jax.experimental.pallas import tpu as pltpu
from jax.sharding import PartitionSpec as P

GROUPS = 32
TILE = 32


EPS = 1e-06


def extended(block, sides, width):
    for axis, dim in sides:
        count = lax.axis_size(axis)
        forward = [(i, i + 1) for i in range(count - 1)]
        backward = [(target, source) for source, target in forward]
        low = lax.ppermute(
            lax.slice_in_dim(block, block.shape[dim] - width, None, axis=dim), axis, forward
        )
        high = lax.ppermute(lax.slice_in_dim(block, 0, width, axis=dim), axis, backward)
        block = jnp.concatenate([low, block, high], axis=dim)
    return block


def from_behind(value, axis, steps):
    count = lax.axis_size(axis)
    initial, last = (max(0, -steps), min(count, count - steps))
    return lax.ppermute(value, axis, [(source, source + steps) for source in range(initial, last)])


def crop_weights(boxes, row_start, col_start, row_count, col_count, total_rows, total_cols):
    row_tile = (row_start + jnp.arange(row_count, dtype=jnp.int32)) // TILE
    col_tile = (col_start + jnp.arange(col_count, dtype=jnp.int32)) // TILE
    first_row = boxes[:, :, 0:1]
    first_col = boxes[:, :, 1:2]
    box_height = boxes[:, :, 2:3]
    box_width = boxes[:, :, 3:4]
    in_rows = ((row_tile >= first_row) & (row_tile < first_row + box_height)).astype(jnp.float32)
    in_cols = ((col_tile >= first_col) & (col_tile < first_col + box_width)).astype(jnp.float32)
    tiles = total_rows // TILE * (total_cols // TILE)
    share = tiles / (boxes.shape[1] * (box_height * box_width).astype(jnp.float32))
    return jnp.einsum("mkr,mkc->mrc", in_rows * share, in_cols)


def top_gradient(recon, target, cropped, out_weight):
    diff = 2.0 * (recon.astype(jnp.float32) - target.astype(jnp.float32)) * cropped[:, None]
    return jnp.einsum("mkhw,kc->mhwc", diff, out_weight.astype(jnp.float32)).astype(jnp.bfloat16)


def loss_gradient(
    boxes,
    recon,
    target,
    out_weight,
    row_start,
    col_start,
    row_count,
    col_count,
    total_rows,
    total_cols,
):
    cropped = crop_weights(
        boxes, row_start, col_start, row_count, col_count, total_rows, total_cols
    )
    return top_gradient(recon, target, cropped, out_weight)


def grouped_layout(value_array):
    return value_array.reshape(value_array.shape[:-1] + (GROUPS, value_array.shape[-1] // GROUPS))


def group_sums(value_array):
    shaped = grouped_layout(value_array)
    return (jnp.sum(shaped, axis=(-4, -3, -1)), jnp.sum(shaped * shaped, axis=(-4, -3, -1)))


def expand(stat):
    return stat[..., None, None, :, None]


def normalized_values(value_array, mean_val, rstd_val):
    shaped = grouped_layout(value_array)
    return ((shaped - expand(mean_val)) * expand(rstd_val)).reshape(value_array.shape)


def modulation(latent_batch, mix_weight, scale_row, shift_row):
    channel_count = scale_row.shape[-1]
    coefficients = jnp.einsum(
        "bzhw,zc->bhwc", latent_batch.astype(jnp.float32), mix_weight.astype(jnp.float32)
    )
    return (
        coefficients[..., :channel_count] + scale_row.astype(jnp.float32),
        coefficients[..., channel_count:] + shift_row.astype(jnp.float32),
    )


def transposed(weights):
    channel_count = weights.shape[-1]
    return (
        weights.reshape(9, channel_count, channel_count)
        .transpose(0, 2, 1)
        .reshape(9 * channel_count, channel_count)
    )


def taps(padded, row_count, col_count, flipped):
    pieces = []
    for tap_row in range(3):
        for tap_col in range(3):
            if flipped:
                row_offset, col_offset = (2 - tap_row, 2 - tap_col)
            else:
                row_offset, col_offset = (tap_row, tap_col)
            pieces.append(
                padded[:, row_offset : row_offset + row_count, col_offset : col_offset + col_count]
            )
    return jnp.concatenate(pieces, axis=-1).reshape(-1, 9 * padded.shape[-1])


def pick(value_array, index):
    return lax.dynamic_slice_in_dim(value_array, index, 1, 0)


def section_backward(
    value_array, latent_batch, incoming, spatial_scale, spatial_shift, weights_t, count
):
    batch, row_count, col_count, channel_count = value_array.shape
    sum_one, sum_two = group_sums(value_array)
    sum_one, sum_two = lax.psum((sum_one, sum_two), ("rows", "sub"))
    group_mean = sum_one / count
    inverse_deviation = lax.rsqrt(sum_two / count - group_mean * group_mean + EPS)
    centered_scaled = normalized_values(value_array, group_mean, inverse_deviation)
    pre_activation = centered_scaled * spatial_scale + spatial_shift
    hidden = jax.nn.silu(pre_activation).astype(jnp.bfloat16)
    padded_h = extended(hidden, (("rows", 1), ("sub", 2)), 1)
    padded_g = extended(incoming, (("rows", 1), ("sub", 2)), 1)
    patches = taps(padded_h, row_count, col_count, False)
    kernel_term = lax.dot_general(
        patches,
        incoming.reshape(-1, channel_count),
        (((0,), (0,)), ((), ())),
        preferred_element_type=jnp.float32,
    )
    hidden_grad = jnp.dot(
        taps(padded_g, row_count, col_count, True), weights_t, preferred_element_type=jnp.float32
    ).reshape(value_array.shape)
    sig = jax.nn.sigmoid(pre_activation)
    pre_activation_gradient = hidden_grad * (sig * (1.0 + pre_activation * (1.0 - sig)))
    paired_parts = jnp.concatenate(
        [pre_activation_gradient * centered_scaled, pre_activation_gradient], axis=-1
    )
    mod_term = jnp.einsum("bzhw,bhwc->zc", latent_batch.astype(jnp.float32), paired_parts)
    bias_term = jnp.sum(paired_parts, axis=(0, 1, 2))
    shaped_grad = grouped_layout(pre_activation_gradient * spatial_scale)
    reshaped_normalized = grouped_layout(centered_scaled)
    part_one = jnp.sum(shaped_grad, axis=(1, 2, 4))
    part_two = jnp.sum(shaped_grad * reshaped_normalized, axis=(1, 2, 4))
    part_one, part_two = lax.psum((part_one, part_two), ("rows", "sub"))
    mean_grad = part_one / count
    mean_cross = part_two / count
    adjust = expand(inverse_deviation) * (
        shaped_grad - expand(mean_grad) - reshaped_normalized * expand(mean_cross)
    )
    result = (incoming.astype(jnp.float32) + adjust.reshape(value_array.shape)).astype(jnp.bfloat16)
    return (result, kernel_term, mod_term, bias_term)


def general_body(
    activations,
    latent,
    recon,
    target,
    boxes,
    kernel,
    mod_weight,
    scale_bias,
    shift_bias,
    out_weight,
):
    segments = lax.axis_size("segment")
    segment_index = lax.axis_index("segment")
    micro, row_count, col_count, channel_count = activations.shape[1:]
    total_rows = row_count * lax.axis_size("rows")
    total_cols = col_count * lax.axis_size("sub")
    count = total_rows * total_cols * (channel_count // GROUPS)
    row_start = lax.axis_index("rows") * row_count
    col_start = lax.axis_index("sub") * col_count
    acts = activations[0]
    weights_t = transposed(kernel[0])
    mix_weight = mod_weight[0]
    scale_row = scale_bias[0]
    shift_row = shift_bias[0]
    top = loss_gradient(
        boxes,
        recon,
        target,
        out_weight,
        row_start,
        col_start,
        row_count,
        col_count,
        total_rows,
        total_cols,
    )

    def tick(step, carry):
        passing, grads_out, kernel_grad, mod_grad, bias_grad = carry
        offset = step - (segments - 1 - segment_index)
        valid = (offset >= 0) & (offset < micro)
        index = jnp.clip(offset, 0, micro - 1)
        received = from_behind(passing, "segment", -1)
        incoming = jnp.where(segment_index == segments - 1, pick(top, index), received)
        value_array = pick(acts, index).astype(jnp.float32)
        latent_m = pick(latent, index)
        spatial_scale, spatial_shift = modulation(latent_m, mix_weight, scale_row, shift_row)
        result, kernel_term, mod_term, bias_term = section_backward(
            value_array, latent_m, incoming, spatial_scale, spatial_shift, weights_t, count
        )
        weight = valid.astype(jnp.float32)
        current = pick(grads_out, index)
        grads_out = lax.dynamic_update_slice_in_dim(
            grads_out, jnp.where(valid, result, current), index, 0
        )
        return (
            result,
            grads_out,
            kernel_grad + weight * kernel_term,
            mod_grad + weight * mod_term,
            bias_grad + weight * bias_term,
        )

    initial = (
        jnp.zeros((1, row_count, col_count, channel_count), jnp.bfloat16),
        jnp.zeros_like(acts),
        jnp.zeros((9 * channel_count, channel_count), jnp.float32),
        jnp.zeros((mix_weight.shape[0], 2 * channel_count), jnp.float32),
        jnp.zeros((2 * channel_count,), jnp.float32),
    )
    final = lax.fori_loop(0, micro + segments - 1, tick, initial)
    grads_out = final[1][None]
    kernel_grad = final[2][None]
    mod_grad = final[3][None]
    bias_grad = final[4][None]
    kernel_grad, mod_grad, bias_grad = lax.psum((kernel_grad, mod_grad, bias_grad), ("rows", "sub"))
    return (grads_out, kernel_grad, mod_grad, bias_grad)


EXACT = lax.Precision.HIGHEST
TN = (((0,), (0,)), ((), ()))
NT = (((1,), (1,)), ((), ()))
F32 = jnp.float32
BF16 = jnp.bfloat16


def swap(value, axis):
    return lax.ppermute(value, axis, [(0, 1), (1, 0)])


def shift(value, axis, steps):
    count = lax.axis_size(axis)
    return lax.ppermute(value, axis, [(i, (i + steps) % count) for i in range(count)])


def swap_and_shift(value, steps):
    count = lax.axis_size("rows")
    pairs = [(2 * i + s, 2 * ((i + steps) % count) + 1 - s) for i in range(count) for s in range(2)]
    return lax.ppermute(value, ("rows", "segment"), pairs)


def pixel_total(value):
    value = value + swap(value, "sub")
    one, two, three = [shift(value, "rows", steps) for steps in (1, 2, 3)]
    return (value + two) + (one + three)


def same_group(channels):
    per = channels // GROUPS
    left = lax.broadcasted_iota(jnp.int32, (channels, channels), 0) // per
    right = lax.broadcasted_iota(jnp.int32, (channels, channels), 1) // per
    return (left == right).astype(F32)


def statistics(sums_ref, micro, micros, count):
    member = same_group(sums_ref.shape[-1])
    both = jnp.concatenate([sums_ref[pl.ds(micro, 1), :], sums_ref[pl.ds(micros + micro, 1), :]], axis=0)
    both = jnp.dot(both, member, precision=EXACT, preferred_element_type=F32) / count
    mean = both[0:1]
    return mean, lax.rsqrt(both[1:2] - mean * mean + EPS)


def gradient_means(total, mix, count):
    mean_grad = jnp.sum(mix[:8] * total[8:], axis=0, keepdims=True)
    mean_cross = jnp.sum(mix[:8] * total[:8], axis=0, keepdims=True)
    both = jnp.concatenate([mean_grad, mean_cross], axis=0)
    both = jnp.dot(both, same_group(total.shape[-1]), precision=EXACT, preferred_element_type=F32) / count
    return both[0:1], both[1:2]


def side_by_side(mix):
    return jnp.concatenate([mix[:8], mix[8:]], axis=1).astype(BF16)


def sums_kernel(n, micro):
    micros = n.sums.shape[0] // 2
    value = n.acts[0].astype(F32)
    n.sums[pl.ds(micro, 1), :] = jnp.sum(value, axis=0, keepdims=True)
    n.sums[pl.ds(micros + micro, 1), :] = jnp.sum(value * value, axis=0, keepdims=True)


class Band:
    def __init__(self, n, micro, rows, cols, bands):
        self.n, self.rows, self.cols = n, rows, cols
        self.head = n.from_up.shape[0] - 16 * (n.from_up.shape[0] // 16)
        self.micro = micro
        self.side = lax.axis_index("sub")
        self.row_start = lax.axis_index("rows") * rows
        self.total_rows = rows * bands
        lane = lax.broadcasted_iota(jnp.int32, (1, cols), 1)
        crops = n.boxes.shape[1]
        tiles = self.total_rows // TILE * (2 * cols // TILE)
        self.boxes = []
        for k in range(crops):
            row, col, height, width = [n.boxes[micro, k, i] for i in range(4)]
            share = tiles / jnp.full((1, cols), crops * height * width, jnp.int32).astype(F32)
            inside = []
            for side in (self.side, 1 - self.side):
                at = lane + side * cols
                inside.append(jnp.where((at >= col * TILE) & (at < (col + width) * TILE), share, 0.0))
            self.boxes.append((row * TILE, (row + height) * TILE, inside[0], inside[1]))
        weight = n.out_weight[...].astype(F32)
        blank = jnp.zeros((8 - weight.shape[0], weight.shape[1]), F32)
        self.own = jnp.concatenate([jnp.concatenate([weight, blank])] * 3).astype(BF16)
        self.other = jnp.concatenate([jnp.concatenate([blank[:3], weight, blank[3:]])] * 3).astype(BF16)

    def border(self, ref, which):
        return ref[pl.ds(pl.multiple_of(self.head + 16 * self.micro + 8 * which, 8), 8), :]

    def planes(self, r):
        if r < 0:
            return self.border(self.n.from_up, r + 2)
        if r >= self.rows:
            return self.border(self.n.from_down, r - self.rows)
        own = self.n.recon[0, :, r, :].astype(F32) - self.n.target[0, :, r, :].astype(F32)
        beside = self.n.recon_beside[0, :, r, :].astype(F32) - self.n.target_beside[0, :, r, :].astype(F32)
        return jnp.concatenate([own, beside, jnp.zeros((2, self.cols), F32)])

    def latent(self, r):
        if r < 0 or r >= self.rows:
            ref = self.n.from_up if r < 0 else self.n.from_down
            value = jnp.concatenate([self.border(ref, 0)[6:8], self.border(ref, 1)[6:8]])
        else:
            value = self.n.latent[0, :, r, :].astype(F32)
        count = value.shape[0]
        return jnp.concatenate([value, jnp.ones((1, self.cols), F32), jnp.zeros((7 - count, self.cols), F32)]).astype(BF16)

    def row(self, r):
        diff = self.planes(r)
        at = self.row_start + r
        own = jnp.zeros((1, self.cols), F32)
        other = jnp.zeros((1, self.cols), F32)
        for first, end, own_share, other_share in self.boxes:
            here = (at >= first) & (at < end)
            own = own + jnp.where(here, own_share, 0.0)
            other = other + jnp.where(here, other_share, 0.0)
        plane = lax.broadcasted_iota(jnp.int32, (8, self.cols), 0)
        diff = 2.0 * diff * jnp.where(plane < 3, own, other)
        high = diff.astype(BF16).astype(F32)
        middle = (diff - high).astype(BF16).astype(F32)
        parts = jnp.concatenate([high, middle, diff - high - middle]).astype(BF16)
        value = lax.dot_general(parts, self.own, TN, preferred_element_type=F32).astype(BF16)
        beside = lax.dot_general(parts, self.other, TN, preferred_element_type=F32).astype(BF16).astype(F32)
        return value, jnp.where(self.side == 0, beside[0:1], beside[self.cols - 1 : self.cols])


def spread(index, cols, value, near, shifted):
    channels = value.shape[-1]
    side = lax.axis_index("sub")
    at = slice(index * cols, (index + 1) * cols)
    place = lax.broadcasted_iota(jnp.int32, (cols, channels), 0)
    wide = value.astype(F32)
    before = jnp.where(side == 1, near, 0.0)
    behind = jnp.where(side == 0, near, 0.0)
    shifted[at, 0:channels] = jnp.where(place == 0, before, pltpu.roll(wide, 1, 0)).astype(BF16)
    shifted[at, channels : 2 * channels] = value
    shifted[at, 2 * channels :] = jnp.where(place == cols - 1, behind, pltpu.roll(wide, cols - 1, 0)).astype(BF16)


def tap_of(row, col):
    return 3 * (2 - row) + (2 - col)


def arrange_weights(kernel_ref, weights):
    channels = kernel_ref.shape[-1]
    for row in range(3):
        for col in range(3):
            tap = tap_of(row, col)
            weights[row, :, col * channels : (col + 1) * channels] = kernel_ref[tap * channels : (tap + 1) * channels, :]


def hidden_gradient(rows, cols, shifted, weights, hidden_grad):
    pixels = rows * cols
    total = lax.dot_general(shifted[0:pixels, :], weights[0], NT, preferred_element_type=F32)
    total = total + lax.dot_general(shifted[cols : cols + pixels, :], weights[1], NT, preferred_element_type=F32)
    hidden_grad[0:pixels, :] = total + lax.dot_general(
        shifted[2 * cols : 2 * cols + pixels, :], weights[2], NT, preferred_element_type=F32
    )


def pixel_values(acts, latent, mix, mean, rstd):
    channels = mean.shape[-1]
    xhat = (acts.astype(F32) - mean) * rstd
    mixed = lax.dot_general(latent, mix, TN, preferred_element_type=F32)
    scale = mixed[:, :channels]
    pre = xhat * scale + mixed[:, channels:]
    sig = 0.5 * jnp.tanh(0.5 * pre) + 0.5
    hidden = pre * sig
    return xhat, scale, hidden, sig + hidden * (1.0 - sig)


def reduce_block(n, band, mean, rstd, mix, base=False):
    rows, cols = band.rows, band.cols
    channels = n.acts.shape[-1]
    hidden_gradient(rows, cols, n.shifted, n.weights, n.hidden_grad)
    for r in range(rows):
        at = slice(r * cols, (r + 1) * cols)
        latent = band.latent(r)
        n.latent_keep[:, at] = latent
        xhat, scale, hidden, slope = pixel_values(n.acts[0, at, :], latent, mix, mean, rstd)
        pre_grad = n.hidden_grad[at, :] * slope
        norm = pre_grad * scale
        if base:
            norm = n.shifted[(r + 1) * cols : (r + 2) * cols, channels : 2 * channels].astype(F32) + rstd * norm
            n.base[0, (r + 1) * cols : (r + 2) * cols, :] = norm.astype(BF16)
        else:
            n.norm[0, at, :] = norm.astype(BF16)
            n.hidden[at, :] = hidden.astype(BF16)
        n.pairs[at, 0:channels] = (pre_grad * xhat).astype(BF16)
        n.pairs[at, channels:] = pre_grad.astype(BF16)
    reduced = jnp.dot(n.latent_keep[...], n.pairs[...], preferred_element_type=F32)
    n.reduced[0, 0:8, :] = reduced[:, :channels]
    n.reduced[0, 8:16, :] = reduced[:, channels:]


def upper_kernel(rows, cols, bands, micros, count, n, step):
    active = lax.axis_index("segment") == 1

    @pl.when(active)
    def _():
        @pl.when(step == 0)
        def _():
            arrange_weights(n.kernel, n.weights)
            head = 2 * micros
            n.sums_keep[...] = (n.sums[...] + n.across[...]) + (n.from_up[0:head, :] + n.from_down[0:head, :])

        mean, rstd = statistics(n.sums_keep, step, micros, count)
        channels = mean.shape[-1]
        mix = [n.mod_weight[0].astype(F32), jnp.concatenate([n.scale_bias[...], n.shift_bias[...]], axis=1).astype(F32)]
        mix.append(jnp.zeros((7 - mix[0].shape[0], 2 * channels), F32))
        band = Band(n, step, rows, cols, bands)
        for r in range(rows + 2):
            spread(r, cols, *band.row(r - 1), n.shifted)
        reduce_block(n, band, mean, rstd, jnp.concatenate(mix).astype(BF16), base=True)

    @pl.when(jnp.logical_not(active))
    def _():
        @pl.when(step == 0)
        def _():
            arrange_weights(n.kernel_passed, n.weights)

        n.reduced[...] = jnp.zeros_like(n.reduced)
        band = Band(n, step, rows, cols, bands)
        for r in range(rows + 4):
            spread(r, cols, *band.row(r - 2), n.shifted)
        hidden_gradient(rows + 2, cols, n.shifted, n.weights, n.hidden_grad)
        n.base[0] = n.hidden_grad[...].astype(BF16)


def own_kernel(rows, cols, bands, micros, count, n, step):
    pixels = rows * cols
    side = lax.axis_index("sub")
    segment = lax.axis_index("segment")

    @pl.when(step == 0)
    def _():
        n.total[...] = jnp.zeros_like(n.total)

        @pl.when(segment == 0)
        def _():
            arrange_weights(n.kernel, n.weights)

    mean, rstd = statistics(n.sums, step, micros, count)
    band = Band(n, step, rows, cols, bands)
    mix = side_by_side(n.mix[...])

    @pl.when(segment == 1)
    def _():
        n.reduced[...] = jnp.zeros_like(n.reduced)
        for r in range(rows + 2):
            spread(r, cols, *band.row(r - 1), n.shifted)
        for r in range(rows):
            at = slice(r * cols, (r + 1) * cols)
            n.hidden[at, :] = pixel_values(n.acts[0, at, :], band.latent(r), mix, mean, rstd)[2].astype(BF16)

    @pl.when(segment == 0)
    def _():
        near = n.near[0].astype(F32)
        for r in range(rows + 2):
            spread(r, cols, n.result[0, r * cols : (r + 1) * cols, :], near[r : r + 1], n.shifted)
        reduce_block(n, band, mean, rstd, mix)

    for row in range(3):
        n.total[row] += lax.dot_general(
            n.hidden[...], n.shifted[row * cols : row * cols + pixels, :], TN, preferred_element_type=F32
        )

    @pl.when(step == micros - 1)
    def _():
        half, channels = n.keep.shape
        for which in range(2):
            for ref, owner in ((n.keep, which), (n.give, 1 - which)):

                @pl.when(side == owner)
                def _(ref=ref, first=which * half):
                    for row in range(3):
                        for col in range(3):
                            at = tap_of(row, col) * channels - first
                            low, high = max(at, 0), min(at + channels, half)
                            if low < high:
                                ref[low:high, :] = n.total[row, low - at : high - at, col * channels : (col + 1) * channels]


def finish_kernel(rows, cols, bands, micros, count, n, step):
    channels = n.acts.shape[-1]
    segment = lax.axis_index("segment")
    side = lax.axis_index("sub")

    @pl.when(segment == 1)
    def _():
        mean, rstd = statistics(n.sums, step, micros, count)
        total = n.total[pl.ds(pl.multiple_of(16 * step, 8), 16), :]
        mean_grad, mean_cross = gradient_means(total, n.mix[...], count)
        for r in range(rows):
            at = slice((r + 1) * cols, (r + 2) * cols)
            xhat = (n.acts[0, r * cols : (r + 1) * cols, :].astype(F32) - mean) * rstd
            n.result[0, at, :] = (n.base[0, at, :].astype(F32) - rstd * (mean_grad + xhat * mean_cross)).astype(BF16)

    @pl.when(segment == 0)
    def _():
        mean, rstd = statistics(n.packed, step, micros, count)
        total = n.packed[pl.ds(pl.multiple_of(2 * micros + 16 * step, 8), 16), :]
        mix = n.packed[2 * micros + 16 * micros :, :]
        mean_grad, mean_cross = gradient_means(total, mix, count)
        wide_mix = side_by_side(mix)
        band = Band(n, step, rows, cols, bands)
        edges = []
        for r in range(rows + 2):
            at = slice(r * cols, (r + 1) * cols)
            if r == 0:
                acts = n.above[0]
            elif r == rows + 1:
                acts = n.below[0]
            else:
                row = slice((r - 1) * cols, r * cols)
                acts = jnp.where(step < 1, n.passed_early[0, row, :], n.passed_late[0, row, :])
            xhat, scale, _, slope = pixel_values(acts, band.latent(r - 1), wide_mix, mean, rstd)
            change = rstd * (n.base[0, at, :].astype(F32) * slope * scale - mean_grad - xhat * mean_cross)
            value = band.row(r - 1)[0].astype(F32) + change
            if r == 0 or r == rows + 1:
                row = band.row_start + (r - 1)
                value = jnp.where((row >= 0) & (row < band.total_rows), value, 0.0)
            n.result[0, at, :] = value.astype(BF16)
            edges.append(jnp.where(side == 0, value[cols - 1 : cols], value[0:1]))
        edges.append(jnp.zeros((16 - rows - 2, channels), F32))
        n.edge[0] = jnp.concatenate(edges).astype(BF16)


def last_kernel(rows, cols, micros, count, n, step):
    lower = lax.axis_index("segment") == 0

    @pl.when(step == 0)
    def _():
        latents, channels = n.mod_grad.shape[1], n.total_lower.shape[-1]
        total = jnp.zeros((16, channels), F32)
        for m in range(micros):
            at = slice(16 * m, 16 * (m + 1))
            total = total + jnp.where(lower, n.total_lower[at, :], n.total_upper[at, :])
        total = jnp.concatenate([total[:8], total[8:]], axis=1)
        n.mod_grad[0] = total[:latents]
        n.bias_grad[...] = total[latents : latents + 1]

    @pl.when(lower)
    def _():
        mean, rstd = statistics(n.sums, step, micros, count)
        total = n.total_lower[pl.ds(pl.multiple_of(16 * step, 8), 16), :]
        mean_grad, mean_cross = gradient_means(total, n.mix[...], count)
        for r in range(rows):
            at = slice(r * cols, (r + 1) * cols)
            xhat = (n.acts[0, at, :].astype(F32) - mean) * rstd
            change = rstd * (n.norm[0, at, :].astype(F32) - mean_grad - xhat * mean_cross)
            n.grads[0, at, :] = (n.result[0, (r + 1) * cols : (r + 2) * cols, :].astype(F32) + change).astype(BF16)

    @pl.when(jnp.logical_not(lower))
    def _():
        n.grads[0] = n.result[0, cols : (rows + 1) * cols, :]


def by_micro(value):
    if isinstance(value, tuple):
        value, first, size = value
        rest = (0,) * (len(value.shape) - 1)
        return pl.BlockSpec((1,) + tuple(value.shape[1:]), lambda m: (jnp.clip(m - first, 0, size - 1),) + rest)
    rest = (0,) * (len(value.shape) - 1)
    return pl.BlockSpec((1,) + tuple(value.shape[1:]), lambda m: (m,) + rest)


def whole(value):
    return pl.BlockSpec(tuple(value.shape), lambda m: (0,) * len(value.shape))


def call(kernel, name, micros, scalars, fixed, cut, outs, fixed_outs, scratch, work=4, room=16):
    names = [*scalars, *fixed, *cut, *outs, *fixed_outs, *scratch]
    cut_shape = [jax.ShapeDtypeStruct(s, d) for s, d in outs.values()]
    fixed_shape = [jax.ShapeDtypeStruct(s, d) for s, d in fixed_outs.values()]

    def body(*refs):
        kernel(types.SimpleNamespace(**dict(zip(names, refs))), pl.program_id(0))

    return pl.pallas_call(
        body,
        grid=(micros,),
        in_specs=[pl.BlockSpec(memory_space=pltpu.SMEM) for _ in scalars]
        + [whole(v) for v in fixed.values()]
        + [by_micro(v) for v in cut.values()],
        out_specs=[by_micro(s) for s in cut_shape] + [whole(s) for s in fixed_shape],
        out_shape=cut_shape + fixed_shape,
        scratch_shapes=[pltpu.VMEM(s, d) for s, d in scratch.values()],
        compiler_params=pltpu.CompilerParams(vmem_limit_bytes=room * 1024 * 1024),
        cost_estimate=pl.CostEstimate(flops=work, bytes_accessed=work // 4, transcendentals=0),
        name=name,
    )(*scalars.values(), *fixed.values(), *[v[0] if isinstance(v, tuple) else v for v in cut.values()])


def pair_body(
    activations, latent, recon, target, boxes, kernel, mod_weight, scale_bias, shift_bias, out_weight
):
    micros, rows, cols, channels = activations.shape[1:]
    latents = latent.shape[1]
    pixels = rows * cols
    bands = lax.axis_size("rows")
    count = float(pixels * bands * 2 * (channels // GROUPS))
    segment = lax.axis_index("segment")
    side = lax.axis_index("sub")
    acts = activations[0].reshape(micros, pixels, channels)

    early = 1
    passed = [swap(acts[:early], "segment"), swap(acts[early:], "segment")]
    above = swap_and_shift(acts[:, pixels - cols :], 1)
    below = swap_and_shift(acts[:, :cols], bands - 1)
    kernel_passed = swap(kernel[0], "segment")
    recon_beside, target_beside = swap(recon, "sub"), swap(target, "sub")

    (sums,) = call(sums_kernel, "input_sums", micros, {}, {}, {"acts": acts}, {}, {"sums": ((2 * micros, channels), F32)}, {})
    sums = sums + swap(sums, "sub")

    def border(first, r):
        def difference(one, two):
            part = slice(first, first + 2)
            return (one[:, :, part].astype(F32) - two[:, :, part].astype(F32)).transpose(0, 2, 1, 3)

        extra = latent[:, :, r].astype(F32).reshape(micros, 2, latents // 2, cols)
        two = jnp.concatenate([difference(recon, target), difference(recon_beside, target_beside), extra], axis=2)
        return jnp.concatenate([sums, two.reshape(micros * 16, cols)])

    from_up = shift(border(rows - 2, rows - 1), "rows", 1)
    from_down = shift(border(0, 0), "rows", bands - 1)
    across = shift(sums, "rows", 2)

    from_up, kernel_passed = lax.optimization_barrier((from_up, kernel_passed))
    image = {
        "latent": latent,
        "recon": recon,
        "target": target,
        "recon_beside": recon_beside,
        "target_beside": target_beside,
    }
    borders = {"from_up": from_up, "from_down": from_down, "out_weight": out_weight}
    wide = (rows + 2) * cols
    triple = 3 * channels
    shifted = {"shifted": ((wide, triple), BF16)}
    work = {
        **shifted,
        "weights": ((3, channels, triple), BF16),
        "hidden_grad": ((pixels, channels), F32),
        "latent_keep": ((8, pixels), BF16),
        "pairs": ((pixels, 2 * channels), BF16),
    }
    size = (rows, cols, bands, micros, count)
    sums_own = (sums + across) + (from_up[: 2 * micros] + from_down[: 2 * micros])
    mix = jnp.concatenate([mod_weight[0], jnp.concatenate([scale_bias, shift_bias], axis=1)]).astype(F32)
    mix = jnp.pad(mix, ((0, 7 - latents), (0, 0)))
    mix = jnp.concatenate([mix[:, :channels], mix[:, channels:]])
    base, reduced = call(
        functools.partial(upper_kernel, *size),
        "upper_block",
        micros,
        {"boxes": boxes},
        {
            "sums": sums,
            "across": across,
            "mod_weight": mod_weight,
            "scale_bias": scale_bias,
            "shift_bias": shift_bias,
            "kernel": kernel[0],
            "kernel_passed": kernel_passed,
            **borders,
        },
        {"acts": acts, **image},
        {"base": ((micros, wide, channels), BF16), "reduced": ((micros, 16, channels), F32)},
        {},
        {
            **work,
            "shifted": (((rows + 4) * cols, triple), BF16),
            "hidden_grad": ((wide, channels), F32),
            "sums_keep": ((2 * micros, channels), F32),
        },
    )
    sums = sums_own
    reduced, passed[0] = lax.optimization_barrier((reduced, passed[0]))
    total_upper = pixel_total(reduced.reshape(micros * 16, channels))
    packed = jnp.concatenate([sums, total_upper, mix])
    packed, passed[1], above, below = lax.optimization_barrier((packed, passed[1], above, below))
    packed = swap(packed, "segment")
    result, edge = call(
        functools.partial(finish_kernel, *size),
        "finish_upper",
        micros,
        {"boxes": boxes},
        {"sums": sums, "mix": mix, "packed": packed, "total": total_upper, **borders},
        {
            "base": base,
            "acts": acts,
            "passed_early": (passed[0], 0, early),
            "passed_late": (passed[1], early, micros - early),
            "above": above,
            "below": below,
            **image,
        },
        {"result": ((micros, wide, channels), BF16), "edge": ((micros, 16, channels), BF16)},
        {},
        {},
    )
    near = swap(edge, "sub")
    half = kernel.shape[1] // 2
    norm, reduced, keep, give = call(
        functools.partial(own_kernel, *size),
        "own_block",
        micros,
        {"boxes": boxes},
        {"sums": sums, "mix": mix, "kernel": kernel[0], **borders},
        {"result": result, "near": near, "acts": acts, **image},
        {"norm": ((micros, pixels, channels), BF16), "reduced": ((micros, 16, channels), F32)},
        {"keep": ((half, channels), F32), "give": ((half, channels), F32)},
        {**work, "hidden": ((pixels, channels), BF16), "total": ((3, channels, triple), F32)},
    )
    keep = (keep + swap(give, "sub")).astype(BF16)
    others = [shift(keep, "rows", steps) for steps in (1, 2, 3)]
    total_lower = pixel_total(reduced.reshape(micros * 16, channels))
    grads, mod_grad, bias_grad = call(
        functools.partial(last_kernel, rows, cols, micros, count),
        "input_gradient",
        micros,
        {},
        {"sums": sums, "mix": mix, "total_lower": total_lower, "total_upper": total_upper},
        {"acts": acts, "norm": norm, "result": result},
        {"grads": ((micros, pixels, channels), BF16)},
        {"mod_grad": ((1, latents, 2 * channels), F32), "bias_grad": ((1, 2 * channels), F32)},
        {},
        work=1 << 25,
    )
    grads, *others = lax.optimization_barrier((grads, *others))
    one, two, three = [value.astype(F32) for value in others]
    keep = (keep.astype(F32) + two) + (one + three)
    give = swap(keep, "sub")
    kernel_grad = jnp.where(side == 0, jnp.concatenate([keep, give]), jnp.concatenate([give, keep]))
    return (grads.reshape(activations.shape), kernel_grad[None], mod_grad, bias_grad)


def solution(mesh):
    pair = mesh.shape["segment"] == 2 and mesh.shape["rows"] == 4 and mesh.shape["sub"] == 2
    body = pair_body if pair else general_body
    placed = (
        P("segment", "groups", "rows", "sub", None),
        P("groups", None, "rows", "sub"),
        P("groups", None, "rows", "sub"),
        P("groups", None, "rows", "sub"),
        P("groups", None, None),
        P("segment", None, None),
        P("segment", None, None),
        P("segment", None),
        P("segment", None),
        P(),
    )
    return jax.shard_map(
        body,
        mesh=mesh,
        in_specs=placed,
        out_specs=(
            P("segment", "groups", "rows", "sub", None),
            P("segment", "groups", None),
            P("segment", "groups", None),
            P("segment", "groups"),
        ),
        check_vma=False,
    )
```

```python
import functools
import types

import jax
import jax.numpy as jnp
from jax import lax
from jax.experimental import pallas as pl
from jax.experimental.pallas import tpu as pltpu
from jax.sharding import PartitionSpec as P

GROUPS = 32
TILE = 32


EPS = 1e-06


def extended(block, sides, width):
    for axis, dim in sides:
        count = lax.axis_size(axis)
        forward = [(i, i + 1) for i in range(count - 1)]
        backward = [(target, source) for source, target in forward]
        low = lax.ppermute(
            lax.slice_in_dim(block, block.shape[dim] - width, None, axis=dim), axis, forward
        )
        high = lax.ppermute(lax.slice_in_dim(block, 0, width, axis=dim), axis, backward)
        block = jnp.concatenate([low, block, high], axis=dim)
    return block


def from_behind(value, axis, steps):
    count = lax.axis_size(axis)
    initial, last = (max(0, -steps), min(count, count - steps))
    return lax.ppermute(value, axis, [(source, source + steps) for source in range(initial, last)])


def crop_weights(boxes, row_start, col_start, row_count, col_count, total_rows, total_cols):
    row_tile = (row_start + jnp.arange(row_count, dtype=jnp.int32)) // TILE
    col_tile = (col_start + jnp.arange(col_count, dtype=jnp.int32)) // TILE
    first_row = boxes[:, :, 0:1]
    first_col = boxes[:, :, 1:2]
    box_height = boxes[:, :, 2:3]
    box_width = boxes[:, :, 3:4]
    in_rows = ((row_tile >= first_row) & (row_tile < first_row + box_height)).astype(jnp.float32)
    in_cols = ((col_tile >= first_col) & (col_tile < first_col + box_width)).astype(jnp.float32)
    tiles = total_rows // TILE * (total_cols // TILE)
    share = tiles / (boxes.shape[1] * (box_height * box_width).astype(jnp.float32))
    return jnp.einsum("mkr,mkc->mrc", in_rows * share, in_cols)


def top_gradient(recon, target, cropped, out_weight):
    diff = 2.0 * (recon.astype(jnp.float32) - target.astype(jnp.float32)) * cropped[:, None]
    return jnp.einsum("mkhw,kc->mhwc", diff, out_weight.astype(jnp.float32)).astype(jnp.bfloat16)


def loss_gradient(
    boxes,
    recon,
    target,
    out_weight,
    row_start,
    col_start,
    row_count,
    col_count,
    total_rows,
    total_cols,
):
    cropped = crop_weights(
        boxes, row_start, col_start, row_count, col_count, total_rows, total_cols
    )
    return top_gradient(recon, target, cropped, out_weight)


def grouped_layout(value_array):
    return value_array.reshape(value_array.shape[:-1] + (GROUPS, value_array.shape[-1] // GROUPS))


def group_sums(value_array):
    shaped = grouped_layout(value_array)
    return (jnp.sum(shaped, axis=(-4, -3, -1)), jnp.sum(shaped * shaped, axis=(-4, -3, -1)))


def expand(stat):
    return stat[..., None, None, :, None]


def normalized_values(value_array, mean_val, rstd_val):
    shaped = grouped_layout(value_array)
    return ((shaped - expand(mean_val)) * expand(rstd_val)).reshape(value_array.shape)


def modulation(latent_batch, mix_weight, scale_row, shift_row):
    channel_count = scale_row.shape[-1]
    coefficients = jnp.einsum(
        "bzhw,zc->bhwc", latent_batch.astype(jnp.float32), mix_weight.astype(jnp.float32)
    )
    return (
        coefficients[..., :channel_count] + scale_row.astype(jnp.float32),
        coefficients[..., channel_count:] + shift_row.astype(jnp.float32),
    )


def transposed(weights):
    channel_count = weights.shape[-1]
    return (
        weights.reshape(9, channel_count, channel_count)
        .transpose(0, 2, 1)
        .reshape(9 * channel_count, channel_count)
    )


def taps(padded, row_count, col_count, flipped):
    pieces = []
    for tap_row in range(3):
        for tap_col in range(3):
            if flipped:
                row_offset, col_offset = (2 - tap_row, 2 - tap_col)
            else:
                row_offset, col_offset = (tap_row, tap_col)
            pieces.append(
                padded[:, row_offset : row_offset + row_count, col_offset : col_offset + col_count]
            )
    return jnp.concatenate(pieces, axis=-1).reshape(-1, 9 * padded.shape[-1])


def pick(value_array, index):
    return lax.dynamic_slice_in_dim(value_array, index, 1, 0)


def section_backward(
    value_array, latent_batch, incoming, spatial_scale, spatial_shift, weights_t, count
):
    batch, row_count, col_count, channel_count = value_array.shape
    sum_one, sum_two = group_sums(value_array)
    sum_one, sum_two = lax.psum((sum_one, sum_two), ("rows", "sub"))
    group_mean = sum_one / count
    inverse_deviation = lax.rsqrt(sum_two / count - group_mean * group_mean + EPS)
    centered_scaled = normalized_values(value_array, group_mean, inverse_deviation)
    pre_activation = centered_scaled * spatial_scale + spatial_shift
    hidden = jax.nn.silu(pre_activation).astype(jnp.bfloat16)
    padded_h = extended(hidden, (("rows", 1), ("sub", 2)), 1)
    padded_g = extended(incoming, (("rows", 1), ("sub", 2)), 1)
    patches = taps(padded_h, row_count, col_count, False)
    kernel_term = lax.dot_general(
        patches,
        incoming.reshape(-1, channel_count),
        (((0,), (0,)), ((), ())),
        preferred_element_type=jnp.float32,
    )
    hidden_grad = jnp.dot(
        taps(padded_g, row_count, col_count, True), weights_t, preferred_element_type=jnp.float32
    ).reshape(value_array.shape)
    sig = jax.nn.sigmoid(pre_activation)
    pre_activation_gradient = hidden_grad * (sig * (1.0 + pre_activation * (1.0 - sig)))
    paired_parts = jnp.concatenate(
        [pre_activation_gradient * centered_scaled, pre_activation_gradient], axis=-1
    )
    mod_term = jnp.einsum("bzhw,bhwc->zc", latent_batch.astype(jnp.float32), paired_parts)
    bias_term = jnp.sum(paired_parts, axis=(0, 1, 2))
    shaped_grad = grouped_layout(pre_activation_gradient * spatial_scale)
    reshaped_normalized = grouped_layout(centered_scaled)
    part_one = jnp.sum(shaped_grad, axis=(1, 2, 4))
    part_two = jnp.sum(shaped_grad * reshaped_normalized, axis=(1, 2, 4))
    part_one, part_two = lax.psum((part_one, part_two), ("rows", "sub"))
    mean_grad = part_one / count
    mean_cross = part_two / count
    adjust = expand(inverse_deviation) * (
        shaped_grad - expand(mean_grad) - reshaped_normalized * expand(mean_cross)
    )
    result = (incoming.astype(jnp.float32) + adjust.reshape(value_array.shape)).astype(jnp.bfloat16)
    return (result, kernel_term, mod_term, bias_term)


def general_body(
    activations,
    latent,
    recon,
    target,
    boxes,
    kernel,
    mod_weight,
    scale_bias,
    shift_bias,
    out_weight,
):
    segments = lax.axis_size("segment")
    segment_index = lax.axis_index("segment")
    micro, row_count, col_count, channel_count = activations.shape[1:]
    total_rows = row_count * lax.axis_size("rows")
    total_cols = col_count * lax.axis_size("sub")
    count = total_rows * total_cols * (channel_count // GROUPS)
    row_start = lax.axis_index("rows") * row_count
    col_start = lax.axis_index("sub") * col_count
    acts = activations[0]
    weights_t = transposed(kernel[0])
    mix_weight = mod_weight[0]
    scale_row = scale_bias[0]
    shift_row = shift_bias[0]
    top = loss_gradient(
        boxes,
        recon,
        target,
        out_weight,
        row_start,
        col_start,
        row_count,
        col_count,
        total_rows,
        total_cols,
    )

    def tick(step, carry):
        passing, grads_out, kernel_grad, mod_grad, bias_grad = carry
        offset = step - (segments - 1 - segment_index)
        valid = (offset >= 0) & (offset < micro)
        index = jnp.clip(offset, 0, micro - 1)
        received = from_behind(passing, "segment", -1)
        incoming = jnp.where(segment_index == segments - 1, pick(top, index), received)
        value_array = pick(acts, index).astype(jnp.float32)
        latent_m = pick(latent, index)
        spatial_scale, spatial_shift = modulation(latent_m, mix_weight, scale_row, shift_row)
        result, kernel_term, mod_term, bias_term = section_backward(
            value_array, latent_m, incoming, spatial_scale, spatial_shift, weights_t, count
        )
        weight = valid.astype(jnp.float32)
        current = pick(grads_out, index)
        grads_out = lax.dynamic_update_slice_in_dim(
            grads_out, jnp.where(valid, result, current), index, 0
        )
        return (
            result,
            grads_out,
            kernel_grad + weight * kernel_term,
            mod_grad + weight * mod_term,
            bias_grad + weight * bias_term,
        )

    initial = (
        jnp.zeros((1, row_count, col_count, channel_count), jnp.bfloat16),
        jnp.zeros_like(acts),
        jnp.zeros((9 * channel_count, channel_count), jnp.float32),
        jnp.zeros((mix_weight.shape[0], 2 * channel_count), jnp.float32),
        jnp.zeros((2 * channel_count,), jnp.float32),
    )
    final = lax.fori_loop(0, micro + segments - 1, tick, initial)
    grads_out = final[1][None]
    kernel_grad = final[2][None]
    mod_grad = final[3][None]
    bias_grad = final[4][None]
    kernel_grad, mod_grad, bias_grad = lax.psum((kernel_grad, mod_grad, bias_grad), ("rows", "sub"))
    return (grads_out, kernel_grad, mod_grad, bias_grad)


EXACT = lax.Precision.HIGHEST
TN = (((0,), (0,)), ((), ()))
NT = (((1,), (1,)), ((), ()))
F32 = jnp.float32
BF16 = jnp.bfloat16


def swap(value, axis):
    return lax.ppermute(value, axis, [(0, 1), (1, 0)])


def shift(value, axis, steps):
    count = lax.axis_size(axis)
    return lax.ppermute(value, axis, [(i, (i + steps) % count) for i in range(count)])


def pixel_total(value):
    return rows_total(value + swap(value, "sub"))


def rows_total(value):
    one, two, three = [shift(value, "rows", steps) for steps in (1, 2, 3)]
    return (value + two) + (one + three)


def same_group(channels):
    per = channels // GROUPS
    left = lax.broadcasted_iota(jnp.int32, (channels, channels), 0) // per
    right = lax.broadcasted_iota(jnp.int32, (channels, channels), 1) // per
    return (left == right).astype(F32)


def statistics(sums_ref, micro, micros, count):
    member = same_group(sums_ref.shape[-1])
    both = jnp.concatenate([sums_ref[pl.ds(micro, 1), :], sums_ref[pl.ds(micros + micro, 1), :]], axis=0)
    both = jnp.dot(both, member, precision=EXACT, preferred_element_type=F32) / count
    mean = both[0:1]
    return mean, lax.rsqrt(both[1:2] - mean * mean + EPS)


def gradient_means(total, mix, count):
    mean_grad = jnp.sum(mix[:8] * total[8:], axis=0, keepdims=True)
    mean_cross = jnp.sum(mix[:8] * total[:8], axis=0, keepdims=True)
    both = jnp.concatenate([mean_grad, mean_cross], axis=0)
    both = jnp.dot(both, same_group(total.shape[-1]), precision=EXACT, preferred_element_type=F32) / count
    return both[0:1], both[1:2]


def side_by_side(mix):
    return jnp.concatenate([mix[:8], mix[8:]], axis=1).astype(BF16)


def sums_kernel(n, micro):
    micros = n.sums.shape[0] // 2
    value = n.acts[0].astype(F32)
    n.sums[pl.ds(micro, 1), :] = jnp.sum(value, axis=0, keepdims=True)
    n.sums[pl.ds(micros + micro, 1), :] = jnp.sum(value * value, axis=0, keepdims=True)


class Band:
    def __init__(self, n, micro, rows, cols, bands):
        self.n, self.rows, self.cols = n, rows, cols
        self.head = n.from_up.shape[0] - 16 * (n.from_up.shape[0] // 16)
        self.micro = micro
        self.side = lax.axis_index("sub")
        self.row_start = lax.axis_index("rows") * rows
        self.total_rows = rows * bands
        lane = lax.broadcasted_iota(jnp.int32, (1, cols), 1)
        crops = n.boxes.shape[1]
        tiles = self.total_rows // TILE * (2 * cols // TILE)
        self.boxes = []
        for k in range(crops):
            row, col, height, width = [n.boxes[micro, k, i] for i in range(4)]
            share = tiles / jnp.full((1, cols), crops * height * width, jnp.int32).astype(F32)
            inside = []
            for side in (self.side, 1 - self.side):
                at = lane + side * cols
                inside.append(jnp.where((at >= col * TILE) & (at < (col + width) * TILE), share, 0.0))
            self.boxes.append((row * TILE, (row + height) * TILE, inside[0], inside[1]))
        weight = n.out_weight[...].astype(F32)
        blank = jnp.zeros((8 - weight.shape[0], weight.shape[1]), F32)
        self.own = jnp.concatenate([jnp.concatenate([weight, blank])] * 3).astype(BF16)
        self.other = jnp.concatenate([jnp.concatenate([blank[:3], weight, blank[3:]])] * 3).astype(BF16)

    def border(self, ref, which):
        return ref[pl.ds(pl.multiple_of(self.head + 16 * self.micro + 8 * which, 8), 8), :]

    def planes(self, r):
        if r < 0:
            return self.border(self.n.from_up, r + 2)
        if r >= self.rows:
            return self.border(self.n.from_down, r - self.rows)
        own = self.n.recon[0, :, r, :].astype(F32) - self.n.target[0, :, r, :].astype(F32)
        beside = self.n.recon_beside[0, :, r, :].astype(F32) - self.n.target_beside[0, :, r, :].astype(F32)
        return jnp.concatenate([own, beside, jnp.zeros((2, self.cols), F32)])

    def latent(self, r):
        if r < 0 or r >= self.rows:
            ref = self.n.from_up if r < 0 else self.n.from_down
            value = jnp.concatenate([self.border(ref, 0)[6:8], self.border(ref, 1)[6:8]])
        else:
            value = self.n.latent[0, :, r, :].astype(F32)
        count = value.shape[0]
        return jnp.concatenate([value, jnp.ones((1, self.cols), F32), jnp.zeros((7 - count, self.cols), F32)]).astype(BF16)

    def row(self, r):
        diff = self.planes(r)
        at = self.row_start + r
        own = jnp.zeros((1, self.cols), F32)
        other = jnp.zeros((1, self.cols), F32)
        for first, end, own_share, other_share in self.boxes:
            here = (at >= first) & (at < end)
            own = own + jnp.where(here, own_share, 0.0)
            other = other + jnp.where(here, other_share, 0.0)
        plane = lax.broadcasted_iota(jnp.int32, (8, self.cols), 0)
        diff = 2.0 * diff * jnp.where(plane < 3, own, other)
        high = diff.astype(BF16).astype(F32)
        middle = (diff - high).astype(BF16).astype(F32)
        parts = jnp.concatenate([high, middle, diff - high - middle]).astype(BF16)
        value = lax.dot_general(parts, self.own, TN, preferred_element_type=F32).astype(BF16)
        beside = lax.dot_general(parts, self.other, TN, preferred_element_type=F32).astype(BF16).astype(F32)
        return value, jnp.where(self.side == 0, beside[0:1], beside[self.cols - 1 : self.cols])


def spread(index, cols, value, near, shifted):
    channels = value.shape[-1]
    side = lax.axis_index("sub")
    at = slice(index * cols, (index + 1) * cols)
    place = lax.broadcasted_iota(jnp.int32, (cols, channels), 0)
    wide = value.astype(F32)
    before = jnp.where(side == 1, near, 0.0)
    behind = jnp.where(side == 0, near, 0.0)
    shifted[at, 0:channels] = jnp.where(place == 0, before, pltpu.roll(wide, 1, 0)).astype(BF16)
    shifted[at, channels : 2 * channels] = value
    shifted[at, 2 * channels :] = jnp.where(place == cols - 1, behind, pltpu.roll(wide, cols - 1, 0)).astype(BF16)


def tap_of(row, col):
    return 3 * (2 - row) + (2 - col)


def arrange_weights(kernel_ref, weights):
    channels = kernel_ref.shape[-1]
    for row in range(3):
        for col in range(3):
            tap = tap_of(row, col)
            weights[row, :, col * channels : (col + 1) * channels] = kernel_ref[tap * channels : (tap + 1) * channels, :]


def hidden_gradient(rows, cols, shifted, weights, hidden_grad):
    pixels = rows * cols
    total = lax.dot_general(shifted[0:pixels, :], weights[0], NT, preferred_element_type=F32)
    total = total + lax.dot_general(shifted[cols : cols + pixels, :], weights[1], NT, preferred_element_type=F32)
    hidden_grad[0:pixels, :] = total + lax.dot_general(
        shifted[2 * cols : 2 * cols + pixels, :], weights[2], NT, preferred_element_type=F32
    )


def pixel_values(acts, latent, mix, mean, rstd):
    channels = mean.shape[-1]
    xhat = (acts.astype(F32) - mean) * rstd
    mixed = lax.dot_general(latent, mix, TN, preferred_element_type=F32)
    scale = mixed[:, :channels]
    pre = xhat * scale + mixed[:, channels:]
    sig = 0.5 * jnp.tanh(0.5 * pre) + 0.5
    hidden = pre * sig
    return xhat, scale, hidden, sig + hidden * (1.0 - sig)


def reduce_block(n, band, mean, rstd, mix, step, base=False):
    rows, cols = band.rows, band.cols
    channels = n.acts.shape[-1]
    hidden_gradient(rows, cols, n.shifted, n.weights, n.hidden_grad)
    for r in range(rows):
        at = slice(r * cols, (r + 1) * cols)
        latent = band.latent(r)
        n.latent_keep[:, at] = latent
        xhat, scale, hidden, slope = pixel_values(n.acts[0, at, :], latent, mix, mean, rstd)
        pre_grad = n.hidden_grad[at, :] * slope
        norm = pre_grad * scale
        if base:
            norm = n.shifted[(r + 1) * cols : (r + 2) * cols, channels : 2 * channels].astype(F32) + rstd * norm
            n.base[0, (r + 1) * cols : (r + 2) * cols, :] = norm.astype(BF16)
        else:
            n.norm[0, at, :] = norm.astype(BF16)
            n.hidden[at, :] = hidden.astype(BF16)
        n.pairs[at, 0:channels] = (pre_grad * xhat).astype(BF16)
        n.pairs[at, channels:] = pre_grad.astype(BF16)
    reduced = jnp.dot(n.latent_keep[...], n.pairs[...], preferred_element_type=F32)
    reduced = jnp.concatenate([reduced[:, :channels], reduced[:, channels:]])
    n.reduced[0] = reduced
    if not base:
        n.give[pl.ds(pl.multiple_of(n.keep.shape[0] + 16 * step, 8), 16), :] = reduced


def upper_kernel(rows, cols, bands, micros, count, n, step):
    active = lax.axis_index("segment") == 1

    @pl.when(active)
    def _():
        @pl.when(step == 0)
        def _():
            arrange_weights(n.kernel, n.weights)
            head = 2 * micros
            n.sums_keep[...] = (n.sums[...] + n.across[...]) + (n.from_up[0:head, :] + n.from_down[0:head, :])

        mean, rstd = statistics(n.sums_keep, step, micros, count)
        channels = mean.shape[-1]
        mix = [n.mod_weight[0].astype(F32), jnp.concatenate([n.scale_bias[...], n.shift_bias[...]], axis=1).astype(F32)]
        mix.append(jnp.zeros((7 - mix[0].shape[0], 2 * channels), F32))
        band = Band(n, step, rows, cols, bands)
        for r in range(rows + 2):
            spread(r, cols, *band.row(r - 1), n.shifted)
        reduce_block(n, band, mean, rstd, jnp.concatenate(mix).astype(BF16), step, base=True)

    @pl.when(jnp.logical_not(active))
    def _():
        @pl.when(step == 0)
        def _():
            arrange_weights(n.kernel_passed, n.weights)

        n.reduced[...] = jnp.zeros_like(n.reduced)
        band = Band(n, step, rows, cols, bands)
        for r in range(rows + 4):
            spread(r, cols, *band.row(r - 2), n.shifted)
        hidden_gradient(rows + 2, cols, n.shifted, n.weights, n.hidden_grad)
        n.base[0] = n.hidden_grad[...].astype(BF16)


def own_kernel(rows, cols, bands, micros, count, n, step):
    pixels = rows * cols
    side = lax.axis_index("sub")
    segment = lax.axis_index("segment")

    @pl.when(step == 0)
    def _():
        n.total[...] = jnp.zeros_like(n.total)

        @pl.when(segment == 0)
        def _():
            arrange_weights(n.kernel, n.weights)

    mean, rstd = statistics(n.sums, step, micros, count)
    band = Band(n, step, rows, cols, bands)
    mix = side_by_side(n.mix[...])

    @pl.when(segment == 1)
    def _():
        n.reduced[...] = jnp.zeros_like(n.reduced)
        n.give[pl.ds(pl.multiple_of(n.keep.shape[0] + 16 * step, 8), 16), :] = jnp.zeros_like(n.reduced[0])
        for r in range(rows + 2):
            spread(r, cols, *band.row(r - 1), n.shifted)
        for r in range(rows):
            at = slice(r * cols, (r + 1) * cols)
            n.hidden[at, :] = pixel_values(n.acts[0, at, :], band.latent(r), mix, mean, rstd)[2].astype(BF16)

    @pl.when(segment == 0)
    def _():
        near = n.near[0].astype(F32)
        for r in range(rows + 2):
            spread(r, cols, n.result[0, r * cols : (r + 1) * cols, :], near[r : r + 1], n.shifted)
        reduce_block(n, band, mean, rstd, mix, step)

    for row in range(3):
        n.total[row] += lax.dot_general(
            n.hidden[...], n.shifted[row * cols : row * cols + pixels, :], TN, preferred_element_type=F32
        )

    @pl.when(step == micros - 1)
    def _():
        half, channels = n.keep.shape
        for which in range(2):
            for ref, owner in ((n.keep, which), (n.give, 1 - which)):

                @pl.when(side == owner)
                def _(ref=ref, first=which * half):
                    for row in range(3):
                        for col in range(3):
                            at = tap_of(row, col) * channels - first
                            low, high = max(at, 0), min(at + channels, half)
                            if low < high:
                                ref[low:high, :] = n.total[row, low - at : high - at, col * channels : (col + 1) * channels]


def finish_kernel(rows, cols, bands, micros, count, n, step):
    channels = n.acts.shape[-1]
    segment = lax.axis_index("segment")
    side = lax.axis_index("sub")

    @pl.when(segment == 1)
    def _():
        mean, rstd = statistics(n.sums, step, micros, count)
        total = n.total[pl.ds(pl.multiple_of(16 * step, 8), 16), :]
        mean_grad, mean_cross = gradient_means(total, n.mix[...], count)
        for r in range(rows):
            at = slice((r + 1) * cols, (r + 2) * cols)
            xhat = (n.acts[0, r * cols : (r + 1) * cols, :].astype(F32) - mean) * rstd
            n.result[0, at, :] = (n.base[0, at, :].astype(F32) - rstd * (mean_grad + xhat * mean_cross)).astype(BF16)

    @pl.when(segment == 0)
    def _():
        mean, rstd = statistics(n.packed, step, micros, count)
        total = n.packed[pl.ds(pl.multiple_of(2 * micros + 16 * step, 8), 16), :]
        mix = n.packed[2 * micros + 16 * micros :, :]
        mean_grad, mean_cross = gradient_means(total, mix, count)
        wide_mix = side_by_side(mix)
        band = Band(n, step, rows, cols, bands)
        edges = []
        for r in range(rows + 2):
            at = slice(r * cols, (r + 1) * cols)
            if r == 0:
                acts = n.above[0]
            elif r == rows + 1:
                acts = n.below[0]
            elif r == 1 or r == rows:
                acts = n.outer[0, 0:cols, :] if r == 1 else n.outer[0, cols:, :]
            else:
                acts = n.inner[0, (r - 2) * cols : (r - 1) * cols, :]
            xhat, scale, _, slope = pixel_values(acts, band.latent(r - 1), wide_mix, mean, rstd)
            change = rstd * (n.base[0, at, :].astype(F32) * slope * scale - mean_grad - xhat * mean_cross)
            value = band.row(r - 1)[0].astype(F32) + change
            if r == 0 or r == rows + 1:
                row = band.row_start + (r - 1)
                value = jnp.where((row >= 0) & (row < band.total_rows), value, 0.0)
            n.result[0, at, :] = value.astype(BF16)
            edges.append(jnp.where(side == 0, value[cols - 1 : cols], value[0:1]))
        edges.append(jnp.zeros((16 - rows - 2, channels), F32))
        n.edge[0] = jnp.concatenate(edges).astype(BF16)


def last_kernel(rows, cols, micros, count, n, step):
    lower = lax.axis_index("segment") == 0

    @pl.when(step == 0)
    def _():
        latents, channels = n.mod_grad.shape[1], n.total_lower.shape[-1]
        total = jnp.zeros((16, channels), F32)
        for m in range(micros):
            at = slice(16 * m, 16 * (m + 1))
            total = total + jnp.where(lower, n.total_lower[at, :], n.total_upper[at, :])
        total = jnp.concatenate([total[:8], total[8:]], axis=1)
        n.mod_grad[0] = total[:latents]
        n.bias_grad[...] = total[latents : latents + 1]

    @pl.when(lower)
    def _():
        mean, rstd = statistics(n.sums, step, micros, count)
        total = n.total_lower[pl.ds(pl.multiple_of(16 * step, 8), 16), :]
        mean_grad, mean_cross = gradient_means(total, n.mix[...], count)
        for r in range(rows):
            at = slice(r * cols, (r + 1) * cols)
            xhat = (n.acts[0, at, :].astype(F32) - mean) * rstd
            change = rstd * (n.norm[0, at, :].astype(F32) - mean_grad - xhat * mean_cross)
            n.grads[0, at, :] = (n.result[0, (r + 1) * cols : (r + 2) * cols, :].astype(F32) + change).astype(BF16)

    @pl.when(jnp.logical_not(lower))
    def _():
        n.grads[0] = n.result[0, cols : (rows + 1) * cols, :]


def by_micro(value):
    rest = (0,) * (len(value.shape) - 1)
    return pl.BlockSpec((1,) + tuple(value.shape[1:]), lambda m: (m,) + rest)


def whole(value):
    return pl.BlockSpec(tuple(value.shape), lambda m: (0,) * len(value.shape))


def call(kernel, name, micros, scalars, fixed, cut, outs, fixed_outs, scratch, work=4, room=16):
    names = [*scalars, *fixed, *cut, *outs, *fixed_outs, *scratch]
    cut_shape = [jax.ShapeDtypeStruct(s, d) for s, d in outs.values()]
    fixed_shape = [jax.ShapeDtypeStruct(s, d) for s, d in fixed_outs.values()]

    def body(*refs):
        kernel(types.SimpleNamespace(**dict(zip(names, refs))), pl.program_id(0))

    return pl.pallas_call(
        body,
        grid=(micros,),
        in_specs=[pl.BlockSpec(memory_space=pltpu.SMEM) for _ in scalars]
        + [whole(v) for v in fixed.values()]
        + [by_micro(v) for v in cut.values()],
        out_specs=[by_micro(s) for s in cut_shape] + [whole(s) for s in fixed_shape],
        out_shape=cut_shape + fixed_shape,
        scratch_shapes=[pltpu.VMEM(s, d) for s, d in scratch.values()],
        compiler_params=pltpu.CompilerParams(vmem_limit_bytes=room * 1024 * 1024),
        cost_estimate=pl.CostEstimate(flops=work, bytes_accessed=work // 4, transcendentals=0),
        name=name,
    )(*scalars.values(), *fixed.values(), *cut.values())


def pair_body(
    activations, latent, recon, target, boxes, kernel, mod_weight, scale_bias, shift_bias, out_weight
):
    micros, rows, cols, channels = activations.shape[1:]
    latents = latent.shape[1]
    pixels = rows * cols
    bands = lax.axis_size("rows")
    count = float(pixels * bands * 2 * (channels // GROUPS))
    segment = lax.axis_index("segment")
    side = lax.axis_index("sub")
    acts = activations[0].reshape(micros, pixels, channels)

    outer = swap(jnp.concatenate([acts[:, :cols], acts[:, pixels - cols :]], axis=1), "segment")
    inner = swap(acts[:, cols : pixels - cols], "segment")
    kernel_passed = swap(kernel[0], "segment")
    recon_beside, target_beside = swap(recon, "sub"), swap(target, "sub")

    (sums,) = call(sums_kernel, "input_sums", micros, {}, {}, {"acts": acts}, {}, {"sums": ((2 * micros, channels), F32)}, {})
    sums = sums + swap(sums, "sub")

    def border(first, r):
        def difference(one, two):
            part = slice(first, first + 2)
            return (one[:, :, part].astype(F32) - two[:, :, part].astype(F32)).transpose(0, 2, 1, 3)

        extra = latent[:, :, r].astype(F32).reshape(micros, 2, latents // 2, cols)
        two = jnp.concatenate([difference(recon, target), difference(recon_beside, target_beside), extra], axis=2)
        return jnp.concatenate([sums, two.reshape(micros * 16, cols)])

    from_up = shift(border(rows - 2, rows - 1), "rows", 1)
    from_down = shift(border(0, 0), "rows", bands - 1)
    across = shift(sums, "rows", 2)

    from_up, kernel_passed = lax.optimization_barrier((from_up, kernel_passed))
    image = {
        "latent": latent,
        "recon": recon,
        "target": target,
        "recon_beside": recon_beside,
        "target_beside": target_beside,
    }
    borders = {"from_up": from_up, "from_down": from_down, "out_weight": out_weight}
    wide = (rows + 2) * cols
    triple = 3 * channels
    shifted = {"shifted": ((wide, triple), BF16)}
    work = {
        **shifted,
        "weights": ((3, channels, triple), BF16),
        "hidden_grad": ((pixels, channels), F32),
        "latent_keep": ((8, pixels), BF16),
        "pairs": ((pixels, 2 * channels), BF16),
    }
    size = (rows, cols, bands, micros, count)
    sums_own = (sums + across) + (from_up[: 2 * micros] + from_down[: 2 * micros])
    mix = jnp.concatenate([mod_weight[0], jnp.concatenate([scale_bias, shift_bias], axis=1)]).astype(F32)
    mix = jnp.pad(mix, ((0, 7 - latents), (0, 0)))
    mix = jnp.concatenate([mix[:, :channels], mix[:, channels:]])
    base, reduced = call(
        functools.partial(upper_kernel, *size),
        "upper_block",
        micros,
        {"boxes": boxes},
        {
            "sums": sums,
            "across": across,
            "mod_weight": mod_weight,
            "scale_bias": scale_bias,
            "shift_bias": shift_bias,
            "kernel": kernel[0],
            "kernel_passed": kernel_passed,
            **borders,
        },
        {"acts": acts, **image},
        {"base": ((micros, wide, channels), BF16), "reduced": ((micros, 16, channels), F32)},
        {},
        {
            **work,
            "shifted": (((rows + 4) * cols, triple), BF16),
            "hidden_grad": ((wide, channels), F32),
            "sums_keep": ((2 * micros, channels), F32),
        },
    )
    sums = sums_own
    reduced, outer = lax.optimization_barrier((reduced, outer))
    above = shift(outer[:, cols:], "rows", 1)
    below = shift(outer[:, :cols], "rows", bands - 1)
    total_upper = pixel_total(reduced.reshape(micros * 16, channels))
    packed = jnp.concatenate([sums, total_upper, mix])
    packed, inner, above = lax.optimization_barrier((packed, inner, above))
    packed = swap(packed, "segment")
    result, edge = call(
        functools.partial(finish_kernel, *size),
        "finish_upper",
        micros,
        {"boxes": boxes},
        {"sums": sums, "mix": mix, "packed": packed, "total": total_upper, **borders},
        {
            "base": base,
            "acts": acts,
            "outer": outer,
            "inner": inner,
            "above": above,
            "below": below,
            **image,
        },
        {"result": ((micros, wide, channels), BF16), "edge": ((micros, 16, channels), BF16)},
        {},
        {},
    )
    near = swap(edge, "sub")
    half = kernel.shape[1] // 2
    norm, reduced, keep, give = call(
        functools.partial(own_kernel, *size),
        "own_block",
        micros,
        {"boxes": boxes},
        {"sums": sums, "mix": mix, "kernel": kernel[0], **borders},
        {"result": result, "near": near, "acts": acts, **image},
        {"norm": ((micros, pixels, channels), BF16), "reduced": ((micros, 16, channels), F32)},
        {"keep": ((half, channels), F32), "give": ((half + micros * 16, channels), F32)},
        {**work, "hidden": ((pixels, channels), BF16), "total": ((3, channels, triple), F32)},
    )
    got = swap(give, "sub")
    keep = (keep + got[:half]).astype(BF16)
    others = [shift(keep, "rows", steps) for steps in (1, 2, 3)]
    total_lower = rows_total(reduced.reshape(micros * 16, channels) + got[half:])
    grads, mod_grad, bias_grad = call(
        functools.partial(last_kernel, rows, cols, micros, count),
        "input_gradient",
        micros,
        {},
        {"sums": sums, "mix": mix, "total_lower": total_lower, "total_upper": total_upper},
        {"acts": acts, "norm": norm, "result": result},
        {"grads": ((micros, pixels, channels), BF16)},
        {"mod_grad": ((1, latents, 2 * channels), F32), "bias_grad": ((1, 2 * channels), F32)},
        {},
        work=1 << 25,
    )
    grads, *others = lax.optimization_barrier((grads, *others))
    one, two, three = [value.astype(F32) for value in others]
    keep = (keep.astype(F32) + two) + (one + three)
    give = swap(keep, "sub")
    kernel_grad = jnp.where(side == 0, jnp.concatenate([keep, give]), jnp.concatenate([give, keep]))
    return (grads.reshape(activations.shape), kernel_grad[None], mod_grad, bias_grad)


def solution(mesh):
    pair = mesh.shape["segment"] == 2 and mesh.shape["rows"] == 4 and mesh.shape["sub"] == 2
    body = pair_body if pair else general_body
    placed = (
        P("segment", "groups", "rows", "sub", None),
        P("groups", None, "rows", "sub"),
        P("groups", None, "rows", "sub"),
        P("groups", None, "rows", "sub"),
        P("groups", None, None),
        P("segment", None, None),
        P("segment", None, None),
        P("segment", None),
        P("segment", None),
        P(),
    )
    return jax.shard_map(
        body,
        mesh=mesh,
        in_specs=placed,
        out_specs=(
            P("segment", "groups", "rows", "sub", None),
            P("segment", "groups", None),
            P("segment", "groups", None),
            P("segment", "groups"),
        ),
        check_vma=False,
    )
```

```python
import functools
import types

import jax
import jax.numpy as jnp
from jax import lax
from jax.experimental import pallas as pl
from jax.experimental.pallas import tpu as pltpu
from jax.sharding import PartitionSpec as P

GROUPS = 32
TILE = 32


EPS = 1e-06


def extended(block, sides, width):
    for axis, dim in sides:
        count = lax.axis_size(axis)
        forward = [(i, i + 1) for i in range(count - 1)]
        backward = [(target, source) for source, target in forward]
        low = lax.ppermute(
            lax.slice_in_dim(block, block.shape[dim] - width, None, axis=dim), axis, forward
        )
        high = lax.ppermute(lax.slice_in_dim(block, 0, width, axis=dim), axis, backward)
        block = jnp.concatenate([low, block, high], axis=dim)
    return block


def from_behind(value, axis, steps):
    count = lax.axis_size(axis)
    initial, last = (max(0, -steps), min(count, count - steps))
    return lax.ppermute(value, axis, [(source, source + steps) for source in range(initial, last)])


def crop_weights(boxes, row_start, col_start, row_count, col_count, total_rows, total_cols):
    row_tile = (row_start + jnp.arange(row_count, dtype=jnp.int32)) // TILE
    col_tile = (col_start + jnp.arange(col_count, dtype=jnp.int32)) // TILE
    first_row = boxes[:, :, 0:1]
    first_col = boxes[:, :, 1:2]
    box_height = boxes[:, :, 2:3]
    box_width = boxes[:, :, 3:4]
    in_rows = ((row_tile >= first_row) & (row_tile < first_row + box_height)).astype(jnp.float32)
    in_cols = ((col_tile >= first_col) & (col_tile < first_col + box_width)).astype(jnp.float32)
    tiles = total_rows // TILE * (total_cols // TILE)
    share = tiles / (boxes.shape[1] * (box_height * box_width).astype(jnp.float32))
    return jnp.einsum("mkr,mkc->mrc", in_rows * share, in_cols)


def top_gradient(recon, target, cropped, out_weight):
    diff = 2.0 * (recon.astype(jnp.float32) - target.astype(jnp.float32)) * cropped[:, None]
    return jnp.einsum("mkhw,kc->mhwc", diff, out_weight.astype(jnp.float32)).astype(jnp.bfloat16)


def loss_gradient(
    boxes,
    recon,
    target,
    out_weight,
    row_start,
    col_start,
    row_count,
    col_count,
    total_rows,
    total_cols,
):
    cropped = crop_weights(
        boxes, row_start, col_start, row_count, col_count, total_rows, total_cols
    )
    return top_gradient(recon, target, cropped, out_weight)


def grouped_layout(value_array):
    return value_array.reshape(value_array.shape[:-1] + (GROUPS, value_array.shape[-1] // GROUPS))


def group_sums(value_array):
    shaped = grouped_layout(value_array)
    return (jnp.sum(shaped, axis=(-4, -3, -1)), jnp.sum(shaped * shaped, axis=(-4, -3, -1)))


def expand(stat):
    return stat[..., None, None, :, None]


def normalized_values(value_array, mean_val, rstd_val):
    shaped = grouped_layout(value_array)
    return ((shaped - expand(mean_val)) * expand(rstd_val)).reshape(value_array.shape)


def modulation(latent_batch, mix_weight, scale_row, shift_row):
    channel_count = scale_row.shape[-1]
    coefficients = jnp.einsum(
        "bzhw,zc->bhwc", latent_batch.astype(jnp.float32), mix_weight.astype(jnp.float32)
    )
    return (
        coefficients[..., :channel_count] + scale_row.astype(jnp.float32),
        coefficients[..., channel_count:] + shift_row.astype(jnp.float32),
    )


def transposed(weights):
    channel_count = weights.shape[-1]
    return (
        weights.reshape(9, channel_count, channel_count)
        .transpose(0, 2, 1)
        .reshape(9 * channel_count, channel_count)
    )


def taps(padded, row_count, col_count, flipped):
    pieces = []
    for tap_row in range(3):
        for tap_col in range(3):
            if flipped:
                row_offset, col_offset = (2 - tap_row, 2 - tap_col)
            else:
                row_offset, col_offset = (tap_row, tap_col)
            pieces.append(
                padded[:, row_offset : row_offset + row_count, col_offset : col_offset + col_count]
            )
    return jnp.concatenate(pieces, axis=-1).reshape(-1, 9 * padded.shape[-1])


def pick(value_array, index):
    return lax.dynamic_slice_in_dim(value_array, index, 1, 0)


def section_backward(
    value_array, latent_batch, incoming, spatial_scale, spatial_shift, weights_t, count
):
    batch, row_count, col_count, channel_count = value_array.shape
    sum_one, sum_two = group_sums(value_array)
    sum_one, sum_two = lax.psum((sum_one, sum_two), ("rows", "sub"))
    group_mean = sum_one / count
    inverse_deviation = lax.rsqrt(sum_two / count - group_mean * group_mean + EPS)
    centered_scaled = normalized_values(value_array, group_mean, inverse_deviation)
    pre_activation = centered_scaled * spatial_scale + spatial_shift
    hidden = jax.nn.silu(pre_activation).astype(jnp.bfloat16)
    padded_h = extended(hidden, (("rows", 1), ("sub", 2)), 1)
    padded_g = extended(incoming, (("rows", 1), ("sub", 2)), 1)
    patches = taps(padded_h, row_count, col_count, False)
    kernel_term = lax.dot_general(
        patches,
        incoming.reshape(-1, channel_count),
        (((0,), (0,)), ((), ())),
        preferred_element_type=jnp.float32,
    )
    hidden_grad = jnp.dot(
        taps(padded_g, row_count, col_count, True), weights_t, preferred_element_type=jnp.float32
    ).reshape(value_array.shape)
    sig = jax.nn.sigmoid(pre_activation)
    pre_activation_gradient = hidden_grad * (sig * (1.0 + pre_activation * (1.0 - sig)))
    paired_parts = jnp.concatenate(
        [pre_activation_gradient * centered_scaled, pre_activation_gradient], axis=-1
    )
    mod_term = jnp.einsum("bzhw,bhwc->zc", latent_batch.astype(jnp.float32), paired_parts)
    bias_term = jnp.sum(paired_parts, axis=(0, 1, 2))
    shaped_grad = grouped_layout(pre_activation_gradient * spatial_scale)
    reshaped_normalized = grouped_layout(centered_scaled)
    part_one = jnp.sum(shaped_grad, axis=(1, 2, 4))
    part_two = jnp.sum(shaped_grad * reshaped_normalized, axis=(1, 2, 4))
    part_one, part_two = lax.psum((part_one, part_two), ("rows", "sub"))
    mean_grad = part_one / count
    mean_cross = part_two / count
    adjust = expand(inverse_deviation) * (
        shaped_grad - expand(mean_grad) - reshaped_normalized * expand(mean_cross)
    )
    result = (incoming.astype(jnp.float32) + adjust.reshape(value_array.shape)).astype(jnp.bfloat16)
    return (result, kernel_term, mod_term, bias_term)


def general_body(
    activations,
    latent,
    recon,
    target,
    boxes,
    kernel,
    mod_weight,
    scale_bias,
    shift_bias,
    out_weight,
):
    segments = lax.axis_size("segment")
    segment_index = lax.axis_index("segment")
    micro, row_count, col_count, channel_count = activations.shape[1:]
    total_rows = row_count * lax.axis_size("rows")
    total_cols = col_count * lax.axis_size("sub")
    count = total_rows * total_cols * (channel_count // GROUPS)
    row_start = lax.axis_index("rows") * row_count
    col_start = lax.axis_index("sub") * col_count
    acts = activations[0]
    weights_t = transposed(kernel[0])
    mix_weight = mod_weight[0]
    scale_row = scale_bias[0]
    shift_row = shift_bias[0]
    top = loss_gradient(
        boxes,
        recon,
        target,
        out_weight,
        row_start,
        col_start,
        row_count,
        col_count,
        total_rows,
        total_cols,
    )

    def tick(step, carry):
        passing, grads_out, kernel_grad, mod_grad, bias_grad = carry
        offset = step - (segments - 1 - segment_index)
        valid = (offset >= 0) & (offset < micro)
        index = jnp.clip(offset, 0, micro - 1)
        received = from_behind(passing, "segment", -1)
        incoming = jnp.where(segment_index == segments - 1, pick(top, index), received)
        value_array = pick(acts, index).astype(jnp.float32)
        latent_m = pick(latent, index)
        spatial_scale, spatial_shift = modulation(latent_m, mix_weight, scale_row, shift_row)
        result, kernel_term, mod_term, bias_term = section_backward(
            value_array, latent_m, incoming, spatial_scale, spatial_shift, weights_t, count
        )
        weight = valid.astype(jnp.float32)
        current = pick(grads_out, index)
        grads_out = lax.dynamic_update_slice_in_dim(
            grads_out, jnp.where(valid, result, current), index, 0
        )
        return (
            result,
            grads_out,
            kernel_grad + weight * kernel_term,
            mod_grad + weight * mod_term,
            bias_grad + weight * bias_term,
        )

    initial = (
        jnp.zeros((1, row_count, col_count, channel_count), jnp.bfloat16),
        jnp.zeros_like(acts),
        jnp.zeros((9 * channel_count, channel_count), jnp.float32),
        jnp.zeros((mix_weight.shape[0], 2 * channel_count), jnp.float32),
        jnp.zeros((2 * channel_count,), jnp.float32),
    )
    final = lax.fori_loop(0, micro + segments - 1, tick, initial)
    grads_out = final[1][None]
    kernel_grad = final[2][None]
    mod_grad = final[3][None]
    bias_grad = final[4][None]
    kernel_grad, mod_grad, bias_grad = lax.psum((kernel_grad, mod_grad, bias_grad), ("rows", "sub"))
    return (grads_out, kernel_grad, mod_grad, bias_grad)


EXACT = lax.Precision.HIGHEST
TN = (((0,), (0,)), ((), ()))
NT = (((1,), (1,)), ((), ()))
F32 = jnp.float32
BF16 = jnp.bfloat16


def swap(value, axis):
    return lax.ppermute(value, axis, [(0, 1), (1, 0)])


def shift(value, axis, steps):
    count = lax.axis_size(axis)
    return lax.ppermute(value, axis, [(i, (i + steps) % count) for i in range(count)])


def pair(value, mask):
    count = lax.axis_size("rows")
    return lax.ppermute(value, "rows", [(i, i ^ mask) for i in range(count)])


def pixel_total(value):
    return rows_total(value + swap(value, "sub"))


def rows_total(value):
    one, two, three = [shift(value, "rows", steps) for steps in (1, 2, 3)]
    return (value + two) + (one + three)


def same_group(channels):
    per = channels // GROUPS
    left = lax.broadcasted_iota(jnp.int32, (channels, channels), 0) // per
    right = lax.broadcasted_iota(jnp.int32, (channels, channels), 1) // per
    return (left == right).astype(F32)


def statistics(sums_ref, micro, micros, count):
    member = same_group(sums_ref.shape[-1])
    both = jnp.concatenate([sums_ref[pl.ds(micro, 1), :], sums_ref[pl.ds(micros + micro, 1), :]], axis=0)
    both = jnp.dot(both, member, precision=EXACT, preferred_element_type=F32) / count
    mean = both[0:1]
    return mean, lax.rsqrt(both[1:2] - mean * mean + EPS)


def gradient_means(total, mix, count):
    mean_grad = jnp.sum(mix[:8] * total[8:], axis=0, keepdims=True)
    mean_cross = jnp.sum(mix[:8] * total[:8], axis=0, keepdims=True)
    both = jnp.concatenate([mean_grad, mean_cross], axis=0)
    both = jnp.dot(both, same_group(total.shape[-1]), precision=EXACT, preferred_element_type=F32) / count
    return both[0:1], both[1:2]


def side_by_side(mix):
    return jnp.concatenate([mix[:8], mix[8:]], axis=1).astype(BF16)


def sums_kernel(n, micro):
    micros = n.sums.shape[0] // 2
    value = n.acts[0].astype(F32)
    n.sums[pl.ds(micro, 1), :] = jnp.sum(value, axis=0, keepdims=True)
    n.sums[pl.ds(micros + micro, 1), :] = jnp.sum(value * value, axis=0, keepdims=True)


class Band:
    def __init__(self, n, micro, rows, cols, bands):
        self.n, self.rows, self.cols = n, rows, cols
        self.head = n.from_up.shape[0] - 16 * (n.from_up.shape[0] // 16)
        self.micro = micro
        self.side = lax.axis_index("sub")
        self.row_start = lax.axis_index("rows") * rows
        self.total_rows = rows * bands
        lane = lax.broadcasted_iota(jnp.int32, (1, cols), 1)
        crops = n.boxes.shape[1]
        tiles = self.total_rows // TILE * (2 * cols // TILE)
        self.boxes = []
        for k in range(crops):
            row, col, height, width = [n.boxes[micro, k, i] for i in range(4)]
            share = tiles / jnp.full((1, cols), crops * height * width, jnp.int32).astype(F32)
            inside = []
            for side in (self.side, 1 - self.side):
                at = lane + side * cols
                inside.append(jnp.where((at >= col * TILE) & (at < (col + width) * TILE), share, 0.0))
            self.boxes.append((row * TILE, (row + height) * TILE, inside[0], inside[1]))
        weight = n.out_weight[...].astype(F32)
        blank = jnp.zeros((8 - weight.shape[0], weight.shape[1]), F32)
        self.own = jnp.concatenate([jnp.concatenate([weight, blank])] * 3).astype(BF16)
        self.other = jnp.concatenate([jnp.concatenate([blank[:3], weight, blank[3:]])] * 3).astype(BF16)

    def border(self, ref, which):
        return ref[pl.ds(pl.multiple_of(self.head + 16 * self.micro + 8 * which, 8), 8), :]

    def planes(self, r):
        if r < 0:
            return self.border(self.n.from_up, r + 2)
        if r >= self.rows:
            return self.border(self.n.from_down, r - self.rows)
        own = self.n.recon[0, :, r, :].astype(F32) - self.n.target[0, :, r, :].astype(F32)
        beside = self.n.recon_beside[0, :, r, :].astype(F32) - self.n.target_beside[0, :, r, :].astype(F32)
        return jnp.concatenate([own, beside, jnp.zeros((2, self.cols), F32)])

    def latent(self, r):
        if r < 0 or r >= self.rows:
            ref = self.n.from_up if r < 0 else self.n.from_down
            value = jnp.concatenate([self.border(ref, 0)[6:8], self.border(ref, 1)[6:8]])
        else:
            value = self.n.latent[0, :, r, :].astype(F32)
        count = value.shape[0]
        return jnp.concatenate([value, jnp.ones((1, self.cols), F32), jnp.zeros((7 - count, self.cols), F32)]).astype(BF16)

    def row(self, r):
        diff = self.planes(r)
        at = self.row_start + r
        own = jnp.zeros((1, self.cols), F32)
        other = jnp.zeros((1, self.cols), F32)
        for first, end, own_share, other_share in self.boxes:
            here = (at >= first) & (at < end)
            own = own + jnp.where(here, own_share, 0.0)
            other = other + jnp.where(here, other_share, 0.0)
        plane = lax.broadcasted_iota(jnp.int32, (8, self.cols), 0)
        diff = 2.0 * diff * jnp.where(plane < 3, own, other)
        high = diff.astype(BF16).astype(F32)
        middle = (diff - high).astype(BF16).astype(F32)
        parts = jnp.concatenate([high, middle, diff - high - middle]).astype(BF16)
        value = lax.dot_general(parts, self.own, TN, preferred_element_type=F32).astype(BF16)
        beside = lax.dot_general(parts, self.other, TN, preferred_element_type=F32).astype(BF16).astype(F32)
        return value, jnp.where(self.side == 0, beside[0:1], beside[self.cols - 1 : self.cols])


def spread(index, cols, value, near, shifted):
    channels = value.shape[-1]
    side = lax.axis_index("sub")
    at = slice(index * cols, (index + 1) * cols)
    place = lax.broadcasted_iota(jnp.int32, (cols, channels), 0)
    wide = value.astype(F32)
    before = jnp.where(side == 1, near, 0.0)
    behind = jnp.where(side == 0, near, 0.0)
    shifted[at, 0:channels] = jnp.where(place == 0, before, pltpu.roll(wide, 1, 0)).astype(BF16)
    shifted[at, channels : 2 * channels] = value
    shifted[at, 2 * channels :] = jnp.where(place == cols - 1, behind, pltpu.roll(wide, cols - 1, 0)).astype(BF16)


def tap_of(row, col):
    return 3 * (2 - row) + (2 - col)


def arrange_weights(kernel_ref, weights):
    channels = kernel_ref.shape[-1]
    for row in range(3):
        for col in range(3):
            tap = tap_of(row, col)
            weights[row, :, col * channels : (col + 1) * channels] = kernel_ref[tap * channels : (tap + 1) * channels, :]


def hidden_gradient(rows, cols, shifted, weights, hidden_grad):
    pixels = rows * cols
    total = lax.dot_general(shifted[0:pixels, :], weights[0], NT, preferred_element_type=F32)
    total = total + lax.dot_general(shifted[cols : cols + pixels, :], weights[1], NT, preferred_element_type=F32)
    hidden_grad[0:pixels, :] = total + lax.dot_general(
        shifted[2 * cols : 2 * cols + pixels, :], weights[2], NT, preferred_element_type=F32
    )


def pixel_values(acts, latent, mix, mean, rstd):
    channels = mean.shape[-1]
    xhat = (acts.astype(F32) - mean) * rstd
    mixed = lax.dot_general(latent, mix, TN, preferred_element_type=F32)
    scale = mixed[:, :channels]
    pre = xhat * scale + mixed[:, channels:]
    sig = 0.5 * jnp.tanh(0.5 * pre) + 0.5
    hidden = pre * sig
    return xhat, scale, hidden, sig + hidden * (1.0 - sig)


def reduce_block(n, band, mean, rstd, mix, step, base=False):
    rows, cols = band.rows, band.cols
    channels = n.acts.shape[-1]
    hidden_gradient(rows, cols, n.shifted, n.weights, n.hidden_grad)
    for r in range(rows):
        at = slice(r * cols, (r + 1) * cols)
        latent = band.latent(r)
        n.latent_keep[:, at] = latent
        xhat, scale, hidden, slope = pixel_values(n.acts[0, at, :], latent, mix, mean, rstd)
        pre_grad = n.hidden_grad[at, :] * slope
        norm = pre_grad * scale
        if base:
            norm = n.shifted[(r + 1) * cols : (r + 2) * cols, channels : 2 * channels].astype(F32) + rstd * norm
            n.base[0, (r + 1) * cols : (r + 2) * cols, :] = norm.astype(BF16)
        else:
            n.norm[0, at, :] = norm.astype(BF16)
            n.hidden[at, :] = hidden.astype(BF16)
        n.pairs[at, 0:channels] = (pre_grad * xhat).astype(BF16)
        n.pairs[at, channels:] = pre_grad.astype(BF16)
    reduced = jnp.dot(n.latent_keep[...], n.pairs[...], preferred_element_type=F32)
    reduced = jnp.concatenate([reduced[:, :channels], reduced[:, channels:]])
    n.reduced[0] = reduced
    if not base:
        n.give[pl.ds(pl.multiple_of(n.keep.shape[0] + 16 * step, 8), 16), :] = reduced


def upper_kernel(rows, cols, bands, micros, count, n, step):
    active = lax.axis_index("segment") == 1

    @pl.when(active)
    def _():
        @pl.when(step == 0)
        def _():
            arrange_weights(n.kernel, n.weights)
            head = 2 * micros
            n.sums_keep[...] = (n.sums[...] + n.across[...]) + (n.from_up[0:head, :] + n.from_down[0:head, :])

        mean, rstd = statistics(n.sums_keep, step, micros, count)
        channels = mean.shape[-1]
        mix = [n.mod_weight[0].astype(F32), jnp.concatenate([n.scale_bias[...], n.shift_bias[...]], axis=1).astype(F32)]
        mix.append(jnp.zeros((7 - mix[0].shape[0], 2 * channels), F32))
        band = Band(n, step, rows, cols, bands)
        for r in range(rows + 2):
            spread(r, cols, *band.row(r - 1), n.shifted)
        reduce_block(n, band, mean, rstd, jnp.concatenate(mix).astype(BF16), step, base=True)

    @pl.when(jnp.logical_not(active))
    def _():
        @pl.when(step == 0)
        def _():
            arrange_weights(n.kernel_passed, n.weights)

        n.reduced[...] = jnp.zeros_like(n.reduced)
        band = Band(n, step, rows, cols, bands)
        for r in range(rows + 4):
            spread(r, cols, *band.row(r - 2), n.shifted)
        hidden_gradient(rows + 2, cols, n.shifted, n.weights, n.hidden_grad)
        n.base[0] = n.hidden_grad[...].astype(BF16)


def own_kernel(rows, cols, bands, micros, count, n, step):
    pixels = rows * cols
    side = lax.axis_index("sub")
    segment = lax.axis_index("segment")

    @pl.when(step == 0)
    def _():
        n.total[...] = jnp.zeros_like(n.total)

        @pl.when(segment == 0)
        def _():
            arrange_weights(n.kernel, n.weights)

    mean, rstd = statistics(n.sums, step, micros, count)
    band = Band(n, step, rows, cols, bands)
    mix = side_by_side(n.mix[...])

    @pl.when(segment == 1)
    def _():
        n.reduced[...] = jnp.zeros_like(n.reduced)
        n.give[pl.ds(pl.multiple_of(n.keep.shape[0] + 16 * step, 8), 16), :] = jnp.zeros_like(n.reduced[0])
        for r in range(rows + 2):
            spread(r, cols, *band.row(r - 1), n.shifted)
        for r in range(rows):
            at = slice(r * cols, (r + 1) * cols)
            n.hidden[at, :] = pixel_values(n.acts[0, at, :], band.latent(r), mix, mean, rstd)[2].astype(BF16)

    @pl.when(segment == 0)
    def _():
        near = n.near[0].astype(F32)
        for r in range(rows + 2):
            spread(r, cols, n.result[0, r * cols : (r + 1) * cols, :], near[r : r + 1], n.shifted)
        reduce_block(n, band, mean, rstd, mix, step)

    for row in range(3):
        n.total[row] += lax.dot_general(
            n.hidden[...], n.shifted[row * cols : row * cols + pixels, :], TN, preferred_element_type=F32
        )

    @pl.when(step == micros - 1)
    def _():
        half, channels = n.keep.shape
        for which in range(2):
            for ref, owner in ((n.keep, which), (n.give, 1 - which)):

                @pl.when(side == owner)
                def _(ref=ref, first=which * half):
                    for row in range(3):
                        for col in range(3):
                            at = tap_of(row, col) * channels - first
                            low, high = max(at, 0), min(at + channels, half)
                            if low < high:
                                ref[low:high, :] = n.total[row, low - at : high - at, col * channels : (col + 1) * channels]


def finish_kernel(rows, cols, bands, micros, count, n, step):
    channels = n.acts.shape[-1]
    segment = lax.axis_index("segment")
    side = lax.axis_index("sub")

    @pl.when(segment == 1)
    def _():
        mean, rstd = statistics(n.sums, step, micros, count)
        total = n.total[pl.ds(pl.multiple_of(16 * step, 8), 16), :]
        mean_grad, mean_cross = gradient_means(total, n.mix[...], count)
        for r in range(rows):
            at = slice((r + 1) * cols, (r + 2) * cols)
            xhat = (n.acts[0, r * cols : (r + 1) * cols, :].astype(F32) - mean) * rstd
            n.result[0, at, :] = (n.base[0, at, :].astype(F32) - rstd * (mean_grad + xhat * mean_cross)).astype(BF16)

    @pl.when(segment == 0)
    def _():
        mean, rstd = statistics(n.packed, step, micros, count)
        total = n.packed[pl.ds(pl.multiple_of(2 * micros + 16 * step, 8), 16), :]
        mix = n.packed[2 * micros + 16 * micros :, :]
        mean_grad, mean_cross = gradient_means(total, mix, count)
        wide_mix = side_by_side(mix)
        band = Band(n, step, rows, cols, bands)
        edges = []
        for r in range(rows + 2):
            at = slice(r * cols, (r + 1) * cols)
            if r == 0:
                acts = n.above[0]
            elif r == rows + 1:
                acts = n.below[0]
            elif r == 1 or r == rows:
                acts = n.outer[0, 0:cols, :] if r == 1 else n.outer[0, cols:, :]
            else:
                acts = n.inner[0, (r - 2) * cols : (r - 1) * cols, :]
            xhat, scale, _, slope = pixel_values(acts, band.latent(r - 1), wide_mix, mean, rstd)
            change = rstd * (n.base[0, at, :].astype(F32) * slope * scale - mean_grad - xhat * mean_cross)
            value = band.row(r - 1)[0].astype(F32) + change
            if r == 0 or r == rows + 1:
                row = band.row_start + (r - 1)
                value = jnp.where((row >= 0) & (row < band.total_rows), value, 0.0)
            n.result[0, at, :] = value.astype(BF16)
            edges.append(jnp.where(side == 0, value[cols - 1 : cols], value[0:1]))
        edges.append(jnp.zeros((16 - rows - 2, channels), F32))
        n.edge[0] = jnp.concatenate(edges).astype(BF16)


def last_kernel(rows, cols, micros, count, n, step):
    lower = lax.axis_index("segment") == 0

    @pl.when(step == 0)
    def _():
        latents, channels = n.mod_grad.shape[1], n.total_lower.shape[-1]
        total = jnp.zeros((16, channels), F32)
        for m in range(micros):
            at = slice(16 * m, 16 * (m + 1))
            total = total + jnp.where(lower, n.total_lower[at, :], n.total_upper[at, :])
        total = jnp.concatenate([total[:8], total[8:]], axis=1)
        n.mod_grad[0] = total[:latents]
        n.bias_grad[...] = total[latents : latents + 1]

    @pl.when(lower)
    def _():
        mean, rstd = statistics(n.sums, step, micros, count)
        total = n.total_lower[pl.ds(pl.multiple_of(16 * step, 8), 16), :]
        mean_grad, mean_cross = gradient_means(total, n.mix[...], count)
        for r in range(rows):
            at = slice(r * cols, (r + 1) * cols)
            xhat = (n.acts[0, at, :].astype(F32) - mean) * rstd
            change = rstd * (n.norm[0, at, :].astype(F32) - mean_grad - xhat * mean_cross)
            n.grads[0, at, :] = (n.result[0, (r + 1) * cols : (r + 2) * cols, :].astype(F32) + change).astype(BF16)

    @pl.when(jnp.logical_not(lower))
    def _():
        n.grads[0] = n.result[0, cols : (rows + 1) * cols, :]


def by_micro(value):
    rest = (0,) * (len(value.shape) - 1)
    return pl.BlockSpec((1,) + tuple(value.shape[1:]), lambda m: (m,) + rest)


def whole(value):
    return pl.BlockSpec(tuple(value.shape), lambda m: (0,) * len(value.shape))


def call(kernel, name, micros, scalars, fixed, cut, outs, fixed_outs, scratch, work=4, room=16):
    names = [*scalars, *fixed, *cut, *outs, *fixed_outs, *scratch]
    cut_shape = [jax.ShapeDtypeStruct(s, d) for s, d in outs.values()]
    fixed_shape = [jax.ShapeDtypeStruct(s, d) for s, d in fixed_outs.values()]

    def body(*refs):
        kernel(types.SimpleNamespace(**dict(zip(names, refs))), pl.program_id(0))

    return pl.pallas_call(
        body,
        grid=(micros,),
        in_specs=[pl.BlockSpec(memory_space=pltpu.SMEM) for _ in scalars]
        + [whole(v) for v in fixed.values()]
        + [by_micro(v) for v in cut.values()],
        out_specs=[by_micro(s) for s in cut_shape] + [whole(s) for s in fixed_shape],
        out_shape=cut_shape + fixed_shape,
        scratch_shapes=[pltpu.VMEM(s, d) for s, d in scratch.values()],
        compiler_params=pltpu.CompilerParams(vmem_limit_bytes=room * 1024 * 1024),
        cost_estimate=pl.CostEstimate(flops=work, bytes_accessed=work // 4, transcendentals=0),
        name=name,
    )(*scalars.values(), *fixed.values(), *cut.values())


def pair_body(
    activations, latent, recon, target, boxes, kernel, mod_weight, scale_bias, shift_bias, out_weight
):
    micros, rows, cols, channels = activations.shape[1:]
    latents = latent.shape[1]
    pixels = rows * cols
    bands = lax.axis_size("rows")
    count = float(pixels * bands * 2 * (channels // GROUPS))
    segment = lax.axis_index("segment")
    side = lax.axis_index("sub")
    acts = activations[0].reshape(micros, pixels, channels)

    outer = swap(jnp.concatenate([acts[:, :cols], acts[:, pixels - cols :]], axis=1), "segment")
    inner = swap(acts[:, cols : pixels - cols], "segment")
    kernel_passed = swap(kernel[0], "segment")
    recon_beside, target_beside = swap(recon, "sub"), swap(target, "sub")

    (sums,) = call(sums_kernel, "input_sums", micros, {}, {}, {"acts": acts}, {}, {"sums": ((2 * micros, channels), F32)}, {})
    sums = sums + swap(sums, "sub")

    def border(first, r):
        def difference(one, two):
            part = slice(first, first + 2)
            return (one[:, :, part].astype(F32) - two[:, :, part].astype(F32)).transpose(0, 2, 1, 3)

        extra = latent[:, :, r].astype(F32).reshape(micros, 2, latents // 2, cols)
        two = jnp.concatenate([difference(recon, target), difference(recon_beside, target_beside), extra], axis=2)
        return jnp.concatenate([sums, two.reshape(micros * 16, cols)])

    from_up = shift(border(rows - 2, rows - 1), "rows", 1)
    from_down = shift(border(0, 0), "rows", bands - 1)
    across = shift(sums, "rows", 2)

    from_up, kernel_passed = lax.optimization_barrier((from_up, kernel_passed))
    image = {
        "latent": latent,
        "recon": recon,
        "target": target,
        "recon_beside": recon_beside,
        "target_beside": target_beside,
    }
    borders = {"from_up": from_up, "from_down": from_down, "out_weight": out_weight}
    wide = (rows + 2) * cols
    triple = 3 * channels
    shifted = {"shifted": ((wide, triple), BF16)}
    work = {
        **shifted,
        "weights": ((3, channels, triple), BF16),
        "hidden_grad": ((pixels, channels), F32),
        "latent_keep": ((8, pixels), BF16),
        "pairs": ((pixels, 2 * channels), BF16),
    }
    size = (rows, cols, bands, micros, count)
    sums_own = (sums + across) + (from_up[: 2 * micros] + from_down[: 2 * micros])
    mix = jnp.concatenate([mod_weight[0], jnp.concatenate([scale_bias, shift_bias], axis=1)]).astype(F32)
    mix = jnp.pad(mix, ((0, 7 - latents), (0, 0)))
    mix = jnp.concatenate([mix[:, :channels], mix[:, channels:]])
    base, reduced = call(
        functools.partial(upper_kernel, *size),
        "upper_block",
        micros,
        {"boxes": boxes},
        {
            "sums": sums,
            "across": across,
            "mod_weight": mod_weight,
            "scale_bias": scale_bias,
            "shift_bias": shift_bias,
            "kernel": kernel[0],
            "kernel_passed": kernel_passed,
            **borders,
        },
        {"acts": acts, **image},
        {"base": ((micros, wide, channels), BF16), "reduced": ((micros, 16, channels), F32)},
        {},
        {
            **work,
            "shifted": (((rows + 4) * cols, triple), BF16),
            "hidden_grad": ((wide, channels), F32),
            "sums_keep": ((2 * micros, channels), F32),
        },
    )
    sums = sums_own
    reduced, outer = lax.optimization_barrier((reduced, outer))
    above = shift(outer[:, cols:], "rows", 1)
    below = shift(outer[:, :cols], "rows", bands - 1)
    total_upper = pixel_total(reduced.reshape(micros * 16, channels))
    packed = jnp.concatenate([sums, total_upper, mix])
    packed, inner, above = lax.optimization_barrier((packed, inner, above))
    packed = swap(packed, "segment")
    result, edge = call(
        functools.partial(finish_kernel, *size),
        "finish_upper",
        micros,
        {"boxes": boxes},
        {"sums": sums, "mix": mix, "packed": packed, "total": total_upper, **borders},
        {
            "base": base,
            "acts": acts,
            "outer": outer,
            "inner": inner,
            "above": above,
            "below": below,
            **image,
        },
        {"result": ((micros, wide, channels), BF16), "edge": ((micros, 16, channels), BF16)},
        {},
        {},
    )
    near = swap(edge, "sub")
    half = kernel.shape[1] // 2
    norm, reduced, keep, give = call(
        functools.partial(own_kernel, *size),
        "own_block",
        micros,
        {"boxes": boxes},
        {"sums": sums, "mix": mix, "kernel": kernel[0], **borders},
        {"result": result, "near": near, "acts": acts, **image},
        {"norm": ((micros, pixels, channels), BF16), "reduced": ((micros, 16, channels), F32)},
        {"keep": ((half, channels), F32), "give": ((half + micros * 16, channels), F32)},
        {**work, "hidden": ((pixels, channels), BF16), "total": ((3, channels, triple), F32)},
    )
    got = swap(give, "sub")
    keep = (keep + got[:half]).astype(BF16)
    keep = (keep.astype(F32) + pair(keep, 1).astype(F32)).astype(BF16)
    other_pair = pair(keep, 2)
    total_lower = rows_total(reduced.reshape(micros * 16, channels) + got[half:])
    grads, mod_grad, bias_grad = call(
        functools.partial(last_kernel, rows, cols, micros, count),
        "input_gradient",
        micros,
        {},
        {"sums": sums, "mix": mix, "total_lower": total_lower, "total_upper": total_upper},
        {"acts": acts, "norm": norm, "result": result},
        {"grads": ((micros, pixels, channels), BF16)},
        {"mod_grad": ((1, latents, 2 * channels), F32), "bias_grad": ((1, 2 * channels), F32)},
        {},
        work=1 << 25,
    )
    grads, other_pair = lax.optimization_barrier((grads, other_pair))
    keep = keep.astype(F32) + other_pair.astype(F32)
    give = swap(keep, "sub")
    kernel_grad = jnp.where(side == 0, jnp.concatenate([keep, give]), jnp.concatenate([give, keep]))
    return (grads.reshape(activations.shape), kernel_grad[None], mod_grad, bias_grad)


def solution(mesh):
    pair = mesh.shape["segment"] == 2 and mesh.shape["rows"] == 4 and mesh.shape["sub"] == 2
    body = pair_body if pair else general_body
    placed = (
        P("segment", "groups", "rows", "sub", None),
        P("groups", None, "rows", "sub"),
        P("groups", None, "rows", "sub"),
        P("groups", None, "rows", "sub"),
        P("groups", None, None),
        P("segment", None, None),
        P("segment", None, None),
        P("segment", None),
        P("segment", None),
        P(),
    )
    return jax.shard_map(
        body,
        mesh=mesh,
        in_specs=placed,
        out_specs=(
            P("segment", "groups", "rows", "sub", None),
            P("segment", "groups", None),
            P("segment", "groups", None),
            P("segment", "groups"),
        ),
        check_vma=False,
    )
```

```python
import functools
import types

import jax
import jax.numpy as jnp
from jax import lax
from jax.experimental import pallas as pl
from jax.experimental.pallas import tpu as pltpu
from jax.sharding import PartitionSpec as P

GROUPS = 32
TILE = 32


EPS = 1e-06


def extended(block, sides, width):
    for axis, dim in sides:
        count = lax.axis_size(axis)
        forward = [(i, i + 1) for i in range(count - 1)]
        backward = [(target, source) for source, target in forward]
        low = lax.ppermute(
            lax.slice_in_dim(block, block.shape[dim] - width, None, axis=dim), axis, forward
        )
        high = lax.ppermute(lax.slice_in_dim(block, 0, width, axis=dim), axis, backward)
        block = jnp.concatenate([low, block, high], axis=dim)
    return block


def from_behind(value, axis, steps):
    count = lax.axis_size(axis)
    initial, last = (max(0, -steps), min(count, count - steps))
    return lax.ppermute(value, axis, [(source, source + steps) for source in range(initial, last)])


def crop_weights(boxes, row_start, col_start, row_count, col_count, total_rows, total_cols):
    row_tile = (row_start + jnp.arange(row_count, dtype=jnp.int32)) // TILE
    col_tile = (col_start + jnp.arange(col_count, dtype=jnp.int32)) // TILE
    first_row = boxes[:, :, 0:1]
    first_col = boxes[:, :, 1:2]
    box_height = boxes[:, :, 2:3]
    box_width = boxes[:, :, 3:4]
    in_rows = ((row_tile >= first_row) & (row_tile < first_row + box_height)).astype(jnp.float32)
    in_cols = ((col_tile >= first_col) & (col_tile < first_col + box_width)).astype(jnp.float32)
    tiles = total_rows // TILE * (total_cols // TILE)
    share = tiles / (boxes.shape[1] * (box_height * box_width).astype(jnp.float32))
    return jnp.einsum("mkr,mkc->mrc", in_rows * share, in_cols)


def top_gradient(recon, target, cropped, out_weight):
    diff = 2.0 * (recon.astype(jnp.float32) - target.astype(jnp.float32)) * cropped[:, None]
    return jnp.einsum("mkhw,kc->mhwc", diff, out_weight.astype(jnp.float32)).astype(jnp.bfloat16)


def loss_gradient(
    boxes,
    recon,
    target,
    out_weight,
    row_start,
    col_start,
    row_count,
    col_count,
    total_rows,
    total_cols,
):
    cropped = crop_weights(
        boxes, row_start, col_start, row_count, col_count, total_rows, total_cols
    )
    return top_gradient(recon, target, cropped, out_weight)


def grouped_layout(value_array):
    return value_array.reshape(value_array.shape[:-1] + (GROUPS, value_array.shape[-1] // GROUPS))


def group_sums(value_array):
    shaped = grouped_layout(value_array)
    return (jnp.sum(shaped, axis=(-4, -3, -1)), jnp.sum(shaped * shaped, axis=(-4, -3, -1)))


def expand(stat):
    return stat[..., None, None, :, None]


def normalized_values(value_array, mean_val, rstd_val):
    shaped = grouped_layout(value_array)
    return ((shaped - expand(mean_val)) * expand(rstd_val)).reshape(value_array.shape)


def modulation(latent_batch, mix_weight, scale_row, shift_row):
    channel_count = scale_row.shape[-1]
    coefficients = jnp.einsum(
        "bzhw,zc->bhwc", latent_batch.astype(jnp.float32), mix_weight.astype(jnp.float32)
    )
    return (
        coefficients[..., :channel_count] + scale_row.astype(jnp.float32),
        coefficients[..., channel_count:] + shift_row.astype(jnp.float32),
    )


def transposed(weights):
    channel_count = weights.shape[-1]
    return (
        weights.reshape(9, channel_count, channel_count)
        .transpose(0, 2, 1)
        .reshape(9 * channel_count, channel_count)
    )


def taps(padded, row_count, col_count, flipped):
    pieces = []
    for tap_row in range(3):
        for tap_col in range(3):
            if flipped:
                row_offset, col_offset = (2 - tap_row, 2 - tap_col)
            else:
                row_offset, col_offset = (tap_row, tap_col)
            pieces.append(
                padded[:, row_offset : row_offset + row_count, col_offset : col_offset + col_count]
            )
    return jnp.concatenate(pieces, axis=-1).reshape(-1, 9 * padded.shape[-1])


def pick(value_array, index):
    return lax.dynamic_slice_in_dim(value_array, index, 1, 0)


def section_backward(
    value_array, latent_batch, incoming, spatial_scale, spatial_shift, weights_t, count
):
    batch, row_count, col_count, channel_count = value_array.shape
    sum_one, sum_two = group_sums(value_array)
    sum_one, sum_two = lax.psum((sum_one, sum_two), ("rows", "sub"))
    group_mean = sum_one / count
    inverse_deviation = lax.rsqrt(sum_two / count - group_mean * group_mean + EPS)
    centered_scaled = normalized_values(value_array, group_mean, inverse_deviation)
    pre_activation = centered_scaled * spatial_scale + spatial_shift
    hidden = jax.nn.silu(pre_activation).astype(jnp.bfloat16)
    padded_h = extended(hidden, (("rows", 1), ("sub", 2)), 1)
    padded_g = extended(incoming, (("rows", 1), ("sub", 2)), 1)
    patches = taps(padded_h, row_count, col_count, False)
    kernel_term = lax.dot_general(
        patches,
        incoming.reshape(-1, channel_count),
        (((0,), (0,)), ((), ())),
        preferred_element_type=jnp.float32,
    )
    hidden_grad = jnp.dot(
        taps(padded_g, row_count, col_count, True), weights_t, preferred_element_type=jnp.float32
    ).reshape(value_array.shape)
    sig = jax.nn.sigmoid(pre_activation)
    pre_activation_gradient = hidden_grad * (sig * (1.0 + pre_activation * (1.0 - sig)))
    paired_parts = jnp.concatenate(
        [pre_activation_gradient * centered_scaled, pre_activation_gradient], axis=-1
    )
    mod_term = jnp.einsum("bzhw,bhwc->zc", latent_batch.astype(jnp.float32), paired_parts)
    bias_term = jnp.sum(paired_parts, axis=(0, 1, 2))
    shaped_grad = grouped_layout(pre_activation_gradient * spatial_scale)
    reshaped_normalized = grouped_layout(centered_scaled)
    part_one = jnp.sum(shaped_grad, axis=(1, 2, 4))
    part_two = jnp.sum(shaped_grad * reshaped_normalized, axis=(1, 2, 4))
    part_one, part_two = lax.psum((part_one, part_two), ("rows", "sub"))
    mean_grad = part_one / count
    mean_cross = part_two / count
    adjust = expand(inverse_deviation) * (
        shaped_grad - expand(mean_grad) - reshaped_normalized * expand(mean_cross)
    )
    result = (incoming.astype(jnp.float32) + adjust.reshape(value_array.shape)).astype(jnp.bfloat16)
    return (result, kernel_term, mod_term, bias_term)


def general_body(
    activations,
    latent,
    recon,
    target,
    boxes,
    kernel,
    mod_weight,
    scale_bias,
    shift_bias,
    out_weight,
):
    segments = lax.axis_size("segment")
    segment_index = lax.axis_index("segment")
    micro, row_count, col_count, channel_count = activations.shape[1:]
    total_rows = row_count * lax.axis_size("rows")
    total_cols = col_count * lax.axis_size("sub")
    count = total_rows * total_cols * (channel_count // GROUPS)
    row_start = lax.axis_index("rows") * row_count
    col_start = lax.axis_index("sub") * col_count
    acts = activations[0]
    weights_t = transposed(kernel[0])
    mix_weight = mod_weight[0]
    scale_row = scale_bias[0]
    shift_row = shift_bias[0]
    top = loss_gradient(
        boxes,
        recon,
        target,
        out_weight,
        row_start,
        col_start,
        row_count,
        col_count,
        total_rows,
        total_cols,
    )

    def tick(step, carry):
        passing, grads_out, kernel_grad, mod_grad, bias_grad = carry
        offset = step - (segments - 1 - segment_index)
        valid = (offset >= 0) & (offset < micro)
        index = jnp.clip(offset, 0, micro - 1)
        received = from_behind(passing, "segment", -1)
        incoming = jnp.where(segment_index == segments - 1, pick(top, index), received)
        value_array = pick(acts, index).astype(jnp.float32)
        latent_m = pick(latent, index)
        spatial_scale, spatial_shift = modulation(latent_m, mix_weight, scale_row, shift_row)
        result, kernel_term, mod_term, bias_term = section_backward(
            value_array, latent_m, incoming, spatial_scale, spatial_shift, weights_t, count
        )
        weight = valid.astype(jnp.float32)
        current = pick(grads_out, index)
        grads_out = lax.dynamic_update_slice_in_dim(
            grads_out, jnp.where(valid, result, current), index, 0
        )
        return (
            result,
            grads_out,
            kernel_grad + weight * kernel_term,
            mod_grad + weight * mod_term,
            bias_grad + weight * bias_term,
        )

    initial = (
        jnp.zeros((1, row_count, col_count, channel_count), jnp.bfloat16),
        jnp.zeros_like(acts),
        jnp.zeros((9 * channel_count, channel_count), jnp.float32),
        jnp.zeros((mix_weight.shape[0], 2 * channel_count), jnp.float32),
        jnp.zeros((2 * channel_count,), jnp.float32),
    )
    final = lax.fori_loop(0, micro + segments - 1, tick, initial)
    grads_out = final[1][None]
    kernel_grad = final[2][None]
    mod_grad = final[3][None]
    bias_grad = final[4][None]
    kernel_grad, mod_grad, bias_grad = lax.psum((kernel_grad, mod_grad, bias_grad), ("rows", "sub"))
    return (grads_out, kernel_grad, mod_grad, bias_grad)


EXACT = lax.Precision.HIGHEST
TN = (((0,), (0,)), ((), ()))
NT = (((1,), (1,)), ((), ()))
F32 = jnp.float32
BF16 = jnp.bfloat16


def swap(value, axis):
    return lax.ppermute(value, axis, [(0, 1), (1, 0)])


def shift(value, axis, steps):
    count = lax.axis_size(axis)
    return lax.ppermute(value, axis, [(i, (i + steps) % count) for i in range(count)])


def pair(value, mask):
    count = lax.axis_size("rows")
    return lax.ppermute(value, "rows", [(i, i ^ mask) for i in range(count)])


def pixel_total(value):
    return rows_total(value + swap(value, "sub"))


def rows_total(value):
    one, two, three = [shift(value, "rows", steps) for steps in (1, 2, 3)]
    return (value + two) + (one + three)


def same_group(channels):
    per = channels // GROUPS
    left = lax.broadcasted_iota(jnp.int32, (channels, channels), 0) // per
    right = lax.broadcasted_iota(jnp.int32, (channels, channels), 1) // per
    return (left == right).astype(F32)


def statistics(sums_ref, micro, micros, count):
    member = same_group(sums_ref.shape[-1])
    both = jnp.concatenate([sums_ref[pl.ds(micro, 1), :], sums_ref[pl.ds(micros + micro, 1), :]], axis=0)
    both = jnp.dot(both, member, precision=EXACT, preferred_element_type=F32) / count
    mean = both[0:1]
    return mean, lax.rsqrt(both[1:2] - mean * mean + EPS)


def gradient_means(total, mix, count):
    mean_grad = jnp.sum(mix[:8] * total[8:], axis=0, keepdims=True)
    mean_cross = jnp.sum(mix[:8] * total[:8], axis=0, keepdims=True)
    both = jnp.concatenate([mean_grad, mean_cross], axis=0)
    both = jnp.dot(both, same_group(total.shape[-1]), precision=EXACT, preferred_element_type=F32) / count
    return both[0:1], both[1:2]


def side_by_side(mix):
    return jnp.concatenate([mix[:8], mix[8:]], axis=1).astype(BF16)


def sums_kernel(n, micro):
    micros = n.sums.shape[0] // 2
    value = n.acts[0].astype(F32)
    n.sums[pl.ds(micro, 1), :] = jnp.sum(value, axis=0, keepdims=True)
    n.sums[pl.ds(micros + micro, 1), :] = jnp.sum(value * value, axis=0, keepdims=True)


class Band:
    def __init__(self, n, micro, rows, cols, bands):
        self.n, self.rows, self.cols = n, rows, cols
        self.head = n.from_up.shape[0] - 16 * (n.from_up.shape[0] // 16)
        self.micro = micro
        self.side = lax.axis_index("sub")
        self.row_start = lax.axis_index("rows") * rows
        self.total_rows = rows * bands
        lane = lax.broadcasted_iota(jnp.int32, (1, cols), 1)
        crops = n.boxes.shape[1]
        tiles = self.total_rows // TILE * (2 * cols // TILE)
        self.boxes = []
        for k in range(crops):
            row, col, height, width = [n.boxes[micro, k, i] for i in range(4)]
            share = tiles / jnp.full((1, cols), crops * height * width, jnp.int32).astype(F32)
            inside = []
            for side in (self.side, 1 - self.side):
                at = lane + side * cols
                inside.append(jnp.where((at >= col * TILE) & (at < (col + width) * TILE), share, 0.0))
            self.boxes.append((row * TILE, (row + height) * TILE, inside[0], inside[1]))
        weight = n.out_weight[...].astype(F32)
        blank = jnp.zeros((8 - weight.shape[0], weight.shape[1]), F32)
        self.own = jnp.concatenate([jnp.concatenate([weight, blank])] * 3).astype(BF16)
        self.other = jnp.concatenate([jnp.concatenate([blank[:3], weight, blank[3:]])] * 3).astype(BF16)

    def border(self, ref, which):
        return ref[pl.ds(pl.multiple_of(self.head + 16 * self.micro + 8 * which, 8), 8), :]

    def planes(self, r):
        if r < 0:
            return self.border(self.n.from_up, r + 2)
        if r >= self.rows:
            return self.border(self.n.from_down, r - self.rows)
        own = self.n.recon[0, :, r, :].astype(F32) - self.n.target[0, :, r, :].astype(F32)
        beside = self.n.recon_beside[0, :, r, :].astype(F32) - self.n.target_beside[0, :, r, :].astype(F32)
        return jnp.concatenate([own, beside, jnp.zeros((2, self.cols), F32)])

    def latent(self, r):
        if r < 0 or r >= self.rows:
            ref = self.n.from_up if r < 0 else self.n.from_down
            value = jnp.concatenate([self.border(ref, 0)[6:8], self.border(ref, 1)[6:8]])
        else:
            value = self.n.latent[0, :, r, :].astype(F32)
        count = value.shape[0]
        return jnp.concatenate([value, jnp.ones((1, self.cols), F32), jnp.zeros((7 - count, self.cols), F32)]).astype(BF16)

    def row(self, r):
        diff = self.planes(r)
        at = self.row_start + r
        own = jnp.zeros((1, self.cols), F32)
        other = jnp.zeros((1, self.cols), F32)
        for first, end, own_share, other_share in self.boxes:
            here = (at >= first) & (at < end)
            own = own + jnp.where(here, own_share, 0.0)
            other = other + jnp.where(here, other_share, 0.0)
        plane = lax.broadcasted_iota(jnp.int32, (8, self.cols), 0)
        diff = 2.0 * diff * jnp.where(plane < 3, own, other)
        high = diff.astype(BF16).astype(F32)
        middle = (diff - high).astype(BF16).astype(F32)
        parts = jnp.concatenate([high, middle, diff - high - middle]).astype(BF16)
        value = lax.dot_general(parts, self.own, TN, preferred_element_type=F32).astype(BF16)
        beside = lax.dot_general(parts, self.other, TN, preferred_element_type=F32).astype(BF16).astype(F32)
        return value, jnp.where(self.side == 0, beside[0:1], beside[self.cols - 1 : self.cols])


def spread(index, cols, value, near, shifted):
    channels = value.shape[-1]
    side = lax.axis_index("sub")
    at = slice(index * cols, (index + 1) * cols)
    place = lax.broadcasted_iota(jnp.int32, (cols, channels), 0)
    wide = value.astype(F32)
    before = jnp.where(side == 1, near, 0.0)
    behind = jnp.where(side == 0, near, 0.0)
    shifted[at, 0:channels] = jnp.where(place == 0, before, pltpu.roll(wide, 1, 0)).astype(BF16)
    shifted[at, channels : 2 * channels] = value
    shifted[at, 2 * channels :] = jnp.where(place == cols - 1, behind, pltpu.roll(wide, cols - 1, 0)).astype(BF16)


def tap_of(row, col):
    return 3 * (2 - row) + (2 - col)


def arrange_weights(kernel_ref, weights):
    channels = kernel_ref.shape[-1]
    for row in range(3):
        for col in range(3):
            tap = tap_of(row, col)
            for at in range(2):
                weights[row + at, at * channels : (at + 1) * channels, col * channels : (col + 1) * channels] = kernel_ref[
                    tap * channels : (tap + 1) * channels, :
                ]
    for at in range(2):
        unused = weights[3 * (1 - at), at * channels : (at + 1) * channels, :]
        weights[3 * (1 - at), at * channels : (at + 1) * channels, :] = jnp.zeros_like(unused)


def hidden_gradient(rows, cols, shifted, weights, hidden_grad):
    channels = hidden_grad.shape[-1]
    total = None
    for k in range(4):
        left = jnp.concatenate([shifted[(r + k) * cols : (r + k + 1) * cols, :] for r in range(0, rows, 2)])
        part = lax.dot_general(left, weights[k], NT, preferred_element_type=F32)
        total = part if total is None else total + part
    for r in range(rows):
        half = (r % 2) * channels
        hidden_grad[r * cols : (r + 1) * cols, :] = total[r // 2 * cols : (r // 2 + 1) * cols, half : half + channels]


def pixel_values(acts, latent, mix, mean, rstd):
    channels = mean.shape[-1]
    xhat = (acts.astype(F32) - mean) * rstd
    mixed = lax.dot_general(latent, mix, TN, preferred_element_type=F32)
    scale = mixed[:, :channels]
    pre = xhat * scale + mixed[:, channels:]
    sig = 0.5 * jnp.tanh(0.5 * pre) + 0.5
    hidden = pre * sig
    return xhat, scale, hidden, sig + hidden * (1.0 - sig)


def reduce_block(n, band, mean, rstd, mix, step, base=False):
    rows, cols = band.rows, band.cols
    channels = n.acts.shape[-1]
    hidden_gradient(rows, cols, n.shifted, n.weights, n.hidden_grad)
    for r in range(rows):
        at = slice(r * cols, (r + 1) * cols)
        latent = band.latent(r)
        n.latent_keep[:, at] = latent
        xhat, scale, hidden, slope = pixel_values(n.acts[0, at, :], latent, mix, mean, rstd)
        pre_grad = n.hidden_grad[at, :] * slope
        norm = pre_grad * scale
        if base:
            norm = n.shifted[(r + 1) * cols : (r + 2) * cols, channels : 2 * channels].astype(F32) + rstd * norm
            n.base[0, (r + 1) * cols : (r + 2) * cols, :] = norm.astype(BF16)
        else:
            n.norm[0, at, :] = norm.astype(BF16)
            n.hidden[at, :] = hidden.astype(BF16)
        n.pairs[at, 0:channels] = (pre_grad * xhat).astype(BF16)
        n.pairs[at, channels:] = pre_grad.astype(BF16)
    reduced = jnp.dot(n.latent_keep[...], n.pairs[...], preferred_element_type=F32)
    reduced = jnp.concatenate([reduced[:, :channels], reduced[:, channels:]])
    n.reduced[0] = reduced
    if not base:
        n.give[pl.ds(pl.multiple_of(n.keep.shape[0] + 16 * step, 8), 16), :] = reduced


def upper_kernel(rows, cols, bands, micros, count, n, step):
    active = lax.axis_index("segment") == 1

    @pl.when(active)
    def _():
        @pl.when(step == 0)
        def _():
            arrange_weights(n.kernel, n.weights)
            head = 2 * micros
            n.sums_keep[...] = (n.sums[...] + n.across[...]) + (n.from_up[0:head, :] + n.from_down[0:head, :])

        mean, rstd = statistics(n.sums_keep, step, micros, count)
        channels = mean.shape[-1]
        mix = [n.mod_weight[0].astype(F32), jnp.concatenate([n.scale_bias[...], n.shift_bias[...]], axis=1).astype(F32)]
        mix.append(jnp.zeros((7 - mix[0].shape[0], 2 * channels), F32))
        band = Band(n, step, rows, cols, bands)
        for r in range(rows + 2):
            spread(r, cols, *band.row(r - 1), n.shifted)
        reduce_block(n, band, mean, rstd, jnp.concatenate(mix).astype(BF16), step, base=True)

    @pl.when(jnp.logical_not(active))
    def _():
        @pl.when(step == 0)
        def _():
            arrange_weights(n.kernel_passed, n.weights)

        n.reduced[...] = jnp.zeros_like(n.reduced)
        band = Band(n, step, rows, cols, bands)
        for r in range(rows + 4):
            spread(r, cols, *band.row(r - 2), n.shifted)
        hidden_gradient(rows + 2, cols, n.shifted, n.weights, n.hidden_grad)
        n.base[0] = n.hidden_grad[...].astype(BF16)


def own_kernel(rows, cols, bands, micros, count, n, step):
    pixels = rows * cols
    side = lax.axis_index("sub")
    segment = lax.axis_index("segment")

    @pl.when(step == 0)
    def _():
        n.total[...] = jnp.zeros_like(n.total)

        @pl.when(segment == 0)
        def _():
            arrange_weights(n.kernel, n.weights)

    mean, rstd = statistics(n.sums, step, micros, count)
    band = Band(n, step, rows, cols, bands)
    mix = side_by_side(n.mix[...])

    @pl.when(segment == 1)
    def _():
        n.reduced[...] = jnp.zeros_like(n.reduced)
        n.give[pl.ds(pl.multiple_of(n.keep.shape[0] + 16 * step, 8), 16), :] = jnp.zeros_like(n.reduced[0])
        for r in range(rows + 2):
            spread(r, cols, *band.row(r - 1), n.shifted)
        for r in range(rows):
            at = slice(r * cols, (r + 1) * cols)
            n.hidden[at, :] = pixel_values(n.acts[0, at, :], band.latent(r), mix, mean, rstd)[2].astype(BF16)

    @pl.when(segment == 0)
    def _():
        near = n.near[0].astype(F32)
        for r in range(rows + 2):
            spread(r, cols, n.result[0, r * cols : (r + 1) * cols, :], near[r : r + 1], n.shifted)
        reduce_block(n, band, mean, rstd, mix, step)

    for row in range(3):
        n.total[row] += lax.dot_general(
            n.hidden[...], n.shifted[row * cols : row * cols + pixels, :], TN, preferred_element_type=F32
        )

    @pl.when(step == micros - 1)
    def _():
        half, channels = n.keep.shape
        for which in range(2):
            for ref, owner in ((n.keep, which), (n.give, 1 - which)):

                @pl.when(side == owner)
                def _(ref=ref, first=which * half):
                    for row in range(3):
                        for col in range(3):
                            at = tap_of(row, col) * channels - first
                            low, high = max(at, 0), min(at + channels, half)
                            if low < high:
                                ref[low:high, :] = n.total[row, low - at : high - at, col * channels : (col + 1) * channels]


def finish_kernel(rows, cols, bands, micros, count, n, step):
    channels = n.acts.shape[-1]
    segment = lax.axis_index("segment")
    side = lax.axis_index("sub")

    @pl.when(segment == 1)
    def _():
        mean, rstd = statistics(n.sums, step, micros, count)
        total = n.total[pl.ds(pl.multiple_of(16 * step, 8), 16), :]
        mean_grad, mean_cross = gradient_means(total, n.mix[...], count)
        for r in range(rows):
            at = slice((r + 1) * cols, (r + 2) * cols)
            xhat = (n.acts[0, r * cols : (r + 1) * cols, :].astype(F32) - mean) * rstd
            n.result[0, at, :] = (n.base[0, at, :].astype(F32) - rstd * (mean_grad + xhat * mean_cross)).astype(BF16)

    @pl.when(segment == 0)
    def _():
        mean, rstd = statistics(n.packed, step, micros, count)
        total = n.packed[pl.ds(pl.multiple_of(2 * micros + 16 * step, 8), 16), :]
        mix = n.packed[2 * micros + 16 * micros :, :]
        mean_grad, mean_cross = gradient_means(total, mix, count)
        wide_mix = side_by_side(mix)
        band = Band(n, step, rows, cols, bands)
        edges = []
        for r in range(rows + 2):
            at = slice(r * cols, (r + 1) * cols)
            if r == 0:
                acts = n.above[0]
            elif r == rows + 1:
                acts = n.below[0]
            elif r == 1 or r == rows:
                acts = n.outer[0, 0:cols, :] if r == 1 else n.outer[0, cols:, :]
            else:
                acts = n.inner[0, (r - 2) * cols : (r - 1) * cols, :]
            xhat, scale, _, slope = pixel_values(acts, band.latent(r - 1), wide_mix, mean, rstd)
            change = rstd * (n.base[0, at, :].astype(F32) * slope * scale - mean_grad - xhat * mean_cross)
            value = band.row(r - 1)[0].astype(F32) + change
            if r == 0 or r == rows + 1:
                row = band.row_start + (r - 1)
                value = jnp.where((row >= 0) & (row < band.total_rows), value, 0.0)
            n.result[0, at, :] = value.astype(BF16)
            edges.append(jnp.where(side == 0, value[cols - 1 : cols], value[0:1]))
        edges.append(jnp.zeros((16 - rows - 2, channels), F32))
        n.edge[0] = jnp.concatenate(edges).astype(BF16)


def last_kernel(rows, cols, micros, count, n, step):
    lower = lax.axis_index("segment") == 0

    @pl.when(step == 0)
    def _():
        latents, channels = n.mod_grad.shape[1], n.total_lower.shape[-1]
        total = jnp.zeros((16, channels), F32)
        for m in range(micros):
            at = slice(16 * m, 16 * (m + 1))
            total = total + jnp.where(lower, n.total_lower[at, :], n.total_upper[at, :])
        total = jnp.concatenate([total[:8], total[8:]], axis=1)
        n.mod_grad[0] = total[:latents]
        n.bias_grad[...] = total[latents : latents + 1]

    @pl.when(lower)
    def _():
        mean, rstd = statistics(n.sums, step, micros, count)
        total = n.total_lower[pl.ds(pl.multiple_of(16 * step, 8), 16), :]
        mean_grad, mean_cross = gradient_means(total, n.mix[...], count)
        for r in range(rows):
            at = slice(r * cols, (r + 1) * cols)
            xhat = (n.acts[0, at, :].astype(F32) - mean) * rstd
            change = rstd * (n.norm[0, at, :].astype(F32) - mean_grad - xhat * mean_cross)
            n.grads[0, at, :] = (n.result[0, (r + 1) * cols : (r + 2) * cols, :].astype(F32) + change).astype(BF16)

    @pl.when(jnp.logical_not(lower))
    def _():
        n.grads[0] = n.result[0, cols : (rows + 1) * cols, :]


def by_micro(value):
    rest = (0,) * (len(value.shape) - 1)
    return pl.BlockSpec((1,) + tuple(value.shape[1:]), lambda m: (m,) + rest)


def whole(value):
    return pl.BlockSpec(tuple(value.shape), lambda m: (0,) * len(value.shape))


def call(kernel, name, micros, scalars, fixed, cut, outs, fixed_outs, scratch, work=4, room=16):
    names = [*scalars, *fixed, *cut, *outs, *fixed_outs, *scratch]
    cut_shape = [jax.ShapeDtypeStruct(s, d) for s, d in outs.values()]
    fixed_shape = [jax.ShapeDtypeStruct(s, d) for s, d in fixed_outs.values()]

    def body(*refs):
        kernel(types.SimpleNamespace(**dict(zip(names, refs))), pl.program_id(0))

    return pl.pallas_call(
        body,
        grid=(micros,),
        in_specs=[pl.BlockSpec(memory_space=pltpu.SMEM) for _ in scalars]
        + [whole(v) for v in fixed.values()]
        + [by_micro(v) for v in cut.values()],
        out_specs=[by_micro(s) for s in cut_shape] + [whole(s) for s in fixed_shape],
        out_shape=cut_shape + fixed_shape,
        scratch_shapes=[pltpu.VMEM(s, d) for s, d in scratch.values()],
        compiler_params=pltpu.CompilerParams(vmem_limit_bytes=room * 1024 * 1024),
        cost_estimate=pl.CostEstimate(flops=work, bytes_accessed=work // 4, transcendentals=0),
        name=name,
    )(*scalars.values(), *fixed.values(), *cut.values())


def pair_body(
    activations, latent, recon, target, boxes, kernel, mod_weight, scale_bias, shift_bias, out_weight
):
    micros, rows, cols, channels = activations.shape[1:]
    latents = latent.shape[1]
    pixels = rows * cols
    bands = lax.axis_size("rows")
    count = float(pixels * bands * 2 * (channels // GROUPS))
    segment = lax.axis_index("segment")
    side = lax.axis_index("sub")
    acts = activations[0].reshape(micros, pixels, channels)

    outer = swap(jnp.concatenate([acts[:, :cols], acts[:, pixels - cols :]], axis=1), "segment")
    inner = swap(acts[:, cols : pixels - cols], "segment")
    kernel_passed = swap(kernel[0], "segment")
    recon_beside, target_beside = swap(recon, "sub"), swap(target, "sub")

    (sums,) = call(sums_kernel, "input_sums", micros, {}, {}, {"acts": acts}, {}, {"sums": ((2 * micros, channels), F32)}, {})
    sums = sums + swap(sums, "sub")

    def border(first, r):
        def difference(one, two):
            part = slice(first, first + 2)
            return (one[:, :, part].astype(F32) - two[:, :, part].astype(F32)).transpose(0, 2, 1, 3)

        extra = latent[:, :, r].astype(F32).reshape(micros, 2, latents // 2, cols)
        two = jnp.concatenate([difference(recon, target), difference(recon_beside, target_beside), extra], axis=2)
        return jnp.concatenate([sums, two.reshape(micros * 16, cols)])

    from_up = shift(border(rows - 2, rows - 1), "rows", 1)
    from_down = shift(border(0, 0), "rows", bands - 1)
    across = shift(sums, "rows", 2)

    from_up, kernel_passed = lax.optimization_barrier((from_up, kernel_passed))
    image = {
        "latent": latent,
        "recon": recon,
        "target": target,
        "recon_beside": recon_beside,
        "target_beside": target_beside,
    }
    borders = {"from_up": from_up, "from_down": from_down, "out_weight": out_weight}
    wide = (rows + 2) * cols
    triple = 3 * channels
    shifted = {"shifted": ((wide, triple), BF16)}
    work = {
        **shifted,
        "weights": ((4, 2 * channels, triple), BF16),
        "hidden_grad": ((pixels, channels), F32),
        "latent_keep": ((8, pixels), BF16),
        "pairs": ((pixels, 2 * channels), BF16),
    }
    size = (rows, cols, bands, micros, count)
    sums_own = (sums + across) + (from_up[: 2 * micros] + from_down[: 2 * micros])
    mix = jnp.concatenate([mod_weight[0], jnp.concatenate([scale_bias, shift_bias], axis=1)]).astype(F32)
    mix = jnp.pad(mix, ((0, 7 - latents), (0, 0)))
    mix = jnp.concatenate([mix[:, :channels], mix[:, channels:]])
    base, reduced = call(
        functools.partial(upper_kernel, *size),
        "upper_block",
        micros,
        {"boxes": boxes},
        {
            "sums": sums,
            "across": across,
            "mod_weight": mod_weight,
            "scale_bias": scale_bias,
            "shift_bias": shift_bias,
            "kernel": kernel[0],
            "kernel_passed": kernel_passed,
            **borders,
        },
        {"acts": acts, **image},
        {"base": ((micros, wide, channels), BF16), "reduced": ((micros, 16, channels), F32)},
        {},
        {
            **work,
            "shifted": (((rows + 4) * cols, triple), BF16),
            "hidden_grad": ((wide, channels), F32),
            "sums_keep": ((2 * micros, channels), F32),
        },
    )
    sums = sums_own
    reduced, outer = lax.optimization_barrier((reduced, outer))
    above = shift(outer[:, cols:], "rows", 1)
    below = shift(outer[:, :cols], "rows", bands - 1)
    total_upper = pixel_total(reduced.reshape(micros * 16, channels))
    packed = jnp.concatenate([sums, total_upper, mix])
    packed, inner, above = lax.optimization_barrier((packed, inner, above))
    packed = swap(packed, "segment")
    result, edge = call(
        functools.partial(finish_kernel, *size),
        "finish_upper",
        micros,
        {"boxes": boxes},
        {"sums": sums, "mix": mix, "packed": packed, "total": total_upper, **borders},
        {
            "base": base,
            "acts": acts,
            "outer": outer,
            "inner": inner,
            "above": above,
            "below": below,
            **image,
        },
        {"result": ((micros, wide, channels), BF16), "edge": ((micros, 16, channels), BF16)},
        {},
        {},
    )
    near = swap(edge, "sub")
    half = kernel.shape[1] // 2
    norm, reduced, keep, give = call(
        functools.partial(own_kernel, *size),
        "own_block",
        micros,
        {"boxes": boxes},
        {"sums": sums, "mix": mix, "kernel": kernel[0], **borders},
        {"result": result, "near": near, "acts": acts, **image},
        {"norm": ((micros, pixels, channels), BF16), "reduced": ((micros, 16, channels), F32)},
        {"keep": ((half, channels), F32), "give": ((half + micros * 16, channels), F32)},
        {**work, "hidden": ((pixels, channels), BF16), "total": ((3, channels, triple), F32)},
    )
    got = swap(give, "sub")
    keep = (keep + got[:half]).astype(BF16)
    keep = (keep.astype(F32) + pair(keep, 1).astype(F32)).astype(BF16)
    other_pair = pair(keep, 2)
    total_lower = rows_total(reduced.reshape(micros * 16, channels) + got[half:])
    grads, mod_grad, bias_grad = call(
        functools.partial(last_kernel, rows, cols, micros, count),
        "input_gradient",
        micros,
        {},
        {"sums": sums, "mix": mix, "total_lower": total_lower, "total_upper": total_upper},
        {"acts": acts, "norm": norm, "result": result},
        {"grads": ((micros, pixels, channels), BF16)},
        {"mod_grad": ((1, latents, 2 * channels), F32), "bias_grad": ((1, 2 * channels), F32)},
        {},
        work=1 << 25,
    )
    grads, other_pair = lax.optimization_barrier((grads, other_pair))
    keep = keep.astype(F32) + other_pair.astype(F32)
    give = swap(keep, "sub")
    kernel_grad = jnp.where(side == 0, jnp.concatenate([keep, give]), jnp.concatenate([give, keep]))
    return (grads.reshape(activations.shape), kernel_grad[None], mod_grad, bias_grad)


def solution(mesh):
    pair = mesh.shape["segment"] == 2 and mesh.shape["rows"] == 4 and mesh.shape["sub"] == 2
    body = pair_body if pair else general_body
    placed = (
        P("segment", "groups", "rows", "sub", None),
        P("groups", None, "rows", "sub"),
        P("groups", None, "rows", "sub"),
        P("groups", None, "rows", "sub"),
        P("groups", None, None),
        P("segment", None, None),
        P("segment", None, None),
        P("segment", None),
        P("segment", None),
        P(),
    )
    return jax.shard_map(
        body,
        mesh=mesh,
        in_specs=placed,
        out_specs=(
            P("segment", "groups", "rows", "sub", None),
            P("segment", "groups", None),
            P("segment", "groups", None),
            P("segment", "groups"),
        ),
        check_vma=False,
    )
```
